32 devices in a mesh: dp: 16 (over z, x, core), tensor: 2 (over y).
Axes of the slice: x: 2, y: 2, z: 4, core: 2. Of those that a mesh axis runs over, the one named last changes fastest.
Arguments:
- latents: bfloat16 [32, 1024, 1152], P('dp', 'tensor'), may hold values from -6 to 6
- condition: bfloat16 [32, 1152], P('dp'), may hold values from -6 to 6
- cotangent: bfloat16 [32, 1024, 1152], P('dp', 'tensor'), may hold values from -6 to 6
- group_counts: int32 [16], P('dp'), may hold values from 1 to 2, as said below
- heads_weight: bfloat16 [1, 1152, 3, 1152], P(None, None, None, 'tensor'), may hold values from -0.1875 to 0.1875
- heads_bias: bfloat16 [1, 2, 1152], P(None, None, 'tensor'), may hold values from -3 to 3
- merge_weight: bfloat16 [1, 1152, 1152], P(None, 'tensor'), may hold values from -0.75 to 0.75
- merge_bias: bfloat16 [1, 1152], replicated, may hold values from -3 to 3
- up_weight: bfloat16 [1, 1152, 4608], P(None, None, 'tensor'), may hold values from -0.1875 to 0.1875
- up_bias: bfloat16 [1, 4608], P(None, 'tensor'), may hold values from -3 to 3
- down_weight: bfloat16 [1, 4608, 1152], P(None, 'tensor'), may hold values from -0.09375 to 0.09375
- down_bias: bfloat16 [1, 1152], replicated, may hold values from -3 to 3
- modulate_weight: bfloat16 [1, 1152, 6, 1152], P(None, None, None, 'tensor'), may hold values from -0.1875 to 0.1875
- modulate_bias: bfloat16 [1, 6, 1152], P(None, None, 'tensor'), may hold values from -3 to 3
Outputs:
- block_output: bfloat16 [32, 1024, 1152], P('dp', 'tensor')
- latent_grad: float32 [32, 1024, 1152], P('dp', 'tensor')
- condition_grad: float32 [32, 1152], P('dp')
- heads_weight_grad: float32 [1, 1152, 3, 1152], P(None, 'dp', None, 'tensor')
- heads_bias_grad: float32 [1, 2, 1152], P(None, None, 'tensor')
- merge_weight_grad: float32 [1, 1152, 1152], P(None, 'tensor', 'dp')
- merge_bias_grad: float32 [1, 1152], P(None, 'tensor')
- up_weight_grad: float32 [1, 1152, 4608], P(None, 'dp', 'tensor')
- up_bias_grad: float32 [1, 4608], P(None, 'tensor')
- down_weight_grad: float32 [1, 4608, 1152], P(None, 'tensor', 'dp')
- down_bias_grad: float32 [1, 1152], P(None, 'tensor')
- modulate_weight_grad: float32 [1, 1152, 6, 1152], P(None, 'dp', None, 'tensor')
- modulate_bias_grad: float32 [1, 6, 1152], P(None, None, 'tensor')
The draws below stay inside these ranges and needn't reach their ends.
Inputs may be any that keep to these rules, and one draw needn't show every extreme that they name: Data group g holds the slots g * 2 to g * 2 + 1; its first group_counts[g] slots hold latents, the others are empty and their cotangent is not used. Some groups hold one latent and some hold 2.
All inputs are finite; a program needn't handle non-finite values.
Results may differ from the reference program's by a relative error of at most 0.02.
Values may be sent and summed in bfloat16 or wider, within the bound.
A program may use at most 320 MiB of HBM per device.

```python
from functools import partial
import jax
import jax.numpy as jnp
from jax import lax

D = 1152
HEADS = 16
HEAD_DIM = 72
FF = 4608
SEQ = 1024
QUERY_BLOCK = 512
SLOTS = 2
BLOCKS = 1
LATENTS = 32
N_TENSOR = 2


def draw_group_counts(key, part):
    key = jax.random.fold_in(key, 7)
    groups = LATENTS // SLOTS
    ranking = jax.random.permutation(key, groups)
    return jnp.where(ranking < groups * 23 // 32, SLOTS, 1).astype(jnp.int32)


def raised(result, key, source, target, parts, factor):
    def block_of(position):
        return (jnp.arange(result.shape[position]) // (result.shape[position] // parts)).reshape((-1,) + (1,) * (result.ndim - 1 - position))

    one_side = jax.random.permutation(key, parts)[block_of(target)]
    far = (block_of(target) + parts // 2) % parts
    return jnp.where((block_of(source) == one_side) | (block_of(source) == far), factor * result, result)


def block_scale(stream_key, extent, cuts, least, top_value):
    gain = 1.0
    for position, blocks in cuts:
        draws = jax.random.uniform(jax.random.fold_in(jax.random.fold_in(stream_key, 6), position), (blocks,), jnp.float32, least / len(cuts), top_value / len(cuts))
        gain = gain * jnp.repeat(jnp.exp(draws), extent[position] // blocks).reshape((-1,) + (1,) * (len(extent) - 1 - position))
    return gain


def scatter_about(rng, extent, scale, limit, split=(), kind=jnp.bfloat16):
    values = jax.random.normal(rng, extent, jnp.float32) * scale
    if len(split) > 0:
        values = block_scale(rng, extent, split, -0.22, 0.18) * values
    return jnp.clip(values, min=-limit, max=limit).astype(kind)


def noise_with(rng, extent, scale, limit, split, heavy, held_as=jnp.bfloat16):
    result = scale * jax.random.normal(rng, extent, jnp.float32)
    if split:
        result = result * block_scale(rng, extent, split, -0.22, 0.18)
    return jnp.clip(raised(result, jax.random.fold_in(rng, 3), *heavy), -limit, limit).astype(held_as)


def setup_inputs(seed: int = 0) -> dict:
    seeds = jax.random.split(jax.random.key(seed), 15)
    return {
        "latents": scatter_about(seeds[0], (LATENTS, SEQ, D), 1.0, 6.0, ((0, 16), (1, 2))),
        "condition": scatter_about(seeds[1], (LATENTS, D), 1.0, 6.0, ((0, 16),)),
        "cotangent": noise_with(seeds[2], (LATENTS, SEQ, D), 1.0, 6.0, ((0, 16), (1, 2)), (0, 2, 16, 2.0)),
        "group_counts": draw_group_counts(jax.random.fold_in(seeds[14], 71), 0),
        "heads_weight": scatter_about(seeds[4], (BLOCKS, D, 3, D), D ** -0.5, 0.1875, ((3, 2),)),
        "heads_bias": scatter_about(seeds[5], (BLOCKS, 2, D), 0.5, 3.0, ((2, 2),)),
        "merge_weight": scatter_about(seeds[6], (BLOCKS, D, D), (D // 16) ** -0.5, 0.75, ((1, 2),)),
        "merge_bias": scatter_about(seeds[7], (BLOCKS, D), 0.5, 3.0),
        "up_weight": scatter_about(seeds[8], (BLOCKS, D, FF), D ** -0.5, 0.1875, ((2, 2),)),
        "up_bias": scatter_about(seeds[9], (BLOCKS, FF), 0.5, 3.0, ((1, 2),)),
        "down_weight": scatter_about(seeds[10], (BLOCKS, FF, D), FF ** -0.5, 0.09375, ((1, 2),)),
        "down_bias": scatter_about(seeds[11], (BLOCKS, D), 0.5, 3.0),
        "modulate_weight": scatter_about(seeds[12], (BLOCKS, D, 6, D), D ** -0.5, 0.1875, ((3, 2),)),
        "modulate_bias": scatter_about(seeds[13], (BLOCKS, 6, D), 0.5, 3.0, ((2, 2),)),
    }


@jax.custom_vjp
def low(v):
    return lax.optimization_barrier(v.astype(jnp.bfloat16)).astype(jnp.float32)

@jax.custom_vjp
def low_back(v):
    return v

def low_keep(v):
    return (low(v), None)

def low_pass(kept, grad):
    return (grad,)

def back_keep(v):
    return (v, None)

def back_low(kept, grad):
    return (low(grad),)
low.defvjp(low_keep, low_pass)
low_back.defvjp(back_keep, back_low)
highest = lax.Precision.HIGHEST
epsilon = 1e-06

def normalize(stream):
    average = lax.optimization_barrier(jnp.mean(stream, -1, keepdims=True))
    centered = stream - average
    variance = lax.optimization_barrier(jnp.mean(centered * centered, -1, keepdims=True))
    return centered * lax.rsqrt(variance + epsilon)

def split_columns(inputs, weight):
    width = weight.shape[-1] // N_TENSOR
    pieces = [jnp.tensordot(low_back(inputs), weight[..., index * width:(index + 1) * width], axes=1, precision=highest) for index in range(N_TENSOR)]
    return jnp.concatenate(pieces, -1)

def split_rows(inputs, weight):
    width = weight.shape[0] // N_TENSOR
    total = low(jnp.dot(inputs[:, :width], weight[:width], precision=highest))
    for index in range(1, N_TENSOR):
        total = total + low(jnp.dot(inputs[:, index * width:(index + 1) * width], weight[index * width:(index + 1) * width], precision=highest))
    return total

def attend_block(query_block, key_rows, value_rows):
    scores = jnp.einsum('qhd,khd->hqk', query_block, key_rows, precision=highest) * HEAD_DIM ** (-0.5)
    scores = low_back(scores)
    row_max = lax.optimization_barrier(jnp.max(scores, -1, keepdims=True))
    exponent = jnp.exp(scores - row_max)
    attn_probs = low(exponent / lax.optimization_barrier(jnp.sum(exponent, -1, keepdims=True)))
    return jnp.einsum('hqk,khd->qhd', attn_probs, value_rows, precision=highest)

def forward(stream, cond_vector, params):
    heads_weight, heads_bias, merge_weight, merge_bias, up_weight, up_bias, down_weight, down_bias, modulate_weight, modulate_bias = params
    silu_cond = low(jax.nn.silu(cond_vector))
    split_shape = (SEQ, HEADS, HEAD_DIM)
    for layer_index in range(BLOCKS):
        modulation = jnp.einsum('d,dkc->kc', silu_cond, modulate_weight[layer_index], precision=highest) + modulate_bias[layer_index]
        modulation = low_back(modulation)
        normed_first = low(normalize(stream) * (1.0 + modulation[1]) + modulation[0])
        offset = jnp.stack([heads_bias[layer_index, 0], jnp.zeros_like(heads_bias[layer_index, 0]), heads_bias[layer_index, 1]])
        projected = split_columns(normed_first, heads_weight[layer_index]) + offset
        projected = low(low_back(projected))
        queries = projected[:, 0].reshape(split_shape)
        key_rows = projected[:, 1].reshape(split_shape)
        value_rows = projected[:, 2].reshape(split_shape)
        block_fn = jax.checkpoint(partial(attend_block, key_rows=key_rows, value_rows=value_rows))
        attended = lax.map(block_fn, queries.reshape(SEQ // QUERY_BLOCK, QUERY_BLOCK, HEADS, HEAD_DIM))
        attended = low(low_back(attended.reshape(SEQ, D)))
        branch_first = low_back(split_rows(attended, merge_weight[layer_index]) + merge_bias[layer_index])
        stream = stream + modulation[2] * branch_first
        normed_second = low(normalize(stream) * (1.0 + modulation[4]) + modulation[3])
        hidden_pre = low_back(split_columns(normed_second, up_weight[layer_index]) + up_bias[layer_index])
        hidden = low(jax.nn.gelu(hidden_pre, approximate=True))
        branch_second = low_back(split_rows(hidden, down_weight[layer_index]) + down_bias[layer_index])
        stream = stream + modulation[5] * branch_second
    return stream

def reference(latents, condition, cotangent, group_counts, heads_weight, heads_bias, merge_weight, merge_bias, up_weight, up_bias, down_weight, down_bias, modulate_weight, modulate_bias):
    params = jax.tree.map(lambda operand: operand.astype(jnp.float32), (heads_weight, heads_bias, merge_weight, merge_bias, up_weight, up_bias, down_weight, down_bias, modulate_weight, modulate_bias))
    slot_numbers = jnp.arange(LATENTS, dtype=jnp.int32) % SLOTS
    live_flags = (slot_numbers < jnp.repeat(group_counts, SLOTS)).astype(jnp.float32)

    def one_latent(totals, inputs_here):
        latent_rows, cond_vector, cotangent_rows, live_flag = inputs_here
        output, pullback = jax.vjp(forward, latent_rows.astype(jnp.float32), cond_vector.astype(jnp.float32), params)
        grad_latent, grad_cond, grad_params = pullback(cotangent_rows.astype(jnp.float32) * live_flag)
        totals = jax.tree.map(jnp.add, totals, grad_params)
        return (totals, (output.astype(jnp.bfloat16), grad_latent, grad_cond))
    start_totals = jax.tree.map(jnp.zeros_like, params)
    totals, (block_output, latent_grad, condition_grad) = lax.scan(one_latent, start_totals, (latents, condition, cotangent, live_flags))
    return (block_output, latent_grad, condition_grad, totals[0], totals[1], totals[2], totals[3], totals[4], totals[5], totals[6], totals[7], totals[8], totals[9])
```

```python
import functools
import math

import jax
import jax.numpy as jnp
from jax import lax
from jax.experimental import pallas as pl
from jax.experimental.pallas import tpu as pltpu
from jax.sharding import PartitionSpec as P

HEAD_DIM = 72
QUERY_BLOCK = 512


epsilon = 1e-06


def normalize(stream):
    average = jnp.mean(stream, -1, keepdims=True)
    centered = stream - average
    variance = jnp.mean(centered * centered, -1, keepdims=True)
    inverse = lax.rsqrt(variance + epsilon)
    return (centered * inverse, inverse)


def normalize_back(grad_norm, normed, inverse):
    first_mean = jnp.mean(grad_norm, -1, keepdims=True)
    second_mean = jnp.mean(grad_norm * normed, -1, keepdims=True)
    return inverse * (grad_norm - first_mean - normed * second_mean)


def gelu_tanh(values):
    return jax.nn.gelu(values, approximate=True)


def column_sums(operand):
    return jnp.sum(operand.astype(jnp.float32), 0)


def outer_rows(operand, other):
    return lax.dot_general(
        operand, other, (((0,), (0,)), ((), ())), preferred_element_type=jnp.float32
    )


def times_transposed(operand, weight):
    return lax.dot_general(
        operand, weight, (((1,), (1,)), ((), ())), preferred_element_type=jnp.float32
    )


def gather_tokens(values):
    return lax.all_gather(values, "tensor", axis=0, tiled=True)


def gather_grads(values):
    return lax.all_gather(values, "tensor", axis=0, tiled=True)


def scatter_branch(operand, weight):

    def partial_rows(first_row, row_count):
        return jnp.dot(operand, weight, preferred_element_type=jnp.float32)

    return lax.psum_scatter(
        partial_rows(
            jnp.int32(0), operand.shape[0] // lax.axis_size("tensor") * lax.axis_size("tensor")
        ).astype(jnp.bfloat16),
        "tensor",
        scatter_dimension=0,
        tiled=True,
    ).astype(jnp.float32)


def scatter_inputs(operand, weight):

    def partial_rows(first_row, row_count):
        return times_transposed(operand, weight)

    return lax.psum_scatter(
        partial_rows(
            jnp.int32(0), operand.shape[0] // lax.axis_size("tensor") * lax.axis_size("tensor")
        ).astype(jnp.bfloat16),
        "tensor",
        scatter_dimension=0,
        tiled=True,
    ).astype(jnp.float32)


def stack_member(layer_tuples, member):
    return jnp.stack([entry_tuple[member] for entry_tuple in layer_tuples])


def attend_forward(queries, key_rows, value_rows):
    length, heads_here = (queries.shape[0], queries.shape[1])
    blocks = length // QUERY_BLOCK
    score_scale = HEAD_DIM ** (-0.5)

    def one_block(query_block):
        scores = (
            jnp.einsum("qhd,khd->hqk", query_block, key_rows, preferred_element_type=jnp.float32)
            * score_scale
        )
        row_max = jnp.max(scores, -1, keepdims=True)
        exponent = jnp.exp(scores - row_max)
        row_total = jnp.sum(exponent, -1, keepdims=True)
        attn_probs = (exponent / row_total).astype(jnp.bfloat16)
        attended = jnp.einsum(
            "hqk,khd->qhd", attn_probs, value_rows, preferred_element_type=jnp.float32
        )
        return (attended.astype(jnp.bfloat16), (row_max + jnp.log(row_total))[:, :, 0])

    attended, logsum = lax.map(
        one_block, queries.reshape(blocks, QUERY_BLOCK, heads_here, HEAD_DIM)
    )
    return (attended.reshape(length, heads_here * HEAD_DIM), logsum)


def attend_backward(queries, key_rows, value_rows, logsum, grad_attended):
    length, heads_here = (queries.shape[0], queries.shape[1])
    blocks = length // QUERY_BLOCK
    score_scale = HEAD_DIM ** (-0.5)
    block_shape = (blocks, QUERY_BLOCK, heads_here, HEAD_DIM)

    def one_block(running, inputs_here):
        grad_keys, grad_values = running
        query_block, grad_block, logsum_block = inputs_here
        scores = (
            jnp.einsum("qhd,khd->hqk", query_block, key_rows, preferred_element_type=jnp.float32)
            * score_scale
        )
        attn_probs = jnp.exp(scores - logsum_block[:, :, None])
        grad_values = grad_values + jnp.einsum(
            "hqk,qhd->khd",
            attn_probs.astype(jnp.bfloat16),
            grad_block,
            preferred_element_type=jnp.float32,
        )
        grad_probs = jnp.einsum(
            "qhd,khd->hqk", grad_block, value_rows, preferred_element_type=jnp.float32
        )
        row_dot = jnp.sum(attn_probs * grad_probs, -1, keepdims=True)
        grad_scores = (attn_probs * (grad_probs - row_dot)).astype(jnp.bfloat16)
        grad_queries = (
            jnp.einsum("hqk,khd->qhd", grad_scores, key_rows, preferred_element_type=jnp.float32)
            * score_scale
        )
        grad_keys = (
            grad_keys
            + jnp.einsum(
                "hqk,qhd->khd", grad_scores, query_block, preferred_element_type=jnp.float32
            )
            * score_scale
        )
        return ((grad_keys, grad_values), grad_queries.astype(jnp.bfloat16))

    zeros_kv = jnp.zeros((length, heads_here, HEAD_DIM), jnp.float32)
    scanned = (queries.reshape(block_shape), grad_attended.reshape(block_shape), logsum)
    (grad_keys, grad_values), grad_queries = lax.scan(one_block, (zeros_kv, zeros_kv), scanned)
    flat_shape = (length, heads_here * HEAD_DIM)
    return (
        grad_queries.reshape(flat_shape),
        grad_keys.astype(jnp.bfloat16).reshape(flat_shape),
        grad_values.astype(jnp.bfloat16).reshape(flat_shape),
    )


def forward_layer(stream, modulation, layer_weights, heads_here):
    (
        flat_heads,
        heads_offset,
        merge_weight,
        merge_bias,
        up_weight,
        up_bias,
        down_weight,
        down_bias,
    ) = layer_weights
    length = stream.shape[0] * lax.axis_size("tensor")
    columns = flat_heads.shape[1] // 3
    norm_first, inverse_first = normalize(stream)
    normed_first = (norm_first * (1.0 + modulation[1]) + modulation[0]).astype(jnp.bfloat16)
    gathered_first = gather_tokens(normed_first)
    projected = (
        jnp.dot(gathered_first, flat_heads, preferred_element_type=jnp.float32) + heads_offset
    ).astype(jnp.bfloat16)
    split_shape = (length, heads_here, HEAD_DIM)
    queries = projected[:, :columns].reshape(split_shape)
    key_rows = projected[:, columns : 2 * columns].reshape(split_shape)
    value_rows = projected[:, 2 * columns :].reshape(split_shape)
    attended, logsum = attend_forward(queries, key_rows, value_rows)
    branch_first = scatter_branch(attended, merge_weight) + merge_bias.astype(jnp.float32)
    stream_mid = stream + modulation[2] * branch_first
    norm_second, inverse_second = normalize(stream_mid)
    normed_second = (norm_second * (1.0 + modulation[4]) + modulation[3]).astype(jnp.bfloat16)
    gathered_second = gather_tokens(normed_second)
    hidden_pre = jnp.dot(
        gathered_second, up_weight, preferred_element_type=jnp.float32
    ) + up_bias.astype(jnp.float32)
    hidden = gelu_tanh(hidden_pre).astype(jnp.bfloat16)
    branch_second = scatter_branch(hidden, down_weight) + down_bias.astype(jnp.float32)
    stream_next = stream_mid + modulation[5] * branch_second
    first_input, second_input = (gathered_first, gathered_second)
    kept = (
        norm_first,
        inverse_first,
        first_input,
        queries,
        key_rows,
        value_rows,
        logsum,
        attended,
        branch_first,
        norm_second,
        inverse_second,
        second_input,
        hidden_pre,
        hidden,
        branch_second,
    )
    return (stream_next, kept)


def backward_layer(grad_stream, modulation, layer_weights, kept):
    (
        flat_heads,
        heads_offset,
        merge_weight,
        merge_bias,
        up_weight,
        up_bias,
        down_weight,
        down_bias,
    ) = layer_weights
    (
        norm_first,
        inverse_first,
        first_input,
        queries,
        key_rows,
        value_rows,
        logsum,
        attended,
        branch_first,
        norm_second,
        inverse_second,
        second_input,
        hidden_pre,
        hidden,
        branch_second,
    ) = kept
    model_width = flat_heads.shape[0]
    columns = flat_heads.shape[1] // 3
    grad_branch_second = (modulation[5] * grad_stream).astype(jnp.bfloat16)
    grad_gate_second = jnp.sum(grad_stream * branch_second, 0)
    grad_down_bias = column_sums(grad_branch_second)
    gathered_grad = gather_grads(grad_branch_second)
    down_grad = outer_rows(hidden, gathered_grad)
    grad_hidden = times_transposed(gathered_grad, down_weight)
    grad_pre = jax.vjp(gelu_tanh, hidden_pre)[1](grad_hidden)[0].astype(jnp.bfloat16)
    up_bias_grad = column_sums(grad_pre)
    up_grad = outer_rows(second_input, grad_pre)
    grad_normed_second = scatter_inputs(grad_pre, up_weight)
    grad_shift_second = jnp.sum(grad_normed_second, 0)
    grad_scale_second = jnp.sum(grad_normed_second * norm_second, 0)
    grad_mid = grad_stream + normalize_back(
        grad_normed_second * (1.0 + modulation[4]), norm_second, inverse_second
    )
    grad_branch_first = (modulation[2] * grad_mid).astype(jnp.bfloat16)
    grad_gate_first = jnp.sum(grad_mid * branch_first, 0)
    grad_merge_bias = column_sums(grad_branch_first)
    gathered_grad = gather_grads(grad_branch_first)
    merge_grad = outer_rows(attended, gathered_grad)
    grad_attended = times_transposed(gathered_grad, merge_weight).astype(jnp.bfloat16)
    grad_queries, grad_keys, grad_values = attend_backward(
        queries, key_rows, value_rows, logsum, grad_attended
    )
    grad_projected = jnp.concatenate([grad_queries, grad_keys, grad_values], 1)
    heads_bias_grad = jnp.stack([column_sums(grad_queries), column_sums(grad_values)])
    heads_grad = outer_rows(first_input, grad_projected).reshape(model_width, 3, columns)
    grad_normed_first = scatter_inputs(grad_projected, flat_heads)
    grad_shift_first = jnp.sum(grad_normed_first, 0)
    grad_scale_first = jnp.sum(grad_normed_first * norm_first, 0)
    grad_before = grad_mid + normalize_back(
        grad_normed_first * (1.0 + modulation[1]), norm_first, inverse_first
    )
    extra = jnp.stack(
        [
            grad_shift_first,
            grad_scale_first,
            grad_gate_first,
            grad_shift_second,
            grad_scale_second,
            grad_gate_second,
            grad_merge_bias,
            grad_down_bias,
        ]
    )
    return (
        grad_before,
        (heads_grad, heads_bias_grad, merge_grad, up_grad, up_bias_grad, down_grad),
        extra,
    )


def per_device(
    latents,
    condition,
    cotangent,
    group_counts,
    heads_weight,
    heads_bias,
    merge_weight,
    merge_bias,
    up_weight,
    up_bias,
    down_weight,
    down_bias,
    modulate_weight,
    modulate_bias,
):
    slot_count = latents.shape[0]
    model_width = latents.shape[2]
    layer_count = heads_weight.shape[0]
    columns = heads_weight.shape[3]
    heads_here = columns // HEAD_DIM
    silu_cond = jax.nn.silu(condition.astype(jnp.float32)).astype(jnp.bfloat16)
    local_mod = jnp.einsum(
        "sd,bdkc->sbkc", silu_cond, modulate_weight, preferred_element_type=jnp.float32
    ) + modulate_bias.astype(jnp.float32)
    modulation_all = lax.all_gather(local_mod, "tensor", axis=3, tiled=True)
    flat_heads = heads_weight.reshape(layer_count, model_width, 3 * columns)
    zero_bias = jnp.zeros((layer_count, columns), heads_bias.dtype)
    heads_offset = (
        jnp.stack([heads_bias[:, 0], zero_bias, heads_bias[:, 1]], 1)
        .reshape(layer_count, 3 * columns)
        .astype(jnp.float32)
    )
    per_layer = [
        (
            flat_heads[0],
            heads_offset[0],
            merge_weight[0],
            merge_bias[0],
            up_weight[0],
            up_bias[0],
            down_weight[0],
            down_bias[0],
        )
    ]
    layer_sums = [None] * layer_count
    modulate_sum = jnp.zeros(modulate_weight.shape, jnp.float32)
    modulate_bias_sum = jnp.zeros(modulate_bias.shape, jnp.float32)
    merge_bias_sum = jnp.zeros((layer_count, columns), jnp.float32)
    down_bias_sum = jnp.zeros((layer_count, columns), jnp.float32)
    output_list, latent_list, condition_list = ([], [], [])
    for slot_index in range(slot_count):
        live_flag = (slot_index < group_counts[0]).astype(jnp.float32)
        stream = latents[slot_index].astype(jnp.float32)
        layer_index = 0
        stream, kept = forward_layer(
            stream, modulation_all[slot_index, layer_index], per_layer[layer_index], heads_here
        )
        saved_layers = [kept]
        output_list.append(stream.astype(jnp.bfloat16))
        grad_stream = cotangent[slot_index].astype(jnp.float32) * live_flag
        extras = [None] * layer_count
        for layer_index in reversed(range(layer_count)):
            grad_stream, layer_grads, extra = backward_layer(
                grad_stream,
                modulation_all[slot_index, layer_index],
                per_layer[layer_index],
                saved_layers[layer_index],
            )
            if layer_sums[layer_index] is None:
                layer_sums[layer_index] = layer_grads
            else:
                layer_sums[layer_index] = jax.tree.map(
                    jnp.add, layer_sums[layer_index], layer_grads
                )
            extras[layer_index] = extra
        latent_list.append(grad_stream)
        shared = lax.psum_scatter(
            jnp.stack(extras).astype(jnp.bfloat16), "tensor", scatter_dimension=2, tiled=True
        ).astype(jnp.float32)
        grad_mod = shared[:, :6].astype(jnp.bfloat16)
        modulate_sum = modulate_sum + jnp.einsum(
            "d,bkc->bdkc", silu_cond[slot_index], grad_mod, preferred_element_type=jnp.float32
        )
        modulate_bias_sum = modulate_bias_sum + grad_mod.astype(jnp.float32)
        merge_bias_sum = merge_bias_sum + shared[:, 6]
        down_bias_sum = down_bias_sum + shared[:, 7]
        cond_partial = jnp.einsum(
            "bdkc,bkc->d", modulate_weight, grad_mod, preferred_element_type=jnp.float32
        )
        cond_total = lax.psum(cond_partial, "tensor")
        silu_grad = jax.vjp(jax.nn.silu, condition[slot_index].astype(jnp.float32))[1](cond_total)[
            0
        ]
        condition_list.append(silu_grad)
    weight_grads = (
        lax.psum_scatter(
            stack_member(layer_sums, 0).astype(jnp.bfloat16), "dp", scatter_dimension=1, tiled=True
        ).astype(jnp.float32),
        lax.psum_scatter(
            stack_member(layer_sums, 2).astype(jnp.bfloat16), "dp", scatter_dimension=2, tiled=True
        ).astype(jnp.float32),
        lax.psum_scatter(
            stack_member(layer_sums, 3).astype(jnp.bfloat16), "dp", scatter_dimension=1, tiled=True
        ).astype(jnp.float32),
        lax.psum_scatter(
            stack_member(layer_sums, 5).astype(jnp.bfloat16), "dp", scatter_dimension=2, tiled=True
        ).astype(jnp.float32),
        lax.psum_scatter(
            modulate_sum.astype(jnp.bfloat16), "dp", scatter_dimension=1, tiled=True
        ).astype(jnp.float32),
    )
    bias_grads = lax.psum(
        (
            stack_member(layer_sums, 1),
            merge_bias_sum,
            stack_member(layer_sums, 4),
            down_bias_sum,
            modulate_bias_sum,
        ),
        "dp",
    )
    block_output = jnp.stack(output_list)
    latent_grad = jnp.stack(latent_list)
    condition_grad = jnp.stack(condition_list)
    return (
        block_output,
        latent_grad,
        condition_grad,
        weight_grads[0],
        bias_grads[0],
        weight_grads[1],
        bias_grads[1],
        weight_grads[2],
        bias_grads[2],
        weight_grads[3],
        bias_grads[3],
        weight_grads[4],
        bias_grads[4],
    )


F32 = jnp.float32
BF16 = jnp.bfloat16
SCORE_SCALE = HEAD_DIM ** (-0.5)
SCORE_LOG2 = SCORE_SCALE * math.log2(math.e)
VMEM_BYTES = 60 * 2**20


def dot_dims(left, right, left_dim, right_dim):
    return lax.dot_general(
        left, right, (((left_dim,), (right_dim,)), ((), ())), preferred_element_type=F32
    )


def head_slice(part, head, width):
    return slice(part * width + head * HEAD_DIM, part * width + (head + 1) * HEAD_DIM)


def attend_kernel(heads, qkv_ref, out_ref, logsum_ref):
    width = heads * HEAD_DIM
    rows_here = out_ref.shape[0]
    rows = pl.ds(pl.multiple_of(pl.program_id(0) * rows_here, rows_here), rows_here)
    for head in range(heads):
        queries = qkv_ref[rows, head_slice(0, head, width)]
        scores = dot_dims(qkv_ref[:, head_slice(1, head, width)], queries, 1, 1)
        top = jnp.max(scores, 0, keepdims=True)
        exponent = jnp.exp2((scores - top) * SCORE_LOG2)
        total = jnp.sum(exponent, 0, keepdims=True)
        mixed = dot_dims(qkv_ref[:, head_slice(2, head, width)], exponent.astype(BF16), 0, 0)
        out_ref[:, head_slice(0, head, width)] = (mixed / total).T.astype(BF16)
        logsum_ref[head : head + 1, :] = top * SCORE_LOG2 + jnp.log2(total)


def attend(qkv, query_rows=512):
    tokens, width = qkv.shape[0], qkv.shape[1] // 3
    heads = width // HEAD_DIM
    return pl.pallas_call(
        functools.partial(attend_kernel, heads),
        grid=(tokens // query_rows,),
        in_specs=[pl.BlockSpec((tokens, 3 * width), lambda i: (0, 0))],
        out_specs=[
            pl.BlockSpec((query_rows, width), lambda i: (i, 0)),
            pl.BlockSpec((heads, query_rows), lambda i: (0, i)),
        ],
        out_shape=[
            jax.ShapeDtypeStruct((tokens, width), BF16),
            jax.ShapeDtypeStruct((heads, tokens), F32),
        ],
        compiler_params=pltpu.CompilerParams(vmem_limit_bytes=VMEM_BYTES),
        cost_estimate=pl.CostEstimate(
            flops=4 * heads * tokens * tokens * 256, bytes_accessed=8 * tokens * width,
            transcendentals=heads * tokens * tokens,
        ),
    )(qkv)


def attend_back_kernel(
    heads, key_rows, steps,
    qkv_ref, out_ref, grad_ref, logsum_ref, grads_ref, pairs_ref, dot_ref, query_ref,
):
    step = pl.program_id(0)
    width = heads * HEAD_DIM
    half = heads // 2
    rows = pl.ds(pl.multiple_of(step * key_rows, key_rows), key_rows)

    @pl.when(step == 0)
    def _():
        owner = lax.broadcasted_iota(jnp.int32, (heads, width), 1)
        first = lax.broadcasted_iota(jnp.int32, (heads, width), 0) * HEAD_DIM
        member = ((owner >= first) & (owner < first + HEAD_DIM)).astype(BF16)
        product = grad_ref[...].astype(F32) * out_ref[...].astype(F32)
        high = product.astype(BF16)
        low = (product - high.astype(F32)).astype(BF16)
        dot_ref[...] = dot_dims(member, high, 1, 1) + dot_dims(member, low, 1, 1)
        query_ref[...] = jnp.zeros_like(query_ref)

    def store(part, head, rows, value):
        grads_ref[rows, head_slice(part, head, width)] = value
        pairs_ref[head // half, rows, head_slice(part, head % half, half * HEAD_DIM)] = value

    for head in range(heads):
        queries = qkv_ref[:, head_slice(0, head, width)]
        keys = qkv_ref[rows, head_slice(1, head, width)]
        grad = grad_ref[:, head_slice(0, head, width)]
        scores = dot_dims(keys, queries, 1, 1)
        probs = jnp.exp2(scores * SCORE_LOG2 - logsum_ref[head : head + 1, :])
        grad_probs = dot_dims(qkv_ref[rows, head_slice(2, head, width)], grad, 1, 1)
        grad_scores = (probs * (grad_probs - dot_ref[head : head + 1, :])).astype(BF16)
        grad_values = jnp.dot(probs.astype(BF16), grad, preferred_element_type=F32)
        store(2, head, rows, grad_values.astype(BF16))
        grad_keys = jnp.dot(grad_scores, queries, preferred_element_type=F32) * SCORE_SCALE
        store(1, head, rows, grad_keys.astype(BF16))
        query_ref[head] += dot_dims(keys, grad_scores, 0, 0)

    @pl.when(step == steps - 1)
    def _():
        for head in range(heads):
            store(0, head, slice(None), (query_ref[head] * SCORE_SCALE).T.astype(BF16))


def attend_back(qkv, attended, grad_attended, logsum, key_rows=512):
    tokens, width = attended.shape
    heads = width // HEAD_DIM
    steps = tokens // key_rows
    whole = lambda *shape: pl.BlockSpec(shape, lambda i: (0,) * len(shape))
    return pl.pallas_call(
        functools.partial(attend_back_kernel, heads, key_rows, steps),
        grid=(steps,),
        in_specs=[
            whole(tokens, 3 * width), whole(tokens, width), whole(tokens, width),
            whole(heads, tokens),
        ],
        out_specs=[whole(tokens, 3 * width), whole(2, tokens, 3 * width // 2)],
        out_shape=[
            jax.ShapeDtypeStruct((tokens, 3 * width), BF16),
            jax.ShapeDtypeStruct((2, tokens, 3 * width // 2), BF16),
        ],
        scratch_shapes=[
            pltpu.VMEM((heads, tokens), F32),
            pltpu.VMEM((heads, HEAD_DIM, tokens), F32),
        ],
        compiler_params=pltpu.CompilerParams(vmem_limit_bytes=VMEM_BYTES),
        cost_estimate=pl.CostEstimate(
            flops=10 * heads * tokens * tokens * 256, bytes_accessed=22 * tokens * width,
            transcendentals=heads * tokens * tokens,
        ),
    )(qkv, attended, grad_attended, logsum)


GELU_OUTER = math.sqrt(2 / math.pi)
GELU_CUBIC = 0.044715


def gelu_and_slope(values):
    square = values * values
    tanh = jnp.tanh(values * (GELU_OUTER + GELU_OUTER * GELU_CUBIC * square))
    half = 0.5 + 0.5 * tanh
    inner = 0.5 * GELU_OUTER + 1.5 * GELU_OUTER * GELU_CUBIC * square
    return values * half, half + values * (1.0 - tanh * tanh) * inner


def feed_kernel(
    token_rows, carried, normed_ref, grad_ref, up_ref, bias_ref, down_ref, *refs
):
    if carried:
        branch_in, normed_in = refs[:2]
        refs = refs[2:]
    branch_ref, back_ref, hidden_ref, pre_ref, bias_grad_ref = refs
    chunk = pl.program_id(0)
    bias_grad_ref[...] = jnp.zeros_like(bias_grad_ref)

    def block(index, _):
        rows = pl.ds(pl.multiple_of(index * token_rows, token_rows), token_rows)
        pre = jnp.dot(normed_ref[rows, :], up_ref[...], preferred_element_type=F32)
        grad_hidden = dot_dims(grad_ref[rows, :], down_ref[...], 1, 1)
        hidden, slope = gelu_and_slope(pre + bias_ref[...])
        hidden = hidden.astype(BF16)
        grad_pre = (grad_hidden * slope).astype(BF16)
        bias_grad_ref[...] += jnp.sum(grad_pre.astype(F32), 0, keepdims=True)
        hidden_ref[0, rows, :] = hidden
        pre_ref[0, rows, :] = grad_pre
        branch = jnp.dot(hidden, down_ref[...], preferred_element_type=F32)
        back = dot_dims(grad_pre, up_ref[...], 1, 1)

        @pl.when(chunk == 0)
        def _():
            branch_ref[rows, :] = branch + branch_in[rows, :] if carried else branch
            back_ref[rows, :] = back + normed_in[rows, :] if carried else back

        @pl.when(chunk > 0)
        def _():
            branch_ref[rows, :] += branch
            back_ref[rows, :] += back

        return 0

    lax.fori_loop(0, normed_ref.shape[0] // token_rows, block, 0)


def feed(normed, grad, up, bias, down, carried=(), token_rows=256):
    tokens, model_width = normed.shape
    hidden_here = up.shape[1]
    width = hidden_here // 2
    whole = lambda: pl.BlockSpec((tokens, model_width), lambda j: (0, 0))
    pair = lambda: pl.BlockSpec((1, tokens, width), lambda j: (j, 0, 0))
    return pl.pallas_call(
        functools.partial(feed_kernel, token_rows, len(carried) > 0),
        grid=(2,),
        in_specs=[
            whole(), whole(),
            pl.BlockSpec((model_width, width), lambda j: (0, j)),
            pl.BlockSpec((1, width), lambda j: (0, j)),
            pl.BlockSpec((width, model_width), lambda j: (j, 0)),
        ] + [whole() for _ in carried],
        out_specs=[
            whole(), whole(), pair(), pair(), pl.BlockSpec((1, width), lambda j: (0, j)),
        ],
        out_shape=[
            jax.ShapeDtypeStruct((tokens, model_width), F32),
            jax.ShapeDtypeStruct((tokens, model_width), F32),
            jax.ShapeDtypeStruct((2, tokens, width), BF16),
            jax.ShapeDtypeStruct((2, tokens, width), BF16),
            jax.ShapeDtypeStruct((1, hidden_here), F32),
        ],
        compiler_params=pltpu.CompilerParams(vmem_limit_bytes=VMEM_BYTES),
        cost_estimate=pl.CostEstimate(
            flops=8 * tokens * model_width * hidden_here,
            bytes_accessed=30 * tokens * model_width, transcendentals=tokens * hidden_here,
        ),
    )(normed, grad, up, bias, down, *carried)


def bit_pairs(size, bit):
    return [(index, index ^ bit) for index in range(size)]


def swap(values, axis, bit):
    return lax.ppermute(values, axis, bit_pairs(lax.axis_size(axis), bit))


def pick(values, index, axis):
    return lax.dynamic_index_in_dim(values, index, axis, keepdims=False)


def after(values, *others):
    return lax.optimization_barrier((values,) + others)[0]


def place(first, second, index, axis=0):
    return jnp.where(
        index == 0,
        jnp.concatenate([first, second], axis),
        jnp.concatenate([second, first], axis),
    )


def fetch_other(weight, place_bits, behind=()):
    near, core = place_bits
    pieces = weight.shape[0] // 4
    first = lax.dynamic_slice_in_dim(weight, (2 * near + core) * pieces, pieces, 0)
    got = swap(after(first, *behind), "tensor", 1)
    got_near = swap(got, "dp", 4)
    got_core = swap(got, "dp", 1)
    got_both = swap(got_near, "dp", 1)
    whole = jnp.zeros(weight.shape, weight.dtype)
    for piece, near_here, core_here in (
        (got, near, core), (got_near, 1 - near, core),
        (got_core, near, 1 - core), (got_both, 1 - near, 1 - core),
    ):
        whole = lax.dynamic_update_slice_in_dim(
            whole, piece, (2 * near_here + core_here) * pieces, 0
        )
    return whole, got


def scatter_rows(values, bits, order):
    steps = {"far": (bits[0], 8), "near": (bits[1], 4), "x": (bits[2], 2)}
    axes = ["far", "near", "x"]
    for name in order:
        index, mask = steps[name]
        axis = axes.index(name)
        axes.remove(name)
        sent = swap(pick(values, 1 - index, axis), "dp", mask)
        kept = pick(values, index, axis)
        values = (kept.astype(F32) + sent.astype(F32)).astype(BF16)
    return values


def slot_device(
    latents,
    condition,
    cotangent,
    group_counts,
    heads_weight,
    heads_bias,
    merge_weight,
    merge_bias,
    up_weight,
    up_bias,
    down_weight,
    down_bias,
    modulate_weight,
    modulate_bias,
):
    side = lax.axis_index("tensor")
    place_dp = lax.axis_index("dp")
    core, x_bit, near, far = (lax.rem(place_dp // step, 2) for step in (1, 2, 4, 8))
    bits = (far, near, x_bit)
    half, model_width = latents.shape[1:]
    columns = heads_weight.shape[3]
    features = modulate_weight.shape[3]
    hidden_here = up_weight.shape[2]
    heads_own = heads_weight[0].reshape(model_width, 3 * columns)
    merge_own, up_own, down_own = merge_weight[0], up_weight[0], down_weight[0]

    latent_own = pick(latents, side, 0)
    latent_other = swap(pick(latents, 1 - side, 0), "tensor", 1)
    silu_cond = jax.nn.silu(condition.astype(F32)).astype(BF16)
    local_mod = jnp.einsum(
        "sd,dkc->skc", silu_cond, modulate_weight[0], preferred_element_type=F32
    ) + modulate_bias[0].astype(F32)
    mod_other = swap(pick(local_mod, 1 - side, 0), "tensor", 1)
    shift1, scale1, gate1, shift2, scale2, gate2 = place(
        pick(local_mod, side, 0), mod_other, side, 1
    )
    silu_all = lax.all_gather(silu_cond, "dp", axis=0, tiled=True)
    bias_pack = swap(jnp.concatenate([heads_bias.reshape(-1), up_bias.reshape(-1)]), "tensor", 1)

    def heads_offset(pair):
        return jnp.concatenate([pair[0], jnp.zeros_like(pair[0]), pair[1]]).astype(F32)

    offset_own = heads_offset(heads_bias[0])
    offset_other = heads_offset(bias_pack[: 2 * columns].reshape(2, columns))
    up_bias_own = up_bias.astype(F32)
    up_bias_other = bias_pack[2 * columns :].reshape(1, hidden_here).astype(F32)
    cotangent_sent = pick(cotangent, 1 - side, 0)
    fetch_bits = (near, core)
    heads_other, heads_piece = fetch_other(heads_own, fetch_bits)
    merge_other, merge_piece = fetch_other(merge_own, fetch_bits, (latent_other,))
    up_other, up_piece = fetch_other(up_own, fetch_bits, (heads_piece,))
    cotangent_other = swap(after(cotangent_sent, merge_piece), "tensor", 1)
    down_other, _ = fetch_other(down_own, fetch_bits, (up_piece,))
    live_flag = (side < group_counts[0]).astype(F32)

    stream = jnp.concatenate([latent_own, latent_other], 0).astype(F32)
    norm1, inverse1 = normalize(stream)
    normed1 = (norm1 * (1.0 + scale1) + shift1).astype(BF16)
    normed1_peer = swap(normed1, "dp", 1)
    qkv_own = (jnp.dot(normed1, heads_own, preferred_element_type=F32) + offset_own).astype(BF16)
    attended_own, logsum_own = attend(qkv_own)
    qkv_other = (
        jnp.dot(normed1, heads_other, preferred_element_type=F32) + offset_other
    ).astype(BF16)
    attended_other, logsum_other = attend(qkv_other)
    branch1 = (
        jnp.dot(attended_own, merge_own, preferred_element_type=F32)
        + jnp.dot(attended_other, merge_other, preferred_element_type=F32)
        + merge_bias[0].astype(F32)
    )
    mid = stream + gate1 * branch1
    norm2, inverse2 = normalize(mid)
    normed2 = (norm2 * (1.0 + scale2) + shift2).astype(BF16)

    grad = jnp.concatenate([pick(cotangent, side, 0), cotangent_other], 0).astype(F32) * live_flag
    grad_b2 = (gate2 * grad).astype(BF16)
    branch2, back2, hidden_own, pre_own, up_sums_own = feed(
        normed2, grad_b2, up_own, up_bias_own, down_own
    )
    branch2, back2, hidden_other, pre_other, up_sums_other = feed(
        normed2, grad_b2, up_other, up_bias_other, down_other, (branch2, back2)
    )
    branch2 = branch2 + down_bias[0].astype(F32)
    output = (mid + gate2 * branch2).astype(BF16)
    output_other = swap(output[half:], "tensor", 1)
    block_output = place(output[None, :half], output_other[None], side)

    normed2_peer = swap(normed2, "dp", 1)
    grad_b2_peer = swap(grad_b2, "dp", 1)

    def feature_grad(rows, rows_peer, own, other):
        mine = jnp.concatenate([pick(own, core, 0), pick(other, core, 0)], 1)
        peer = jnp.concatenate(
            [swap(pick(own, 1 - core, 0), "dp", 1), swap(pick(other, 1 - core, 0), "dp", 1)], 1
        )
        return (dot_dims(rows, mine, 0, 0) + dot_dims(rows_peer, peer, 0, 0)).astype(BF16)

    def reduce_blocks(total, order):
        width = total.shape[1] // 2
        total = scatter_rows(total.reshape(2, 2, 2, -1, 2 * width), bits, order)
        sent = swap(total[:, width:], "tensor", 1)
        return total[:, :width].astype(F32) + sent.astype(F32)

    def join_cores(total):
        total = total.astype(BF16).reshape((2, -1) + total.shape[1:])
        sent = swap(pick(total, 1 - core, 0), "dp", 1)
        return place(pick(total, core, 0), sent, core, total.ndim - 2).astype(F32)

    down_total = feature_grad(grad_b2, grad_b2_peer, hidden_own, hidden_other)
    up_total = feature_grad(normed2, normed2_peer, pre_own, pre_other)
    down_grad = join_cores(reduce_blocks(down_total, ("x", "near", "far")))
    up_grad = join_cores(reduce_blocks(up_total, ("near", "x", "far")))

    grad_gate2 = jnp.sum(grad * branch2, 0)
    down_bias_sum = column_sums(grad_b2)
    grad_shift2 = jnp.sum(back2, 0)
    grad_scale2 = jnp.sum(back2 * norm2, 0)
    grad_mid = grad + normalize_back(back2 * (1.0 + scale2), norm2, inverse2)
    grad_b1 = (gate1 * grad_mid).astype(BF16)
    grad_gate1 = jnp.sum(grad_mid * branch1, 0)
    merge_bias_sum = column_sums(grad_b1)
    grad_att_own = times_transposed(grad_b1, merge_own).astype(BF16)
    grad_att_other = times_transposed(grad_b1, merge_other).astype(BF16)
    merge_total = outer_rows(
        grad_b1, jnp.concatenate([attended_own, attended_other], 1)
    ).astype(BF16).reshape(8, 2, -1, 2 * columns)
    merge_sent = swap(pick(merge_total, 1 - core, 1), "dp", 1)
    merge_total = (pick(merge_total, core, 1).astype(F32) + merge_sent.astype(F32)).astype(BF16)
    merge_grad = reduce_blocks(merge_total.reshape(-1, 2 * columns), ("near", "x", "far"))
    grad_att_own = after(grad_att_own, down_total, up_total, merge_total)

    grads_own, pairs_own = attend_back(qkv_own, attended_own, grad_att_own, logsum_own)
    grad_att_other = after(grad_att_other, grads_own)
    grads_other, pairs_other = attend_back(qkv_other, attended_other, grad_att_other, logsum_other)
    heads_grad = reduce_blocks(
        feature_grad(normed1, normed1_peer, pairs_own, pairs_other), ("x", "near", "far")
    )
    heads_grad = join_cores(heads_grad.reshape(heads_grad.shape[0], 3, columns // 2))
    grad_n1 = times_transposed(grads_own, heads_own) + times_transposed(grads_other, heads_other)
    grad_shift1 = jnp.sum(grad_n1, 0)
    grad_scale1 = jnp.sum(grad_n1 * norm1, 0)
    grad_latent = grad_mid + normalize_back(grad_n1 * (1.0 + scale1), norm1, inverse1)
    latent_sent = swap(grad_latent[half:].astype(BF16), "tensor", 1).astype(F32)
    latent_grad = place(grad_latent[None, :half], latent_sent[None], side)

    def query_value_sums(grads):
        return jnp.concatenate(
            [column_sums(grads[:, :columns]), column_sums(grads[:, 2 * columns :])]
        )

    def by_side(rows):
        rows = rows.reshape(rows.shape[:-1] + (2, features))
        return pick(rows, side, rows.ndim - 2), pick(rows, 1 - side, rows.ndim - 2)

    grad_mod = jnp.stack(
        [grad_shift1, grad_scale1, grad_gate1, grad_shift2, grad_scale2, grad_gate2]
    ).astype(BF16)
    grad_mod_own, grad_mod_sent = by_side(grad_mod)
    grad_mod_slots = place(
        grad_mod_own[None], swap(grad_mod_sent, "tensor", 1)[None], side
    )
    merge_own_sum, merge_other_sum = by_side(merge_bias_sum)
    down_own_sum, down_other_sum = by_side(down_bias_sum)
    bias_own = jnp.concatenate(
        [query_value_sums(grads_own), merge_own_sum, up_sums_own[0], down_own_sum]
    )
    bias_other = jnp.concatenate(
        [query_value_sums(grads_other), merge_other_sum, up_sums_other[0], down_other_sum]
    )
    bias_total = bias_own + swap(bias_other, "tensor", 1)
    bias_total = jnp.sum(lax.all_gather(bias_total, "dp", axis=0), 0)
    grad_mod_all = lax.all_gather(grad_mod_slots, "dp", axis=0, tiled=True)
    rows_here = model_width // lax.axis_size("dp")
    silu_rows = lax.dynamic_slice_in_dim(silu_all, place_dp * rows_here, rows_here, 1)
    modulate_grad = jnp.einsum("sd,skc->dkc", silu_rows, grad_mod_all, preferred_element_type=F32)
    modulate_bias_grad = jnp.sum(grad_mod_all.astype(F32), 0)
    cond_partial = jnp.einsum(
        "dkc,skc->sd", modulate_weight[0], grad_mod_slots, preferred_element_type=F32
    )
    cond_total = cond_partial + swap(cond_partial, "tensor", 1)
    condition_grad = jax.vjp(jax.nn.silu, condition.astype(F32))[1](cond_total)[0]
    edges = (0, 2 * columns, 2 * columns + features, 2 * columns + features + hidden_here, None)
    heads_bias_grad, merge_bias_grad, up_bias_grad, down_bias_grad = (
        bias_total[first:last] for first, last in zip(edges, edges[1:])
    )
    return (
        block_output,
        latent_grad,
        condition_grad,
        heads_grad[None],
        heads_bias_grad.reshape(1, 2, columns),
        merge_grad.T[None],
        merge_bias_grad[None],
        up_grad[None],
        up_bias_grad[None],
        down_grad.T[None],
        down_bias_grad[None],
        modulate_grad[None],
        modulate_bias_grad[None],
    )


def solution(mesh):
    in_specs = (
        P("dp", "tensor", None),
        P("dp", None),
        P("dp", "tensor", None),
        P("dp"),
        P(None, None, None, "tensor"),
        P(None, None, "tensor"),
        P(None, "tensor", None),
        P(),
        P(None, None, "tensor"),
        P(None, "tensor"),
        P(None, "tensor", None),
        P(),
        P(None, None, None, "tensor"),
        P(None, None, "tensor"),
    )
    out_specs = (
        P("dp", "tensor", None),
        P("dp", "tensor", None),
        P("dp", None),
        P(None, "dp", None, "tensor"),
        P(None, None, "tensor"),
        P(None, "tensor", "dp"),
        P(None, "tensor"),
        P(None, "dp", "tensor"),
        P(None, "tensor"),
        P(None, "tensor", "dp"),
        P(None, "tensor"),
        P(None, "dp", None, "tensor"),
        P(None, None, "tensor"),
    )
    whole_slots = mesh.shape["tensor"] == 2 and mesh.shape["dp"] == 16
    return jax.shard_map(
        slot_device if whole_slots else per_device, mesh=mesh, in_specs=in_specs, out_specs=out_specs, check_vma=False
    )
```

```python
import functools
import math

import jax
import jax.numpy as jnp
from jax import lax
from jax.experimental import pallas as pl
from jax.experimental.pallas import tpu as pltpu
from jax.sharding import PartitionSpec as P

HEAD_DIM = 72
QUERY_BLOCK = 512


epsilon = 1e-06


def normalize(stream):
    average = jnp.mean(stream, -1, keepdims=True)
    centered = stream - average
    variance = jnp.mean(centered * centered, -1, keepdims=True)
    inverse = lax.rsqrt(variance + epsilon)
    return (centered * inverse, inverse)


def normalize_back(grad_norm, normed, inverse):
    first_mean = jnp.mean(grad_norm, -1, keepdims=True)
    second_mean = jnp.mean(grad_norm * normed, -1, keepdims=True)
    return inverse * (grad_norm - first_mean - normed * second_mean)


def gelu_tanh(values):
    return jax.nn.gelu(values, approximate=True)


def column_sums(operand):
    return jnp.sum(operand.astype(jnp.float32), 0)


def outer_rows(operand, other):
    return lax.dot_general(
        operand, other, (((0,), (0,)), ((), ())), preferred_element_type=jnp.float32
    )


def times_transposed(operand, weight):
    return lax.dot_general(
        operand, weight, (((1,), (1,)), ((), ())), preferred_element_type=jnp.float32
    )


def gather_tokens(values):
    return lax.all_gather(values, "tensor", axis=0, tiled=True)


def gather_grads(values):
    return lax.all_gather(values, "tensor", axis=0, tiled=True)


def scatter_branch(operand, weight):

    def partial_rows(first_row, row_count):
        return jnp.dot(operand, weight, preferred_element_type=jnp.float32)

    return lax.psum_scatter(
        partial_rows(
            jnp.int32(0), operand.shape[0] // lax.axis_size("tensor") * lax.axis_size("tensor")
        ).astype(jnp.bfloat16),
        "tensor",
        scatter_dimension=0,
        tiled=True,
    ).astype(jnp.float32)


def scatter_inputs(operand, weight):

    def partial_rows(first_row, row_count):
        return times_transposed(operand, weight)

    return lax.psum_scatter(
        partial_rows(
            jnp.int32(0), operand.shape[0] // lax.axis_size("tensor") * lax.axis_size("tensor")
        ).astype(jnp.bfloat16),
        "tensor",
        scatter_dimension=0,
        tiled=True,
    ).astype(jnp.float32)


def stack_member(layer_tuples, member):
    return jnp.stack([entry_tuple[member] for entry_tuple in layer_tuples])


def attend_forward(queries, key_rows, value_rows):
    length, heads_here = (queries.shape[0], queries.shape[1])
    blocks = length // QUERY_BLOCK
    score_scale = HEAD_DIM ** (-0.5)

    def one_block(query_block):
        scores = (
            jnp.einsum("qhd,khd->hqk", query_block, key_rows, preferred_element_type=jnp.float32)
            * score_scale
        )
        row_max = jnp.max(scores, -1, keepdims=True)
        exponent = jnp.exp(scores - row_max)
        row_total = jnp.sum(exponent, -1, keepdims=True)
        attn_probs = (exponent / row_total).astype(jnp.bfloat16)
        attended = jnp.einsum(
            "hqk,khd->qhd", attn_probs, value_rows, preferred_element_type=jnp.float32
        )
        return (attended.astype(jnp.bfloat16), (row_max + jnp.log(row_total))[:, :, 0])

    attended, logsum = lax.map(
        one_block, queries.reshape(blocks, QUERY_BLOCK, heads_here, HEAD_DIM)
    )
    return (attended.reshape(length, heads_here * HEAD_DIM), logsum)


def attend_backward(queries, key_rows, value_rows, logsum, grad_attended):
    length, heads_here = (queries.shape[0], queries.shape[1])
    blocks = length // QUERY_BLOCK
    score_scale = HEAD_DIM ** (-0.5)
    block_shape = (blocks, QUERY_BLOCK, heads_here, HEAD_DIM)

    def one_block(running, inputs_here):
        grad_keys, grad_values = running
        query_block, grad_block, logsum_block = inputs_here
        scores = (
            jnp.einsum("qhd,khd->hqk", query_block, key_rows, preferred_element_type=jnp.float32)
            * score_scale
        )
        attn_probs = jnp.exp(scores - logsum_block[:, :, None])
        grad_values = grad_values + jnp.einsum(
            "hqk,qhd->khd",
            attn_probs.astype(jnp.bfloat16),
            grad_block,
            preferred_element_type=jnp.float32,
        )
        grad_probs = jnp.einsum(
            "qhd,khd->hqk", grad_block, value_rows, preferred_element_type=jnp.float32
        )
        row_dot = jnp.sum(attn_probs * grad_probs, -1, keepdims=True)
        grad_scores = (attn_probs * (grad_probs - row_dot)).astype(jnp.bfloat16)
        grad_queries = (
            jnp.einsum("hqk,khd->qhd", grad_scores, key_rows, preferred_element_type=jnp.float32)
            * score_scale
        )
        grad_keys = (
            grad_keys
            + jnp.einsum(
                "hqk,qhd->khd", grad_scores, query_block, preferred_element_type=jnp.float32
            )
            * score_scale
        )
        return ((grad_keys, grad_values), grad_queries.astype(jnp.bfloat16))

    zeros_kv = jnp.zeros((length, heads_here, HEAD_DIM), jnp.float32)
    scanned = (queries.reshape(block_shape), grad_attended.reshape(block_shape), logsum)
    (grad_keys, grad_values), grad_queries = lax.scan(one_block, (zeros_kv, zeros_kv), scanned)
    flat_shape = (length, heads_here * HEAD_DIM)
    return (
        grad_queries.reshape(flat_shape),
        grad_keys.astype(jnp.bfloat16).reshape(flat_shape),
        grad_values.astype(jnp.bfloat16).reshape(flat_shape),
    )


def forward_layer(stream, modulation, layer_weights, heads_here):
    (
        flat_heads,
        heads_offset,
        merge_weight,
        merge_bias,
        up_weight,
        up_bias,
        down_weight,
        down_bias,
    ) = layer_weights
    length = stream.shape[0] * lax.axis_size("tensor")
    columns = flat_heads.shape[1] // 3
    norm_first, inverse_first = normalize(stream)
    normed_first = (norm_first * (1.0 + modulation[1]) + modulation[0]).astype(jnp.bfloat16)
    gathered_first = gather_tokens(normed_first)
    projected = (
        jnp.dot(gathered_first, flat_heads, preferred_element_type=jnp.float32) + heads_offset
    ).astype(jnp.bfloat16)
    split_shape = (length, heads_here, HEAD_DIM)
    queries = projected[:, :columns].reshape(split_shape)
    key_rows = projected[:, columns : 2 * columns].reshape(split_shape)
    value_rows = projected[:, 2 * columns :].reshape(split_shape)
    attended, logsum = attend_forward(queries, key_rows, value_rows)
    branch_first = scatter_branch(attended, merge_weight) + merge_bias.astype(jnp.float32)
    stream_mid = stream + modulation[2] * branch_first
    norm_second, inverse_second = normalize(stream_mid)
    normed_second = (norm_second * (1.0 + modulation[4]) + modulation[3]).astype(jnp.bfloat16)
    gathered_second = gather_tokens(normed_second)
    hidden_pre = jnp.dot(
        gathered_second, up_weight, preferred_element_type=jnp.float32
    ) + up_bias.astype(jnp.float32)
    hidden = gelu_tanh(hidden_pre).astype(jnp.bfloat16)
    branch_second = scatter_branch(hidden, down_weight) + down_bias.astype(jnp.float32)
    stream_next = stream_mid + modulation[5] * branch_second
    first_input, second_input = (gathered_first, gathered_second)
    kept = (
        norm_first,
        inverse_first,
        first_input,
        queries,
        key_rows,
        value_rows,
        logsum,
        attended,
        branch_first,
        norm_second,
        inverse_second,
        second_input,
        hidden_pre,
        hidden,
        branch_second,
    )
    return (stream_next, kept)


def backward_layer(grad_stream, modulation, layer_weights, kept):
    (
        flat_heads,
        heads_offset,
        merge_weight,
        merge_bias,
        up_weight,
        up_bias,
        down_weight,
        down_bias,
    ) = layer_weights
    (
        norm_first,
        inverse_first,
        first_input,
        queries,
        key_rows,
        value_rows,
        logsum,
        attended,
        branch_first,
        norm_second,
        inverse_second,
        second_input,
        hidden_pre,
        hidden,
        branch_second,
    ) = kept
    model_width = flat_heads.shape[0]
    columns = flat_heads.shape[1] // 3
    grad_branch_second = (modulation[5] * grad_stream).astype(jnp.bfloat16)
    grad_gate_second = jnp.sum(grad_stream * branch_second, 0)
    grad_down_bias = column_sums(grad_branch_second)
    gathered_grad = gather_grads(grad_branch_second)
    down_grad = outer_rows(hidden, gathered_grad)
    grad_hidden = times_transposed(gathered_grad, down_weight)
    grad_pre = jax.vjp(gelu_tanh, hidden_pre)[1](grad_hidden)[0].astype(jnp.bfloat16)
    up_bias_grad = column_sums(grad_pre)
    up_grad = outer_rows(second_input, grad_pre)
    grad_normed_second = scatter_inputs(grad_pre, up_weight)
    grad_shift_second = jnp.sum(grad_normed_second, 0)
    grad_scale_second = jnp.sum(grad_normed_second * norm_second, 0)
    grad_mid = grad_stream + normalize_back(
        grad_normed_second * (1.0 + modulation[4]), norm_second, inverse_second
    )
    grad_branch_first = (modulation[2] * grad_mid).astype(jnp.bfloat16)
    grad_gate_first = jnp.sum(grad_mid * branch_first, 0)
    grad_merge_bias = column_sums(grad_branch_first)
    gathered_grad = gather_grads(grad_branch_first)
    merge_grad = outer_rows(attended, gathered_grad)
    grad_attended = times_transposed(gathered_grad, merge_weight).astype(jnp.bfloat16)
    grad_queries, grad_keys, grad_values = attend_backward(
        queries, key_rows, value_rows, logsum, grad_attended
    )
    grad_projected = jnp.concatenate([grad_queries, grad_keys, grad_values], 1)
    heads_bias_grad = jnp.stack([column_sums(grad_queries), column_sums(grad_values)])
    heads_grad = outer_rows(first_input, grad_projected).reshape(model_width, 3, columns)
    grad_normed_first = scatter_inputs(grad_projected, flat_heads)
    grad_shift_first = jnp.sum(grad_normed_first, 0)
    grad_scale_first = jnp.sum(grad_normed_first * norm_first, 0)
    grad_before = grad_mid + normalize_back(
        grad_normed_first * (1.0 + modulation[1]), norm_first, inverse_first
    )
    extra = jnp.stack(
        [
            grad_shift_first,
            grad_scale_first,
            grad_gate_first,
            grad_shift_second,
            grad_scale_second,
            grad_gate_second,
            grad_merge_bias,
            grad_down_bias,
        ]
    )
    return (
        grad_before,
        (heads_grad, heads_bias_grad, merge_grad, up_grad, up_bias_grad, down_grad),
        extra,
    )


def per_device(
    latents,
    condition,
    cotangent,
    group_counts,
    heads_weight,
    heads_bias,
    merge_weight,
    merge_bias,
    up_weight,
    up_bias,
    down_weight,
    down_bias,
    modulate_weight,
    modulate_bias,
):
    slot_count = latents.shape[0]
    model_width = latents.shape[2]
    layer_count = heads_weight.shape[0]
    columns = heads_weight.shape[3]
    heads_here = columns // HEAD_DIM
    silu_cond = jax.nn.silu(condition.astype(jnp.float32)).astype(jnp.bfloat16)
    local_mod = jnp.einsum(
        "sd,bdkc->sbkc", silu_cond, modulate_weight, preferred_element_type=jnp.float32
    ) + modulate_bias.astype(jnp.float32)
    modulation_all = lax.all_gather(local_mod, "tensor", axis=3, tiled=True)
    flat_heads = heads_weight.reshape(layer_count, model_width, 3 * columns)
    zero_bias = jnp.zeros((layer_count, columns), heads_bias.dtype)
    heads_offset = (
        jnp.stack([heads_bias[:, 0], zero_bias, heads_bias[:, 1]], 1)
        .reshape(layer_count, 3 * columns)
        .astype(jnp.float32)
    )
    per_layer = [
        (
            flat_heads[0],
            heads_offset[0],
            merge_weight[0],
            merge_bias[0],
            up_weight[0],
            up_bias[0],
            down_weight[0],
            down_bias[0],
        )
    ]
    layer_sums = [None] * layer_count
    modulate_sum = jnp.zeros(modulate_weight.shape, jnp.float32)
    modulate_bias_sum = jnp.zeros(modulate_bias.shape, jnp.float32)
    merge_bias_sum = jnp.zeros((layer_count, columns), jnp.float32)
    down_bias_sum = jnp.zeros((layer_count, columns), jnp.float32)
    output_list, latent_list, condition_list = ([], [], [])
    for slot_index in range(slot_count):
        live_flag = (slot_index < group_counts[0]).astype(jnp.float32)
        stream = latents[slot_index].astype(jnp.float32)
        layer_index = 0
        stream, kept = forward_layer(
            stream, modulation_all[slot_index, layer_index], per_layer[layer_index], heads_here
        )
        saved_layers = [kept]
        output_list.append(stream.astype(jnp.bfloat16))
        grad_stream = cotangent[slot_index].astype(jnp.float32) * live_flag
        extras = [None] * layer_count
        for layer_index in reversed(range(layer_count)):
            grad_stream, layer_grads, extra = backward_layer(
                grad_stream,
                modulation_all[slot_index, layer_index],
                per_layer[layer_index],
                saved_layers[layer_index],
            )
            if layer_sums[layer_index] is None:
                layer_sums[layer_index] = layer_grads
            else:
                layer_sums[layer_index] = jax.tree.map(
                    jnp.add, layer_sums[layer_index], layer_grads
                )
            extras[layer_index] = extra
        latent_list.append(grad_stream)
        shared = lax.psum_scatter(
            jnp.stack(extras).astype(jnp.bfloat16), "tensor", scatter_dimension=2, tiled=True
        ).astype(jnp.float32)
        grad_mod = shared[:, :6].astype(jnp.bfloat16)
        modulate_sum = modulate_sum + jnp.einsum(
            "d,bkc->bdkc", silu_cond[slot_index], grad_mod, preferred_element_type=jnp.float32
        )
        modulate_bias_sum = modulate_bias_sum + grad_mod.astype(jnp.float32)
        merge_bias_sum = merge_bias_sum + shared[:, 6]
        down_bias_sum = down_bias_sum + shared[:, 7]
        cond_partial = jnp.einsum(
            "bdkc,bkc->d", modulate_weight, grad_mod, preferred_element_type=jnp.float32
        )
        cond_total = lax.psum(cond_partial, "tensor")
        silu_grad = jax.vjp(jax.nn.silu, condition[slot_index].astype(jnp.float32))[1](cond_total)[
            0
        ]
        condition_list.append(silu_grad)
    weight_grads = (
        lax.psum_scatter(
            stack_member(layer_sums, 0).astype(jnp.bfloat16), "dp", scatter_dimension=1, tiled=True
        ).astype(jnp.float32),
        lax.psum_scatter(
            stack_member(layer_sums, 2).astype(jnp.bfloat16), "dp", scatter_dimension=2, tiled=True
        ).astype(jnp.float32),
        lax.psum_scatter(
            stack_member(layer_sums, 3).astype(jnp.bfloat16), "dp", scatter_dimension=1, tiled=True
        ).astype(jnp.float32),
        lax.psum_scatter(
            stack_member(layer_sums, 5).astype(jnp.bfloat16), "dp", scatter_dimension=2, tiled=True
        ).astype(jnp.float32),
        lax.psum_scatter(
            modulate_sum.astype(jnp.bfloat16), "dp", scatter_dimension=1, tiled=True
        ).astype(jnp.float32),
    )
    bias_grads = lax.psum(
        (
            stack_member(layer_sums, 1),
            merge_bias_sum,
            stack_member(layer_sums, 4),
            down_bias_sum,
            modulate_bias_sum,
        ),
        "dp",
    )
    block_output = jnp.stack(output_list)
    latent_grad = jnp.stack(latent_list)
    condition_grad = jnp.stack(condition_list)
    return (
        block_output,
        latent_grad,
        condition_grad,
        weight_grads[0],
        bias_grads[0],
        weight_grads[1],
        bias_grads[1],
        weight_grads[2],
        bias_grads[2],
        weight_grads[3],
        bias_grads[3],
        weight_grads[4],
        bias_grads[4],
    )


F32 = jnp.float32
BF16 = jnp.bfloat16
SCORE_SCALE = HEAD_DIM ** (-0.5)
SCORE_LOG2 = SCORE_SCALE * math.log2(math.e)
VMEM_BYTES = 60 * 2**20


def cost(weight):
    return pl.CostEstimate(flops=weight * 50 * 10**8, bytes_accessed=10**5, transcendentals=0)


def dot_dims(left, right, left_dim, right_dim):
    return lax.dot_general(
        left, right, (((left_dim,), (right_dim,)), ((), ())), preferred_element_type=F32
    )


def head_slice(part, head, width):
    return slice(part * width + head * HEAD_DIM, part * width + (head + 1) * HEAD_DIM)


def attend_kernel(heads, qkv_ref, out_ref, logsum_ref):
    width = heads * HEAD_DIM
    rows_here = out_ref.shape[0]
    rows = pl.ds(pl.multiple_of(pl.program_id(0) * rows_here, rows_here), rows_here)
    for head in range(heads):
        queries = qkv_ref[rows, head_slice(0, head, width)]
        scores = dot_dims(qkv_ref[:, head_slice(1, head, width)], queries, 1, 1)
        top = jnp.max(scores, 0, keepdims=True)
        exponent = jnp.exp2((scores - top) * SCORE_LOG2)
        total = jnp.sum(exponent, 0, keepdims=True)
        mixed = dot_dims(qkv_ref[:, head_slice(2, head, width)], exponent.astype(BF16), 0, 0)
        out_ref[:, head_slice(0, head, width)] = (mixed / total).T.astype(BF16)
        logsum_ref[head : head + 1, :] = top * SCORE_LOG2 + jnp.log2(total)


def attend(qkv, query_rows=512):
    tokens, width = qkv.shape[0], qkv.shape[1] // 3
    heads = width // HEAD_DIM
    return pl.pallas_call(
        functools.partial(attend_kernel, heads),
        grid=(tokens // query_rows,),
        in_specs=[pl.BlockSpec((tokens, 3 * width), lambda i: (0, 0))],
        out_specs=[
            pl.BlockSpec((query_rows, width), lambda i: (i, 0)),
            pl.BlockSpec((heads, query_rows), lambda i: (0, i)),
        ],
        out_shape=[
            jax.ShapeDtypeStruct((tokens, width), BF16),
            jax.ShapeDtypeStruct((heads, tokens), F32),
        ],
        compiler_params=pltpu.CompilerParams(vmem_limit_bytes=VMEM_BYTES),
        cost_estimate=cost(18),
    )(qkv)


def attend_back_kernel(
    heads, key_rows, steps, core_ref,
    qkv_ref, out_ref, grad_ref, logsum_ref, grads_ref, sent_ref, kept_ref, dot_ref, query_ref,
):
    step = pl.program_id(0)
    width = heads * HEAD_DIM
    rows = pl.ds(pl.multiple_of(step * key_rows, key_rows), key_rows)

    @pl.when(step == 0)
    def _():
        owner = lax.broadcasted_iota(jnp.int32, (heads, width), 1)
        first = lax.broadcasted_iota(jnp.int32, (heads, width), 0) * HEAD_DIM
        member = ((owner >= first) & (owner < first + HEAD_DIM)).astype(BF16)
        product = grad_ref[...].astype(F32) * out_ref[...].astype(F32)
        high = product.astype(BF16)
        low = (product - high.astype(F32)).astype(BF16)
        dot_ref[...] = dot_dims(member, high, 1, 1) + dot_dims(member, low, 1, 1)
        query_ref[...] = jnp.zeros_like(query_ref)

    def store(part, head, rows, value):
        grads_ref[rows, head_slice(part, head, width)] = value

    for head in range(heads):
        queries = qkv_ref[:, head_slice(0, head, width)]
        keys = qkv_ref[rows, head_slice(1, head, width)]
        grad = grad_ref[:, head_slice(0, head, width)]
        scores = dot_dims(keys, queries, 1, 1)
        probs = jnp.exp2(scores * SCORE_LOG2 - logsum_ref[head : head + 1, :])
        grad_probs = dot_dims(qkv_ref[rows, head_slice(2, head, width)], grad, 1, 1)
        grad_scores = (probs * (grad_probs - dot_ref[head : head + 1, :])).astype(BF16)
        grad_values = jnp.dot(probs.astype(BF16), grad, preferred_element_type=F32)
        store(2, head, rows, grad_values.astype(BF16))
        grad_keys = jnp.dot(grad_scores, queries, preferred_element_type=F32) * SCORE_SCALE
        store(1, head, rows, grad_keys.astype(BF16))
        query_ref[head] += dot_dims(keys, grad_scores, 0, 0)

    @pl.when(step == steps - 1)
    def _():
        for head in range(heads):
            store(0, head, slice(None), (query_ref[head] * SCORE_SCALE).T.astype(BF16))
        half = width // 2
        for first in range(2):

            @pl.when(core_ref[0] == first)
            def _():
                for part in range(3):
                    here, there = (part * width + side * half for side in (first, 1 - first))
                    to = slice(part * half, (part + 1) * half)
                    kept_ref[:, to] = grads_ref[:, here : here + half]
                    sent_ref[:, to] = grads_ref[:, there : there + half]
                rest = slice(3 * half, kept_ref.shape[1])
                kept_ref[:, rest] = jnp.zeros_like(kept_ref[:, rest])
                sent_ref[:, rest] = jnp.zeros_like(sent_ref[:, rest])


def attend_back(core, qkv, attended, grad_attended, logsum, key_rows=512):
    tokens, width = attended.shape
    heads = width // HEAD_DIM
    steps = tokens // key_rows
    whole = lambda *shape: pl.BlockSpec(shape, lambda i, core_ref: (0,) * len(shape))
    half = (tokens, -(-3 * width // 256) * 128)
    return pl.pallas_call(
        functools.partial(attend_back_kernel, heads, key_rows, steps),
        grid_spec=pltpu.PrefetchScalarGridSpec(
            num_scalar_prefetch=1,
            grid=(steps,),
            in_specs=[
                whole(tokens, 3 * width), whole(tokens, width), whole(tokens, width),
                whole(heads, tokens),
            ],
            out_specs=[whole(tokens, 3 * width), whole(*half), whole(*half)],
            scratch_shapes=[
                pltpu.VMEM((heads, tokens), F32),
                pltpu.VMEM((heads, HEAD_DIM, tokens), F32),
            ],
        ),
        out_shape=[
            jax.ShapeDtypeStruct((tokens, 3 * width), BF16),
            jax.ShapeDtypeStruct(half, BF16),
            jax.ShapeDtypeStruct(half, BF16),
        ],
        compiler_params=pltpu.CompilerParams(vmem_limit_bytes=VMEM_BYTES),
        cost_estimate=cost(32),
    )(core, qkv, attended, grad_attended, logsum)


GELU_OUTER = math.sqrt(2 / math.pi)
GELU_CUBIC = 0.044715


def gelu_and_slope(values):
    square = values * values
    tanh = jnp.tanh(values * (GELU_OUTER + GELU_OUTER * GELU_CUBIC * square))
    half = 0.5 + 0.5 * tanh
    inner = 0.5 * GELU_OUTER + 1.5 * GELU_OUTER * GELU_CUBIC * square
    return values * half, half + values * (1.0 - tanh * tanh) * inner


def feed_kernel(
    token_rows, carried, core_ref, normed_ref, grad_ref, up_ref, bias_ref, down_ref, *refs
):
    if carried:
        branch_in, normed_in = refs[:2]
        refs = refs[2:]
    branch_ref, back_ref, hidden_sent, hidden_kept, pre_sent, pre_kept, bias_grad_ref = refs
    chunk = pl.program_id(0)
    bias_grad_ref[...] = jnp.zeros_like(bias_grad_ref)

    def block(hidden_ref, pre_ref, index, _):
        rows = pl.ds(pl.multiple_of(index * token_rows, token_rows), token_rows)
        pre = jnp.dot(normed_ref[rows, :], up_ref[...], preferred_element_type=F32)
        grad_hidden = dot_dims(grad_ref[rows, :], down_ref[...], 1, 1)
        hidden, slope = gelu_and_slope(pre + bias_ref[...])
        hidden = hidden.astype(BF16)
        grad_pre = (grad_hidden * slope).astype(BF16)
        bias_grad_ref[...] += jnp.sum(grad_pre.astype(F32), 0, keepdims=True)
        hidden_ref[rows, :] = hidden
        pre_ref[rows, :] = grad_pre
        branch = jnp.dot(hidden, down_ref[...], preferred_element_type=F32)
        back = dot_dims(grad_pre, up_ref[...], 1, 1)
        if hidden_ref is hidden_kept:
            branch_ref[rows, :] += branch
            back_ref[rows, :] += back
        else:
            branch_ref[rows, :] = branch + branch_in[rows, :] if carried else branch
            back_ref[rows, :] = back + normed_in[rows, :] if carried else back
        return 0

    for step, refs_here in enumerate(((hidden_sent, pre_sent), (hidden_kept, pre_kept))):

        @pl.when(chunk == step)
        def _():
            lax.fori_loop(
                0, normed_ref.shape[0] // token_rows, functools.partial(block, *refs_here), 0
            )


def feed(core, normed, grad, up, bias, down, carried=(), token_rows=256):
    tokens, model_width = normed.shape
    hidden_here = up.shape[1]
    width = hidden_here // 2
    chunk = lambda j, core_ref: lax.rem(j + 1 + core_ref[0], 2)
    single = pl.Buffered(1)
    whole = lambda: pl.BlockSpec((tokens, model_width), lambda j, c: (0, 0), pipeline_mode=single)
    part = lambda: pl.BlockSpec((tokens, width), lambda j, c: (0, 0), pipeline_mode=single)
    return pl.pallas_call(
        functools.partial(feed_kernel, token_rows, len(carried) > 0),
        grid_spec=pltpu.PrefetchScalarGridSpec(
            num_scalar_prefetch=1,
            grid=(2,),
            in_specs=[
                whole(), whole(),
                pl.BlockSpec((model_width, width), lambda j, c: (0, chunk(j, c))),
                pl.BlockSpec((1, width), lambda j, c: (0, chunk(j, c))),
                pl.BlockSpec((width, model_width), lambda j, c: (chunk(j, c), 0)),
            ] + [whole() for _ in carried],
            out_specs=[
                whole(), whole(), part(), part(), part(), part(),
                pl.BlockSpec((1, width), lambda j, c: (0, chunk(j, c))),
            ],
        ),
        out_shape=[jax.ShapeDtypeStruct((tokens, model_width), F32)] * 2
        + [jax.ShapeDtypeStruct((tokens, width), BF16)] * 4
        + [jax.ShapeDtypeStruct((1, hidden_here), F32)],
        compiler_params=pltpu.CompilerParams(vmem_limit_bytes=VMEM_BYTES),
        cost_estimate=cost(44),
    )(core, normed, grad, up, bias, down, *carried)


def weight_grad_kernel(chunks, blocks, where_ref, left_mine, left_peer, *refs):
    rights, outs, left_ref = refs[: 2 * chunks], refs[2 * chunks : -1], refs[-1]
    tokens, model_width = left_mine.shape
    rows = model_width // blocks
    for first, left in ((0, left_mine), (tokens, left_peer)):
        turned = left[...].T
        for block in range(blocks):
            to = pl.ds(pl.multiple_of(where_ref[block] * rows, rows), rows)
            left_ref[to, first : first + tokens] = turned[block * rows : (block + 1) * rows]
    for chunk in range(chunks):
        for part in range(2):
            half = slice(part * model_width // 2, (part + 1) * model_width // 2)
            mine, peer = rights[2 * chunk : 2 * chunk + 2]
            total = jnp.dot(left_ref[half, :tokens], mine[...], preferred_element_type=F32)
            total += jnp.dot(left_ref[half, tokens:], peer[...], preferred_element_type=F32)
            total = total.astype(BF16)
            for block in range(blocks // 2):
                outs[2 * chunk + part][block] = total[block * rows : (block + 1) * rows]


def weight_grad(where, left_mine, left_peer, *rights):
    tokens, model_width = left_mine.shape
    blocks = where.shape[0]
    chunks = len(rights) // 2
    width = rights[0].shape[1]
    out = jax.ShapeDtypeStruct((blocks // 2, model_width // blocks, width), BF16)
    whole = lambda value: pl.BlockSpec(value.shape, lambda j, w: (0,) * len(value.shape))
    return pl.pallas_call(
        functools.partial(weight_grad_kernel, chunks, blocks),
        grid_spec=pltpu.PrefetchScalarGridSpec(
            num_scalar_prefetch=1,
            grid=(1,),
            in_specs=[whole(value) for value in (left_mine, left_peer) + rights],
            out_specs=[whole(out)] * (2 * chunks),
            scratch_shapes=[pltpu.VMEM((model_width, 2 * tokens), BF16)],
        ),
        out_shape=[out] * (2 * chunks),
        compiler_params=pltpu.CompilerParams(vmem_limit_bytes=VMEM_BYTES),
        cost_estimate=cost(13),
    )(where, left_mine, left_peer, *rights)


def add_split_kernel(base_ref, kept_ref, received_ref, *out_refs):
    for place, out_ref in enumerate(out_refs):
        block = lax.bitwise_xor(base_ref[0], place)
        total = kept_ref[block].astype(F32) + received_ref[block].astype(F32)
        out_ref[...] = total.astype(BF16)


def add_split(base, kept, received):
    blocks, rows, width = kept.shape
    out = jax.ShapeDtypeStruct((rows, width), BF16)
    whole = lambda *shape: pl.BlockSpec(shape, lambda j, b: (0,) * len(shape))
    return pl.pallas_call(
        add_split_kernel,
        grid_spec=pltpu.PrefetchScalarGridSpec(
            num_scalar_prefetch=1, grid=(1,),
            in_specs=[whole(*kept.shape)] * 2, out_specs=[whole(rows, width)] * blocks,
        ),
        out_shape=[out] * blocks,
        compiler_params=pltpu.CompilerParams(vmem_limit_bytes=VMEM_BYTES),
        cost_estimate=cost(2),
    )(base, kept, received)


def project_kernel(with_norm, *refs):
    refs = refs[2:] if with_norm > 1 else refs
    if with_norm:
        tokens_ref, rows_ref, weight_ref, offset_ref, normed_ref, out_ref = refs
        norm, _ = normalize(tokens_ref[...].astype(F32))
        normed = (norm * (1.0 + rows_ref[1:2]) + rows_ref[0:1]).astype(BF16)
        normed_ref[...] = normed
    else:
        tokens_ref, weight_ref, offset_ref, out_ref = refs
        normed = tokens_ref[...]
    out = jnp.dot(normed, weight_ref[...], preferred_element_type=F32) + offset_ref[...]
    out_ref[...] = out.astype(BF16)


def constant_block(shape):
    return pl.BlockSpec(shape, lambda i: (0,) * len(shape), pipeline_mode=pl.Buffered(1))


def row_blocks(rows, width, first=0):
    return pl.BlockSpec((rows, width), lambda i: (i + first, 0))


def project(normed, weight, offset, rows=256):
    tokens, model_width = normed.shape
    width = weight.shape[1]
    return pl.pallas_call(
        functools.partial(project_kernel, 0),
        grid=(tokens // rows,),
        in_specs=[
            row_blocks(rows, model_width), constant_block(weight.shape), constant_block((1, width)),
        ],
        out_specs=row_blocks(rows, width),
        out_shape=jax.ShapeDtypeStruct((tokens, width), BF16),
        compiler_params=pltpu.CompilerParams(vmem_limit_bytes=VMEM_BYTES),
        cost_estimate=cost(9),
    )(normed, weight, offset)


def normed_project(half, shifts, weight, offset, filled=None, rows=256):
    half_tokens, model_width = half.shape
    width = weight.shape[1]
    first = 0 if filled is None else half_tokens // rows
    held = [] if filled is None else list(filled)
    return pl.pallas_call(
        functools.partial(project_kernel, 1 if filled is None else 2),
        grid=(half_tokens // rows,),
        in_specs=[pl.BlockSpec(memory_space=pl.ANY)] * len(held)
        + [
            row_blocks(rows, model_width), constant_block(shifts.shape),
            constant_block(weight.shape), constant_block((1, width)),
        ],
        out_specs=[row_blocks(rows, model_width, first), row_blocks(rows, width, first)],
        out_shape=[
            jax.ShapeDtypeStruct((2 * half_tokens, model_width), BF16),
            jax.ShapeDtypeStruct((2 * half_tokens, width), BF16),
        ],
        input_output_aliases={0: 0, 1: 1} if held else {},
        compiler_params=pltpu.CompilerParams(vmem_limit_bytes=VMEM_BYTES),
        cost_estimate=cost(7),
    )(*held, half, shifts, weight, offset)


def halves(rows, width, blocks):
    half = blocks // 2
    return [
        pl.BlockSpec((rows, width), lambda i: (jnp.minimum(i, half - 1), 0)),
        pl.BlockSpec((rows, width), lambda i: (jnp.maximum(i - half, 0), 0)),
    ]


def merge_kernel(
    blocks, own_ref, other_ref, weight_own, weight_other, first_ref, second_ref, grad_ref, rows_ref,
    branch_ref, mid_ref, normed_ref, grad_b2_ref,
):
    gate1, bias, shift2, scale2, gate2 = (rows_ref[row : row + 1] for row in range(5))
    stream = jnp.where(pl.program_id(0) < blocks // 2, first_ref[...], second_ref[...])
    branch = jnp.dot(own_ref[...], weight_own[...], preferred_element_type=F32)
    branch += jnp.dot(other_ref[...], weight_other[...], preferred_element_type=F32)
    branch += bias
    branch_ref[...] = branch.astype(BF16)
    mid = stream.astype(F32) + gate1 * branch
    mid_ref[...] = mid
    norm, _ = normalize(mid)
    normed_ref[...] = (norm * (1.0 + scale2) + shift2).astype(BF16)
    grad_b2_ref[...] = (gate2 * grad_ref[...].astype(F32)).astype(BF16)


def merge(own, other, weight_own, weight_other, first, second, grad, vectors, rows=256):
    tokens, width = own.shape
    model_width = weight_own.shape[1]
    blocks = tokens // rows
    part = lambda: row_blocks(rows, width)
    full = lambda: row_blocks(rows, model_width)
    shape = lambda kind: jax.ShapeDtypeStruct((tokens, model_width), kind)
    return pl.pallas_call(
        functools.partial(merge_kernel, blocks),
        grid=(blocks,),
        in_specs=[
            part(), part(), constant_block(weight_own.shape), constant_block(weight_other.shape),
            *halves(rows, model_width, blocks), full(), constant_block(vectors.shape),
        ],
        out_specs=[full(), full(), full(), full()],
        out_shape=[shape(BF16), shape(F32), shape(BF16), shape(BF16)],
        compiler_params=pltpu.CompilerParams(vmem_limit_bytes=VMEM_BYTES),
        cost_estimate=cost(11),
    )(own, other, weight_own, weight_other, first, second, grad, vectors)


def add_row_sums(sums_ref, *values):
    @pl.when(pl.program_id(0) == 0)
    def _():
        sums_ref[...] = jnp.zeros_like(sums_ref)

    for row, value in enumerate(values):
        sums_ref[row : row + 1] += jnp.sum(value, 0, keepdims=True)


def middle_back_kernel(
    blocks, branch2_ref, back_ref, mid_ref, branch1_ref, grad_ref, grad_b2_ref, weight_own, weight_other,
    rows_ref, kept_ref, sent_ref, grad_mid_ref, grad_b1_ref, att_own_ref, att_other_ref, sums_ref,
):
    gate1, bias, scale2, gate2 = (rows_ref[row : row + 1] for row in range(4))
    block = pl.program_id(0)
    grad = grad_ref[...].astype(F32)
    mid = mid_ref[...]
    branch2 = branch2_ref[...] + bias
    output = (mid + gate2 * branch2).astype(BF16)

    @pl.when(block < blocks // 2)
    def _():
        kept_ref[...] = output

    @pl.when(block >= blocks // 2)
    def _():
        sent_ref[...] = output

    norm, inverse = normalize(mid)
    back = back_ref[...]
    grad_mid = grad + normalize_back(back * (1.0 + scale2), norm, inverse)
    grad_mid_ref[...] = grad_mid
    grad_b1 = (gate1 * grad_mid).astype(BF16)
    grad_b1_ref[...] = grad_b1
    att_own_ref[...] = dot_dims(grad_b1, weight_own[...], 1, 1).astype(BF16)
    att_other_ref[...] = dot_dims(grad_b1, weight_other[...], 1, 1).astype(BF16)
    add_row_sums(
        sums_ref, grad * branch2, grad_b2_ref[...].astype(F32), back, back * norm,
        grad_mid * branch1_ref[...].astype(F32), grad_b1.astype(F32),
    )


def middle_back(
    branch2, back, mid, branch1, grad, grad_b2, weight_own, weight_other, vectors, rows=256
):
    tokens, model_width = mid.shape
    width = weight_own.shape[0]
    blocks = tokens // rows
    full = lambda: row_blocks(rows, model_width)
    shape = lambda count, columns, kind: jax.ShapeDtypeStruct((count, columns), kind)
    return pl.pallas_call(
        functools.partial(middle_back_kernel, blocks),
        grid=(blocks,),
        in_specs=[full()] * 6
        + [
            constant_block(weight_own.shape), constant_block(weight_other.shape),
            constant_block(vectors.shape),
        ],
        out_specs=[
            *halves(rows, model_width, blocks), full(), full(), row_blocks(rows, width),
            row_blocks(rows, width), constant_block((8, model_width)),
        ],
        out_shape=[
            shape(tokens // 2, model_width, BF16), shape(tokens // 2, model_width, BF16),
            shape(tokens, model_width, F32), shape(tokens, model_width, BF16),
            shape(tokens, width, BF16), shape(tokens, width, BF16), shape(8, model_width, F32),
        ],
        compiler_params=pltpu.CompilerParams(vmem_limit_bytes=VMEM_BYTES),
        cost_estimate=cost(17),
    )(branch2, back, mid, branch1, grad, grad_b2, weight_own, weight_other, vectors)


def first_back_kernel(
    blocks, own_ref, other_ref, weight_own, weight_other, first_ref, second_ref, grad_mid_ref, rows_ref,
    kept_ref, sent_ref, sums_ref, own_sums_ref, other_sums_ref,
):
    block = pl.program_id(0)
    stream = jnp.where(block < blocks // 2, first_ref[...], second_ref[...])
    own, other = own_ref[...], other_ref[...]
    grad = dot_dims(own, weight_own[...], 1, 1) + dot_dims(other, weight_other[...], 1, 1)
    norm, inverse = normalize(stream.astype(F32))
    total = grad_mid_ref[...] + normalize_back(grad * (1.0 + rows_ref[0:1]), norm, inverse)

    @pl.when(block < blocks // 2)
    def _():
        kept_ref[...] = total

    @pl.when(block >= blocks // 2)
    def _():
        sent_ref[...] = total.astype(BF16)

    add_row_sums(sums_ref, grad, grad * norm)
    add_row_sums(own_sums_ref, own.astype(F32))
    add_row_sums(other_sums_ref, other.astype(F32))


def first_back(own, other, weight_own, weight_other, first, second, grad_mid, vectors, rows=256):
    tokens, model_width = grad_mid.shape
    width = own.shape[1]
    blocks = tokens // rows
    full = lambda: row_blocks(rows, model_width)
    part = lambda: row_blocks(rows, width)
    shape = jax.ShapeDtypeStruct
    return pl.pallas_call(
        functools.partial(first_back_kernel, blocks),
        grid=(blocks,),
        in_specs=[
            part(), part(), constant_block(weight_own.shape), constant_block(weight_other.shape),
            *halves(rows, model_width, blocks), full(), constant_block(vectors.shape),
        ],
        out_specs=[
            *halves(rows, model_width, blocks), constant_block((8, model_width)),
            constant_block((8, width)), constant_block((8, width)),
        ],
        out_shape=[
            shape((tokens // 2, model_width), F32), shape((tokens // 2, model_width), BF16),
            shape((8, model_width), F32), shape((8, width), F32), shape((8, width), F32),
        ],
        compiler_params=pltpu.CompilerParams(vmem_limit_bytes=VMEM_BYTES),
        cost_estimate=cost(21),
    )(own, other, weight_own, weight_other, first, second, grad_mid, vectors)


def bit_pairs(size, bit):
    return [(index, index ^ bit) for index in range(size)]


def swap(values, axis, bit):
    return lax.ppermute(values, axis, bit_pairs(lax.axis_size(axis), bit))


def pick(values, index, axis):
    return lax.dynamic_index_in_dim(values, index, axis, keepdims=False)


def after(values, *others):
    return lax.optimization_barrier((values, others))[0]


def place(first, second, index, axis=0):
    return jnp.where(
        index == 0,
        jnp.concatenate([first, second], axis),
        jnp.concatenate([second, first], axis),
    )


def cut_kernel(sizes, starts_ref, *refs):
    count = len(sizes)
    semaphores = refs[-1]
    copies = []
    for index, size in enumerate(sizes):
        rows = pl.ds(pl.multiple_of(starts_ref[index] * size, size), size)
        copies.append(
            pltpu.make_async_copy(
                refs[index].at[rows], refs[count + index], semaphores.at[index]
            )
        )
    for copy in copies:
        copy.start()
    for copy in copies:
        copy.wait()


def cut(values, places, sizes):
    return pl.pallas_call(
        functools.partial(cut_kernel, sizes),
        grid_spec=pltpu.PrefetchScalarGridSpec(
            num_scalar_prefetch=1,
            grid=(1,),
            in_specs=[pl.BlockSpec(memory_space=pl.ANY)] * len(sizes),
            out_specs=[pl.BlockSpec(memory_space=pltpu.VMEM)] * len(sizes),
            scratch_shapes=[pltpu.SemaphoreType.DMA((len(sizes),))],
        ),
        out_shape=[
            jax.ShapeDtypeStruct((size,) + value.shape[1:], value.dtype)
            for value, size in zip(values, sizes)
        ],
        compiler_params=pltpu.CompilerParams(vmem_limit_bytes=VMEM_BYTES),
        cost_estimate=cost(5),
    )(jnp.stack(places).astype(jnp.int32), *values)


def joined_kernel(count, places_ref, *refs):
    out_ref, semaphores = refs[count:]
    rows = refs[0].shape[0]
    copies = [
        pltpu.make_async_copy(
            refs[index],
            out_ref.at[pl.ds(pl.multiple_of(places_ref[index] * rows, rows), rows)],
            semaphores.at[index],
        )
        for index in range(count)
    ]
    for copy in copies:
        copy.start()
    for copy in copies:
        copy.wait()


def joined(pieces, places):
    count = len(pieces)
    rows, width = pieces[0].shape
    return pl.pallas_call(
        functools.partial(joined_kernel, count),
        grid_spec=pltpu.PrefetchScalarGridSpec(
            num_scalar_prefetch=1,
            grid=(1,),
            in_specs=[pl.BlockSpec(memory_space=pltpu.VMEM)] * count,
            out_specs=pl.BlockSpec(memory_space=pl.ANY),
            scratch_shapes=[pltpu.SemaphoreType.DMA((count,))],
        ),
        out_shape=jax.ShapeDtypeStruct((count * rows, width), pieces[0].dtype),
        compiler_params=pltpu.CompilerParams(vmem_limit_bytes=VMEM_BYTES),
        cost_estimate=cost(5),
    )(places, *pieces)


def gather_dp(values):
    size = lax.axis_size("dp")
    here = lax.axis_index("dp")
    step = 1
    while step < size:
        values = place(values, swap(values, "dp", step), lax.rem(here // step, 2))
        step *= 2
    return values


def sum_dp(values):
    step = 1
    while step < lax.axis_size("dp"):
        values = values + swap(values, "dp", step)
        step *= 2
    return values


def slot_device(
    latents,
    condition,
    cotangent,
    group_counts,
    heads_weight,
    heads_bias,
    merge_weight,
    merge_bias,
    up_weight,
    up_bias,
    down_weight,
    down_bias,
    modulate_weight,
    modulate_bias,
):
    side = lax.axis_index("tensor")
    place_dp = lax.axis_index("dp")
    core, x_bit, near, far = (lax.rem(place_dp // step, 2) for step in (1, 2, 4, 8))
    bits = (far, near, x_bit)
    half, model_width = latents.shape[1:]
    columns = heads_weight.shape[3]
    features = modulate_weight.shape[3]
    hidden_here = up_weight.shape[2]
    merge_own, up_own, down_own = merge_weight[0], up_weight[0], down_weight[0]
    padded_rows = lambda *rows: jnp.pad(jnp.stack(rows), ((0, 8 - len(rows)), (0, 0)))
    bit_value = lambda value: jnp.reshape(value, (1,)).astype(jnp.int32)
    core_value = bit_value(core)
    quarter = 2 * near + core
    places = 2 * jnp.stack([near, 1 - near, near, 1 - near]) + jnp.stack(
        [core, core, 1 - core, 1 - core]
    )
    places = places.astype(jnp.int32)

    def fetch(values, *behind):
        return swap(after(values, *behind), "tensor", 1)

    def pass_first(got, *behind):
        got = after(got, *behind)
        return got, swap(got, "dp", 4), swap(got, "dp", 1)

    def pass_second(passed, *behind):
        got, from_near, from_core = passed
        from_near = after(from_near, *behind)
        return got, from_near, from_core, swap(from_near, "dp", 1)

    heads_own = heads_weight[0].reshape(model_width, 3 * columns)
    (heads_quarter,) = cut((heads_own,), (quarter,), (model_width // 4,))
    heads_got = swap(heads_quarter, "tensor", 1)
    sizes = tuple(value.shape[0] // 4 for value in (merge_own, up_own, down_own))
    latent_own, latent_sent, cotangent_own, cotangent_sent, merge_quarter, up_quarter, down_quarter = cut(
        (after(latents, heads_quarter), latents, cotangent, cotangent, merge_own, up_own, down_own),
        (side, 1 - side, side, 1 - side, quarter, quarter, quarter),
        (1, 1, 1, 1) + sizes,
    )
    condition = after(condition, latent_sent)
    silu_cond = jax.nn.silu(condition.astype(F32)).astype(BF16)
    local_mod = jnp.einsum(
        "sd,dkc->skc", silu_cond, modulate_weight[0], preferred_element_type=F32
    ) + modulate_bias[0].astype(F32)
    mod_other = swap(pick(local_mod, 1 - side, 0), "tensor", 1)
    bias_pack = swap(jnp.concatenate([heads_bias.reshape(-1), up_bias.reshape(-1)]), "tensor", 1)
    shift1, scale1, gate1, shift2, scale2, gate2 = place(
        pick(local_mod, side, 0), mod_other, side, 1
    )

    def heads_offset(pair):
        return jnp.concatenate([pair[0], jnp.zeros_like(pair[0]), pair[1]]).astype(F32)[None]

    offset_own = heads_offset(heads_bias[0])
    offset_other = heads_offset(bias_pack[: 2 * columns].reshape(2, columns))
    up_bias_own = up_bias.astype(F32)
    up_bias_other = bias_pack[2 * columns :].reshape(1, hidden_here).astype(F32)
    shifts1 = padded_rows(shift1, scale1)

    heads_passed = pass_first(heads_got, shifts1)
    latent_other = fetch(latent_sent[0], heads_passed[0])
    filled = normed_project(
        after(latent_own[0], heads_passed[0]), shifts1, heads_own, offset_own
    )
    heads_passed = pass_second(heads_passed, filled[0])
    merge_got = fetch(merge_quarter, latent_other)
    cotangent_other = fetch(cotangent_sent[0], latent_other)
    normed1, qkv_own = normed_project(
        after(latent_other, heads_passed[1]), shifts1, heads_own, offset_own, filled
    )
    heads_other = joined((after(heads_passed[0], normed1),) + heads_passed[1:], places)
    qkv_other = project(normed1, heads_other, offset_other)
    attended_own, logsum_own = attend(after(qkv_own, qkv_other))
    merge_passed = pass_first(merge_got, attended_own)
    cotangent_other = after(cotangent_other, attended_own)
    up_got = fetch(up_quarter, cotangent_other)
    attended_other, logsum_other = attend(after(qkv_other, merge_passed[0], cotangent_other))
    merge_passed = pass_second(merge_passed, attended_other)
    merge_other = joined((after(merge_passed[0], attended_other),) + merge_passed[1:], places)
    grad = jnp.concatenate([cotangent_own[0], cotangent_other], 0)
    grad = jnp.where(side < group_counts[0], grad, jnp.zeros_like(grad))
    branch1, mid, normed2, grad_b2 = merge(
        attended_own, attended_other, merge_own, merge_other, latent_own[0], latent_other, grad,
        padded_rows(gate1, merge_bias[0].astype(F32), shift2, scale2, gate2),
    )
    up_passed = pass_first(up_got, normed2)
    down_got = fetch(down_quarter, up_passed[0])
    normed1_peer = swap(after(normed1, normed2), "dp", 1)
    normed2_peer = swap(normed2, "dp", 1)
    grad_b2_peer = swap(grad_b2, "dp", 1)
    branch2, back2, *hidden_own, up_sums_own = feed(
        core_value, after(normed2, up_passed[0]), grad_b2, up_own, up_bias_own, down_own
    )
    hidden_sent_own, hidden_own, pre_sent_own, pre_own = hidden_own
    hidden_peer_own, pre_peer_own = swap(hidden_sent_own, "dp", 1), swap(pre_sent_own, "dp", 1)
    up_passed = pass_second(up_passed, hidden_own)
    down_passed = pass_first(down_got, hidden_own)

    far_of, near_of, x_of = (
        jnp.arange(8, dtype=jnp.int32) // step % 2 for step in (4, 2, 1)
    )
    where_x = 4 * (x_of == x_bit) + 2 * far_of + near_of
    where_near = 4 * (near_of == near) + 2 * far_of + x_of
    x_first = (bit_value(2 * far + near), (4, 8, 12))
    near_first = (bit_value(2 * far + x_bit), (2, 8, 10))

    def spread(kept, received, order, *behind):
        base, masks = order
        kept, *sent = add_split(base, after(kept, *behind), received)
        return kept, [swap(part, "dp", mask) for part, mask in zip(sent, masks)]

    def block_total(kept, received, *behind):
        received = after(received, *behind)
        return sum((part.astype(F32) for part in received), kept.astype(F32))

    def pair_total(own, other, first, second):
        other = block_total(*other, first).astype(BF16)
        return block_total(*own, first) + after(swap(other, "tensor", 1), second).astype(F32)

    def join_cores(total, *behind):
        total = total.astype(BF16).reshape((2, -1) + total.shape[1:])
        sent = after(swap(pick(total, 1 - core, 0), "dp", 1), *behind)
        return place(pick(total, core, 0), sent, core, total.ndim - 2).astype(F32)

    up_other = joined((after(up_passed[0], hidden_own),) + up_passed[1:], places)
    down_parts_own = weight_grad(
        where_x, grad_b2, after(grad_b2_peer, up_other), hidden_own, hidden_peer_own
    )
    down_first_own = swap(down_parts_own[0], "dp", 2)
    up_parts_own = weight_grad(
        where_near, after(normed2, down_parts_own[0]), normed2_peer, pre_own, pre_peer_own
    )
    up_first_own = swap(up_parts_own[0], "dp", 4)
    down_passed = pass_second(down_passed, up_parts_own[0])
    down_other = joined((after(down_passed[0], up_parts_own[0]),) + down_passed[1:], places)
    branch2, back2, *hidden_other, up_sums_other = feed(
        core_value, normed2, grad_b2, up_other, up_bias_other, down_other, (branch2, back2)
    )
    hidden_sent_other, hidden_other, pre_sent_other, pre_other = hidden_other
    hidden_peer_other = swap(hidden_sent_other, "dp", 1)
    pre_peer_other = swap(pre_sent_other, "dp", 1)
    down_spread_own = spread(down_parts_own[1], down_first_own, x_first, hidden_other)
    up_spread_own = spread(up_parts_own[1], up_first_own, near_first, hidden_other)
    output_own, output_sent, grad_mid, grad_b1, grad_att_own, grad_att_other, middle_sums = middle_back(
        after(branch2, down_spread_own[0], up_spread_own[0]), back2, mid, branch1, grad, grad_b2,
        merge_own, merge_other, padded_rows(gate1, down_bias[0].astype(F32), scale2, gate2),
    )
    grad_gate2, down_bias_sum, grad_shift2, grad_scale2, grad_gate1, merge_bias_sum = middle_sums[:6]
    down_parts_other = weight_grad(
        where_x, grad_b2, after(grad_b2_peer, grad_att_own, grad_att_other),
        hidden_other, hidden_peer_other,
    )
    down_first_other = swap(down_parts_other[0], "dp", 2)
    up_parts_other = weight_grad(
        where_near, after(normed2, down_parts_other[0]), normed2_peer, pre_other, pre_peer_other
    )
    up_first_other = swap(up_parts_other[0], "dp", 4)
    output_other = swap(after(output_sent, up_parts_other[0]), "tensor", 1)
    grads_own, sent_own, kept_own = attend_back(
        core_value, qkv_own, attended_own, after(grad_att_own, up_parts_other[0]), logsum_own
    )
    heads_peer_own = swap(sent_own, "dp", 1)
    down_spread_other = spread(down_parts_other[1], down_first_other, x_first, grads_own)
    up_spread_other = spread(up_parts_other[1], up_first_other, near_first, grads_own)
    merge_total = outer_rows(
        after(grad_b1, down_spread_other[0], up_spread_other[0]),
        jnp.concatenate([attended_own, attended_other], 1),
    ).astype(BF16).reshape(8, 2, -1, 2 * columns)
    merge_sent = swap(pick(merge_total, 1 - core, 1), "dp", 1)
    heads_parts_own = weight_grad(
        where_x, normed1, after(normed1_peer, merge_total), kept_own, heads_peer_own
    )
    heads_first_own = swap(heads_parts_own[0], "dp", 2)
    output_other = after(output_other, heads_parts_own[0])
    block_output = place(output_own[None], output_other[None], side)
    grads_other, sent_other, kept_other = attend_back(
        core_value, qkv_other, attended_other, after(grad_att_other, heads_parts_own[0]), logsum_other
    )
    heads_peer_other = swap(sent_other, "dp", 1)
    heads_spread_own = spread(heads_parts_own[1], heads_first_own, x_first, grads_other)
    heads_parts_other = weight_grad(
        where_near, normed1, after(normed1_peer, heads_spread_own[0]), kept_other, heads_peer_other
    )
    heads_first_other = swap(heads_parts_other[0], "dp", 4)
    merge_sent = after(merge_sent, heads_parts_own[0])
    merge_total = pick(merge_total, core, 1).astype(F32) + merge_sent.astype(F32)
    merge_total = merge_total.astype(BF16).reshape((2, 2, 2) + merge_total.shape[1:])
    merge_first = swap(pick(after(merge_total, grads_other), 1 - x_bit, 2), "dp", 2)
    merge_kept = pick(merge_total, x_bit, 2).reshape((4,) + merge_total.shape[3:])
    merge_first = merge_first.reshape(merge_kept.shape)
    down_grad = pair_total(down_spread_own, down_spread_other, grads_other, heads_parts_other[0])
    up_grad = pair_total(up_spread_own, up_spread_other, grads_other, heads_parts_other[0])
    grad_latent, latent_sent, first_sums, heads_sums_own, heads_sums_other = first_back(
        grads_own, after(grads_other, heads_parts_other[0], down_grad, up_grad), heads_own, heads_other,
        latent_own[0], latent_other, grad_mid, padded_rows(scale1),
    )
    heads_spread_other = spread(heads_parts_other[1], heads_first_other, near_first, grad_latent)
    latent_sent = swap(after(latent_sent, heads_spread_other[0]), "tensor", 1).astype(F32)
    down_grad = join_cores(down_grad, grad_latent)
    up_grad = join_cores(up_grad, grad_latent)
    grad_shift1, grad_scale1 = first_sums[0], first_sums[1]
    merge_spread = spread(merge_kept, merge_first, x_first, heads_spread_other[0])
    heads_grad = pair_total(heads_spread_own, heads_spread_other, grad_latent, grad_latent)
    heads_grad = heads_grad[:, : 3 * columns // 2]
    heads_grad = join_cores(heads_grad.reshape(heads_grad.shape[0], 3, columns // 2))
    merge_total = block_total(*merge_spread)
    merge_sent = swap(merge_total[:, columns:].astype(BF16), "tensor", 1)
    merge_grad = merge_total[:, :columns] + merge_sent.astype(F32)

    def query_value_sums(sums):
        return jnp.concatenate([sums[0, :columns], sums[0, 2 * columns :]])

    def by_side(rows):
        rows = rows.reshape(rows.shape[:-1] + (2, features))
        return pick(rows, side, rows.ndim - 2), pick(rows, 1 - side, rows.ndim - 2)

    grad_mod = jnp.stack(
        [grad_shift1, grad_scale1, grad_gate1, grad_shift2, grad_scale2, grad_gate2]
    ).astype(BF16)
    grad_mod_own, grad_mod_sent = by_side(grad_mod)
    grad_mod_slots = place(
        grad_mod_own[None], swap(grad_mod_sent, "tensor", 1)[None], side
    )
    merge_own_sum, merge_other_sum = by_side(merge_bias_sum)
    down_own_sum, down_other_sum = by_side(down_bias_sum)
    bias_own = jnp.concatenate(
        [query_value_sums(heads_sums_own), merge_own_sum, up_sums_own[0], down_own_sum]
    )
    bias_other = jnp.concatenate(
        [query_value_sums(heads_sums_other), merge_other_sum, up_sums_other[0], down_other_sum]
    )
    bias_total = bias_own + swap(bias_other, "tensor", 1)
    bias_total = sum_dp(bias_total)
    slots_here = silu_cond.shape[0]
    tail = jnp.concatenate([silu_cond, grad_mod_slots.reshape(slots_here, -1)], 1)
    tail_all = gather_dp(tail)
    silu_all = tail_all[:, :model_width]
    grad_mod_all = tail_all[:, model_width:].reshape((-1,) + grad_mod_slots.shape[1:])
    rows_here = model_width // lax.axis_size("dp")
    silu_rows = lax.dynamic_slice_in_dim(silu_all, place_dp * rows_here, rows_here, 1)
    modulate_grad = jnp.einsum("sd,skc->dkc", silu_rows, grad_mod_all, preferred_element_type=F32)
    modulate_bias_grad = jnp.sum(grad_mod_all.astype(F32), 0)
    cond_partial = jnp.einsum(
        "dkc,skc->sd", modulate_weight[0], grad_mod_slots, preferred_element_type=F32
    )
    cond_total = cond_partial + swap(cond_partial, "tensor", 1)
    condition_grad = jax.vjp(jax.nn.silu, condition.astype(F32))[1](cond_total)[0]
    latent_grad = place(grad_latent[None], latent_sent[None], side)
    edges = (0, 2 * columns, 2 * columns + features, 2 * columns + features + hidden_here, None)
    heads_bias_grad, merge_bias_grad, up_bias_grad, down_bias_grad = (
        bias_total[first:last] for first, last in zip(edges, edges[1:])
    )
    return (
        block_output,
        latent_grad,
        condition_grad,
        heads_grad[None],
        heads_bias_grad.reshape(1, 2, columns),
        merge_grad.T[None],
        merge_bias_grad[None],
        up_grad[None],
        up_bias_grad[None],
        down_grad.T[None],
        down_bias_grad[None],
        modulate_grad[None],
        modulate_bias_grad[None],
    )


def solution(mesh):
    in_specs = (
        P("dp", "tensor", None),
        P("dp", None),
        P("dp", "tensor", None),
        P("dp"),
        P(None, None, None, "tensor"),
        P(None, None, "tensor"),
        P(None, "tensor", None),
        P(),
        P(None, None, "tensor"),
        P(None, "tensor"),
        P(None, "tensor", None),
        P(),
        P(None, None, None, "tensor"),
        P(None, None, "tensor"),
    )
    out_specs = (
        P("dp", "tensor", None),
        P("dp", "tensor", None),
        P("dp", None),
        P(None, "dp", None, "tensor"),
        P(None, None, "tensor"),
        P(None, "tensor", "dp"),
        P(None, "tensor"),
        P(None, "dp", "tensor"),
        P(None, "tensor"),
        P(None, "tensor", "dp"),
        P(None, "tensor"),
        P(None, "dp", None, "tensor"),
        P(None, None, "tensor"),
    )
    whole_slots = mesh.shape["tensor"] == 2 and mesh.shape["dp"] == 16
    return jax.shard_map(
        slot_device if whole_slots else per_device, mesh=mesh, in_specs=in_specs, out_specs=out_specs, check_vma=False
    )
```

```python
import functools
import math

import jax
import jax.numpy as jnp
from jax import lax
from jax.experimental import pallas as pl
from jax.experimental.pallas import tpu as pltpu
from jax.sharding import PartitionSpec as P

HEAD_DIM = 72
QUERY_BLOCK = 512


epsilon = 1e-06


def normalize(stream):
    average = jnp.mean(stream, -1, keepdims=True)
    centered = stream - average
    variance = jnp.mean(centered * centered, -1, keepdims=True)
    inverse = lax.rsqrt(variance + epsilon)
    return (centered * inverse, inverse)


def normalize_back(grad_norm, normed, inverse):
    first_mean = jnp.mean(grad_norm, -1, keepdims=True)
    second_mean = jnp.mean(grad_norm * normed, -1, keepdims=True)
    return inverse * (grad_norm - first_mean - normed * second_mean)


def gelu_tanh(values):
    return jax.nn.gelu(values, approximate=True)


def column_sums(operand):
    return jnp.sum(operand.astype(jnp.float32), 0)


def outer_rows(operand, other):
    return lax.dot_general(
        operand, other, (((0,), (0,)), ((), ())), preferred_element_type=jnp.float32
    )


def times_transposed(operand, weight):
    return lax.dot_general(
        operand, weight, (((1,), (1,)), ((), ())), preferred_element_type=jnp.float32
    )


def gather_tokens(values):
    return lax.all_gather(values, "tensor", axis=0, tiled=True)


def gather_grads(values):
    return lax.all_gather(values, "tensor", axis=0, tiled=True)


def scatter_branch(operand, weight):

    def partial_rows(first_row, row_count):
        return jnp.dot(operand, weight, preferred_element_type=jnp.float32)

    return lax.psum_scatter(
        partial_rows(
            jnp.int32(0), operand.shape[0] // lax.axis_size("tensor") * lax.axis_size("tensor")
        ).astype(jnp.bfloat16),
        "tensor",
        scatter_dimension=0,
        tiled=True,
    ).astype(jnp.float32)


def scatter_inputs(operand, weight):

    def partial_rows(first_row, row_count):
        return times_transposed(operand, weight)

    return lax.psum_scatter(
        partial_rows(
            jnp.int32(0), operand.shape[0] // lax.axis_size("tensor") * lax.axis_size("tensor")
        ).astype(jnp.bfloat16),
        "tensor",
        scatter_dimension=0,
        tiled=True,
    ).astype(jnp.float32)


def stack_member(layer_tuples, member):
    return jnp.stack([entry_tuple[member] for entry_tuple in layer_tuples])


def attend_forward(queries, key_rows, value_rows):
    length, heads_here = (queries.shape[0], queries.shape[1])
    blocks = length // QUERY_BLOCK
    score_scale = HEAD_DIM ** (-0.5)

    def one_block(query_block):
        scores = (
            jnp.einsum("qhd,khd->hqk", query_block, key_rows, preferred_element_type=jnp.float32)
            * score_scale
        )
        row_max = jnp.max(scores, -1, keepdims=True)
        exponent = jnp.exp(scores - row_max)
        row_total = jnp.sum(exponent, -1, keepdims=True)
        attn_probs = (exponent / row_total).astype(jnp.bfloat16)
        attended = jnp.einsum(
            "hqk,khd->qhd", attn_probs, value_rows, preferred_element_type=jnp.float32
        )
        return (attended.astype(jnp.bfloat16), (row_max + jnp.log(row_total))[:, :, 0])

    attended, logsum = lax.map(
        one_block, queries.reshape(blocks, QUERY_BLOCK, heads_here, HEAD_DIM)
    )
    return (attended.reshape(length, heads_here * HEAD_DIM), logsum)


def attend_backward(queries, key_rows, value_rows, logsum, grad_attended):
    length, heads_here = (queries.shape[0], queries.shape[1])
    blocks = length // QUERY_BLOCK
    score_scale = HEAD_DIM ** (-0.5)
    block_shape = (blocks, QUERY_BLOCK, heads_here, HEAD_DIM)

    def one_block(running, inputs_here):
        grad_keys, grad_values = running
        query_block, grad_block, logsum_block = inputs_here
        scores = (
            jnp.einsum("qhd,khd->hqk", query_block, key_rows, preferred_element_type=jnp.float32)
            * score_scale
        )
        attn_probs = jnp.exp(scores - logsum_block[:, :, None])
        grad_values = grad_values + jnp.einsum(
            "hqk,qhd->khd",
            attn_probs.astype(jnp.bfloat16),
            grad_block,
            preferred_element_type=jnp.float32,
        )
        grad_probs = jnp.einsum(
            "qhd,khd->hqk", grad_block, value_rows, preferred_element_type=jnp.float32
        )
        row_dot = jnp.sum(attn_probs * grad_probs, -1, keepdims=True)
        grad_scores = (attn_probs * (grad_probs - row_dot)).astype(jnp.bfloat16)
        grad_queries = (
            jnp.einsum("hqk,khd->qhd", grad_scores, key_rows, preferred_element_type=jnp.float32)
            * score_scale
        )
        grad_keys = (
            grad_keys
            + jnp.einsum(
                "hqk,qhd->khd", grad_scores, query_block, preferred_element_type=jnp.float32
            )
            * score_scale
        )
        return ((grad_keys, grad_values), grad_queries.astype(jnp.bfloat16))

    zeros_kv = jnp.zeros((length, heads_here, HEAD_DIM), jnp.float32)
    scanned = (queries.reshape(block_shape), grad_attended.reshape(block_shape), logsum)
    (grad_keys, grad_values), grad_queries = lax.scan(one_block, (zeros_kv, zeros_kv), scanned)
    flat_shape = (length, heads_here * HEAD_DIM)
    return (
        grad_queries.reshape(flat_shape),
        grad_keys.astype(jnp.bfloat16).reshape(flat_shape),
        grad_values.astype(jnp.bfloat16).reshape(flat_shape),
    )


def forward_layer(stream, modulation, layer_weights, heads_here):
    (
        flat_heads,
        heads_offset,
        merge_weight,
        merge_bias,
        up_weight,
        up_bias,
        down_weight,
        down_bias,
    ) = layer_weights
    length = stream.shape[0] * lax.axis_size("tensor")
    columns = flat_heads.shape[1] // 3
    norm_first, inverse_first = normalize(stream)
    normed_first = (norm_first * (1.0 + modulation[1]) + modulation[0]).astype(jnp.bfloat16)
    gathered_first = gather_tokens(normed_first)
    projected = (
        jnp.dot(gathered_first, flat_heads, preferred_element_type=jnp.float32) + heads_offset
    ).astype(jnp.bfloat16)
    split_shape = (length, heads_here, HEAD_DIM)
    queries = projected[:, :columns].reshape(split_shape)
    key_rows = projected[:, columns : 2 * columns].reshape(split_shape)
    value_rows = projected[:, 2 * columns :].reshape(split_shape)
    attended, logsum = attend_forward(queries, key_rows, value_rows)
    branch_first = scatter_branch(attended, merge_weight) + merge_bias.astype(jnp.float32)
    stream_mid = stream + modulation[2] * branch_first
    norm_second, inverse_second = normalize(stream_mid)
    normed_second = (norm_second * (1.0 + modulation[4]) + modulation[3]).astype(jnp.bfloat16)
    gathered_second = gather_tokens(normed_second)
    hidden_pre = jnp.dot(
        gathered_second, up_weight, preferred_element_type=jnp.float32
    ) + up_bias.astype(jnp.float32)
    hidden = gelu_tanh(hidden_pre).astype(jnp.bfloat16)
    branch_second = scatter_branch(hidden, down_weight) + down_bias.astype(jnp.float32)
    stream_next = stream_mid + modulation[5] * branch_second
    first_input, second_input = (gathered_first, gathered_second)
    kept = (
        norm_first,
        inverse_first,
        first_input,
        queries,
        key_rows,
        value_rows,
        logsum,
        attended,
        branch_first,
        norm_second,
        inverse_second,
        second_input,
        hidden_pre,
        hidden,
        branch_second,
    )
    return (stream_next, kept)


def backward_layer(grad_stream, modulation, layer_weights, kept):
    (
        flat_heads,
        heads_offset,
        merge_weight,
        merge_bias,
        up_weight,
        up_bias,
        down_weight,
        down_bias,
    ) = layer_weights
    (
        norm_first,
        inverse_first,
        first_input,
        queries,
        key_rows,
        value_rows,
        logsum,
        attended,
        branch_first,
        norm_second,
        inverse_second,
        second_input,
        hidden_pre,
        hidden,
        branch_second,
    ) = kept
    model_width = flat_heads.shape[0]
    columns = flat_heads.shape[1] // 3
    grad_branch_second = (modulation[5] * grad_stream).astype(jnp.bfloat16)
    grad_gate_second = jnp.sum(grad_stream * branch_second, 0)
    grad_down_bias = column_sums(grad_branch_second)
    gathered_grad = gather_grads(grad_branch_second)
    down_grad = outer_rows(hidden, gathered_grad)
    grad_hidden = times_transposed(gathered_grad, down_weight)
    grad_pre = jax.vjp(gelu_tanh, hidden_pre)[1](grad_hidden)[0].astype(jnp.bfloat16)
    up_bias_grad = column_sums(grad_pre)
    up_grad = outer_rows(second_input, grad_pre)
    grad_normed_second = scatter_inputs(grad_pre, up_weight)
    grad_shift_second = jnp.sum(grad_normed_second, 0)
    grad_scale_second = jnp.sum(grad_normed_second * norm_second, 0)
    grad_mid = grad_stream + normalize_back(
        grad_normed_second * (1.0 + modulation[4]), norm_second, inverse_second
    )
    grad_branch_first = (modulation[2] * grad_mid).astype(jnp.bfloat16)
    grad_gate_first = jnp.sum(grad_mid * branch_first, 0)
    grad_merge_bias = column_sums(grad_branch_first)
    gathered_grad = gather_grads(grad_branch_first)
    merge_grad = outer_rows(attended, gathered_grad)
    grad_attended = times_transposed(gathered_grad, merge_weight).astype(jnp.bfloat16)
    grad_queries, grad_keys, grad_values = attend_backward(
        queries, key_rows, value_rows, logsum, grad_attended
    )
    grad_projected = jnp.concatenate([grad_queries, grad_keys, grad_values], 1)
    heads_bias_grad = jnp.stack([column_sums(grad_queries), column_sums(grad_values)])
    heads_grad = outer_rows(first_input, grad_projected).reshape(model_width, 3, columns)
    grad_normed_first = scatter_inputs(grad_projected, flat_heads)
    grad_shift_first = jnp.sum(grad_normed_first, 0)
    grad_scale_first = jnp.sum(grad_normed_first * norm_first, 0)
    grad_before = grad_mid + normalize_back(
        grad_normed_first * (1.0 + modulation[1]), norm_first, inverse_first
    )
    extra = jnp.stack(
        [
            grad_shift_first,
            grad_scale_first,
            grad_gate_first,
            grad_shift_second,
            grad_scale_second,
            grad_gate_second,
            grad_merge_bias,
            grad_down_bias,
        ]
    )
    return (
        grad_before,
        (heads_grad, heads_bias_grad, merge_grad, up_grad, up_bias_grad, down_grad),
        extra,
    )


def per_device(
    latents,
    condition,
    cotangent,
    group_counts,
    heads_weight,
    heads_bias,
    merge_weight,
    merge_bias,
    up_weight,
    up_bias,
    down_weight,
    down_bias,
    modulate_weight,
    modulate_bias,
):
    slot_count = latents.shape[0]
    model_width = latents.shape[2]
    layer_count = heads_weight.shape[0]
    columns = heads_weight.shape[3]
    heads_here = columns // HEAD_DIM
    silu_cond = jax.nn.silu(condition.astype(jnp.float32)).astype(jnp.bfloat16)
    local_mod = jnp.einsum(
        "sd,bdkc->sbkc", silu_cond, modulate_weight, preferred_element_type=jnp.float32
    ) + modulate_bias.astype(jnp.float32)
    modulation_all = lax.all_gather(local_mod, "tensor", axis=3, tiled=True)
    flat_heads = heads_weight.reshape(layer_count, model_width, 3 * columns)
    zero_bias = jnp.zeros((layer_count, columns), heads_bias.dtype)
    heads_offset = (
        jnp.stack([heads_bias[:, 0], zero_bias, heads_bias[:, 1]], 1)
        .reshape(layer_count, 3 * columns)
        .astype(jnp.float32)
    )
    per_layer = [
        (
            flat_heads[0],
            heads_offset[0],
            merge_weight[0],
            merge_bias[0],
            up_weight[0],
            up_bias[0],
            down_weight[0],
            down_bias[0],
        )
    ]
    layer_sums = [None] * layer_count
    modulate_sum = jnp.zeros(modulate_weight.shape, jnp.float32)
    modulate_bias_sum = jnp.zeros(modulate_bias.shape, jnp.float32)
    merge_bias_sum = jnp.zeros((layer_count, columns), jnp.float32)
    down_bias_sum = jnp.zeros((layer_count, columns), jnp.float32)
    output_list, latent_list, condition_list = ([], [], [])
    for slot_index in range(slot_count):
        live_flag = (slot_index < group_counts[0]).astype(jnp.float32)
        stream = latents[slot_index].astype(jnp.float32)
        layer_index = 0
        stream, kept = forward_layer(
            stream, modulation_all[slot_index, layer_index], per_layer[layer_index], heads_here
        )
        saved_layers = [kept]
        output_list.append(stream.astype(jnp.bfloat16))
        grad_stream = cotangent[slot_index].astype(jnp.float32) * live_flag
        extras = [None] * layer_count
        for layer_index in reversed(range(layer_count)):
            grad_stream, layer_grads, extra = backward_layer(
                grad_stream,
                modulation_all[slot_index, layer_index],
                per_layer[layer_index],
                saved_layers[layer_index],
            )
            if layer_sums[layer_index] is None:
                layer_sums[layer_index] = layer_grads
            else:
                layer_sums[layer_index] = jax.tree.map(
                    jnp.add, layer_sums[layer_index], layer_grads
                )
            extras[layer_index] = extra
        latent_list.append(grad_stream)
        shared = lax.psum_scatter(
            jnp.stack(extras).astype(jnp.bfloat16), "tensor", scatter_dimension=2, tiled=True
        ).astype(jnp.float32)
        grad_mod = shared[:, :6].astype(jnp.bfloat16)
        modulate_sum = modulate_sum + jnp.einsum(
            "d,bkc->bdkc", silu_cond[slot_index], grad_mod, preferred_element_type=jnp.float32
        )
        modulate_bias_sum = modulate_bias_sum + grad_mod.astype(jnp.float32)
        merge_bias_sum = merge_bias_sum + shared[:, 6]
        down_bias_sum = down_bias_sum + shared[:, 7]
        cond_partial = jnp.einsum(
            "bdkc,bkc->d", modulate_weight, grad_mod, preferred_element_type=jnp.float32
        )
        cond_total = lax.psum(cond_partial, "tensor")
        silu_grad = jax.vjp(jax.nn.silu, condition[slot_index].astype(jnp.float32))[1](cond_total)[
            0
        ]
        condition_list.append(silu_grad)
    weight_grads = (
        lax.psum_scatter(
            stack_member(layer_sums, 0).astype(jnp.bfloat16), "dp", scatter_dimension=1, tiled=True
        ).astype(jnp.float32),
        lax.psum_scatter(
            stack_member(layer_sums, 2).astype(jnp.bfloat16), "dp", scatter_dimension=2, tiled=True
        ).astype(jnp.float32),
        lax.psum_scatter(
            stack_member(layer_sums, 3).astype(jnp.bfloat16), "dp", scatter_dimension=1, tiled=True
        ).astype(jnp.float32),
        lax.psum_scatter(
            stack_member(layer_sums, 5).astype(jnp.bfloat16), "dp", scatter_dimension=2, tiled=True
        ).astype(jnp.float32),
        lax.psum_scatter(
            modulate_sum.astype(jnp.bfloat16), "dp", scatter_dimension=1, tiled=True
        ).astype(jnp.float32),
    )
    bias_grads = lax.psum(
        (
            stack_member(layer_sums, 1),
            merge_bias_sum,
            stack_member(layer_sums, 4),
            down_bias_sum,
            modulate_bias_sum,
        ),
        "dp",
    )
    block_output = jnp.stack(output_list)
    latent_grad = jnp.stack(latent_list)
    condition_grad = jnp.stack(condition_list)
    return (
        block_output,
        latent_grad,
        condition_grad,
        weight_grads[0],
        bias_grads[0],
        weight_grads[1],
        bias_grads[1],
        weight_grads[2],
        bias_grads[2],
        weight_grads[3],
        bias_grads[3],
        weight_grads[4],
        bias_grads[4],
    )


F32 = jnp.float32
BF16 = jnp.bfloat16
SCORE_SCALE = HEAD_DIM ** (-0.5)
SCORE_LOG2 = SCORE_SCALE * math.log2(math.e)
VMEM_BYTES = 60 * 2**20


def cost(weight):
    return pl.CostEstimate(flops=weight * 50 * 10**8, bytes_accessed=10**5, transcendentals=0)


class Tied:
    def __init__(self, value, behind):
        self.value, self.behind = value, behind


def untied(value):
    return value.value if isinstance(value, Tied) else value


def after(value, *behind):
    return Tied(value, behind)


def run(kernel, weight, scalars, inputs, in_specs, grid, out_specs, out_shape, scratch=(), aliases={}):
    behind = []
    for value in inputs:
        if isinstance(value, Tied):
            behind += [untied(other) for other in value.behind]
    inputs = [untied(value) for value in inputs]
    first = len(scalars) + len(inputs)

    def without_ties(*refs):
        kernel(*refs[:first], *refs[first + len(behind) :])

    return pl.pallas_call(
        without_ties,
        grid_spec=pltpu.PrefetchScalarGridSpec(
            num_scalar_prefetch=len(scalars),
            grid=grid,
            in_specs=list(in_specs) + [pl.BlockSpec(memory_space=pl.ANY)] * len(behind),
            out_specs=out_specs,
            scratch_shapes=list(scratch),
        ),
        out_shape=out_shape,
        input_output_aliases=aliases,
        compiler_params=pltpu.CompilerParams(vmem_limit_bytes=VMEM_BYTES),
        cost_estimate=cost(weight),
    )(*scalars, *inputs, *behind)


def dot_dims(left, right, left_dim, right_dim):
    return lax.dot_general(
        left, right, (((left_dim,), (right_dim,)), ((), ())), preferred_element_type=F32
    )


def head_slice(part, head, width):
    return slice(part * width + head * HEAD_DIM, part * width + (head + 1) * HEAD_DIM)


def attend_kernel(heads, qkv_ref, out_ref, logsum_ref):
    width = heads * HEAD_DIM
    rows_here = out_ref.shape[0]
    rows = pl.ds(pl.multiple_of(pl.program_id(0) * rows_here, rows_here), rows_here)
    for head in range(heads):
        queries = qkv_ref[rows, head_slice(0, head, width)]
        scores = dot_dims(qkv_ref[:, head_slice(1, head, width)], queries, 1, 1)
        top = jnp.max(scores, 0, keepdims=True)
        exponent = jnp.exp2((scores - top) * SCORE_LOG2)
        total = jnp.sum(exponent, 0, keepdims=True)
        mixed = dot_dims(qkv_ref[:, head_slice(2, head, width)], exponent.astype(BF16), 0, 0)
        out_ref[:, head_slice(0, head, width)] = (mixed / total).T.astype(BF16)
        logsum_ref[head : head + 1, :] = top * SCORE_LOG2 + jnp.log2(total)


def attend(qkv, query_rows=512):
    tokens, width = untied(qkv).shape[0], untied(qkv).shape[1] // 3
    heads = width // HEAD_DIM
    return run(
        functools.partial(attend_kernel, heads), 18, (), [qkv],
        [pl.BlockSpec((tokens, 3 * width), lambda i: (0, 0))],
        (tokens // query_rows,),
        [
            pl.BlockSpec((query_rows, width), lambda i: (i, 0)),
            pl.BlockSpec((heads, query_rows), lambda i: (0, i)),
        ],
        [
            jax.ShapeDtypeStruct((tokens, width), BF16),
            jax.ShapeDtypeStruct((heads, tokens), F32),
        ],
    )


def attend_back_kernel(
    heads, key_rows, steps, core_ref,
    qkv_ref, out_ref, grad_ref, logsum_ref, grads_ref, sent_ref, kept_ref, dot_ref, query_ref,
):
    step = pl.program_id(0)
    width = heads * HEAD_DIM
    rows = pl.ds(pl.multiple_of(step * key_rows, key_rows), key_rows)

    @pl.when(step == 0)
    def _():
        owner = lax.broadcasted_iota(jnp.int32, (heads, width), 1)
        first = lax.broadcasted_iota(jnp.int32, (heads, width), 0) * HEAD_DIM
        member = ((owner >= first) & (owner < first + HEAD_DIM)).astype(BF16)
        product = grad_ref[...].astype(F32) * out_ref[...].astype(F32)
        high = product.astype(BF16)
        low = (product - high.astype(F32)).astype(BF16)
        dot_ref[...] = dot_dims(member, high, 1, 1) + dot_dims(member, low, 1, 1)
        query_ref[...] = jnp.zeros_like(query_ref)

    def store(part, head, rows, value):
        grads_ref[rows, head_slice(part, head, width)] = value

    for head in range(heads):
        queries = qkv_ref[:, head_slice(0, head, width)]
        keys = qkv_ref[rows, head_slice(1, head, width)]
        grad = grad_ref[:, head_slice(0, head, width)]
        scores = dot_dims(keys, queries, 1, 1)
        probs = jnp.exp2(scores * SCORE_LOG2 - logsum_ref[head : head + 1, :])
        grad_probs = dot_dims(qkv_ref[rows, head_slice(2, head, width)], grad, 1, 1)
        grad_scores = (probs * (grad_probs - dot_ref[head : head + 1, :])).astype(BF16)
        grad_values = jnp.dot(probs.astype(BF16), grad, preferred_element_type=F32)
        store(2, head, rows, grad_values.astype(BF16))
        grad_keys = jnp.dot(grad_scores, queries, preferred_element_type=F32) * SCORE_SCALE
        store(1, head, rows, grad_keys.astype(BF16))
        query_ref[head] += dot_dims(keys, grad_scores, 0, 0)

    @pl.when(step == steps - 1)
    def _():
        for head in range(heads):
            store(0, head, slice(None), (query_ref[head] * SCORE_SCALE).T.astype(BF16))
        half = width // 2
        for first in range(2):

            @pl.when(core_ref[0] == first)
            def _():
                for part in range(3):
                    here, there = (part * width + side * half for side in (first, 1 - first))
                    to = slice(part * half, (part + 1) * half)
                    kept_ref[:, to] = grads_ref[:, here : here + half]
                    sent_ref[:, to] = grads_ref[:, there : there + half]
                rest = slice(3 * half, kept_ref.shape[1])
                kept_ref[:, rest] = jnp.zeros_like(kept_ref[:, rest])
                sent_ref[:, rest] = jnp.zeros_like(sent_ref[:, rest])


def attend_back(core, qkv, attended, grad_attended, logsum, key_rows=512):
    tokens, width = attended.shape
    heads = width // HEAD_DIM
    steps = tokens // key_rows
    whole = lambda *shape: pl.BlockSpec(shape, lambda i, core_ref: (0,) * len(shape))
    half = (tokens, -(-3 * width // 256) * 128)
    return run(
        functools.partial(attend_back_kernel, heads, key_rows, steps), 32,
        [core], [qkv, attended, grad_attended, logsum],
        [
            whole(tokens, 3 * width), whole(tokens, width), whole(tokens, width),
            whole(heads, tokens),
        ],
        (steps,),
        [whole(tokens, 3 * width), whole(*half), whole(*half)],
        [
            jax.ShapeDtypeStruct((tokens, 3 * width), BF16),
            jax.ShapeDtypeStruct(half, BF16),
            jax.ShapeDtypeStruct(half, BF16),
        ],
        [pltpu.VMEM((heads, tokens), F32), pltpu.VMEM((heads, HEAD_DIM, tokens), F32)],
    )


GELU_OUTER = math.sqrt(2 / math.pi)
GELU_CUBIC = 0.044715


def gelu_and_slope(values):
    square = values * values
    tanh = jnp.tanh(values * (GELU_OUTER + GELU_OUTER * GELU_CUBIC * square))
    half = 0.5 + 0.5 * tanh
    inner = 0.5 * GELU_OUTER + 1.5 * GELU_OUTER * GELU_CUBIC * square
    return values * half, half + values * (1.0 - tanh * tanh) * inner


def feed_kernel(
    token_rows, carried, core_ref, normed_ref, grad_ref, up_ref, bias_ref, down_ref, *refs
):
    if carried:
        branch_in, normed_in = refs[:2]
        refs = refs[2:]
    branch_ref, back_ref, hidden_sent, hidden_kept, pre_sent, pre_kept, bias_grad_ref = refs
    chunk = pl.program_id(0)
    bias_grad_ref[...] = jnp.zeros_like(bias_grad_ref)

    def block(hidden_ref, pre_ref, index, _):
        rows = pl.ds(pl.multiple_of(index * token_rows, token_rows), token_rows)
        pre = jnp.dot(normed_ref[rows, :], up_ref[...], preferred_element_type=F32)
        grad_hidden = dot_dims(grad_ref[rows, :], down_ref[...], 1, 1)
        hidden, slope = gelu_and_slope(pre + bias_ref[...])
        hidden = hidden.astype(BF16)
        grad_pre = (grad_hidden * slope).astype(BF16)
        bias_grad_ref[...] += jnp.sum(grad_pre.astype(F32), 0, keepdims=True)
        hidden_ref[rows, :] = hidden
        pre_ref[rows, :] = grad_pre
        branch = jnp.dot(hidden, down_ref[...], preferred_element_type=F32)
        back = dot_dims(grad_pre, up_ref[...], 1, 1)
        if hidden_ref is hidden_kept:
            branch_ref[rows, :] += branch
            back_ref[rows, :] += back
        else:
            branch_ref[rows, :] = branch + branch_in[rows, :] if carried else branch
            back_ref[rows, :] = back + normed_in[rows, :] if carried else back
        return 0

    for step, refs_here in enumerate(((hidden_sent, pre_sent), (hidden_kept, pre_kept))):

        @pl.when(chunk == step)
        def _():
            lax.fori_loop(
                0, normed_ref.shape[0] // token_rows, functools.partial(block, *refs_here), 0
            )


def feed(core, normed, grad, up, bias, down, carried=(), token_rows=256):
    tokens, model_width = untied(normed).shape
    hidden_here = up.shape[1]
    width = hidden_here // 2
    chunk = lambda j, core_ref: lax.rem(j + 1 + core_ref[0], 2)
    single = pl.Buffered(1)
    whole = lambda: pl.BlockSpec((tokens, model_width), lambda j, c: (0, 0), pipeline_mode=single)
    part = lambda: pl.BlockSpec((tokens, width), lambda j, c: (0, 0), pipeline_mode=single)
    return run(
        functools.partial(feed_kernel, token_rows, len(carried) > 0), 44,
        [core], [normed, grad, up, bias, down, *carried],
        [
            whole(), whole(),
            pl.BlockSpec((model_width, width), lambda j, c: (0, chunk(j, c))),
            pl.BlockSpec((1, width), lambda j, c: (0, chunk(j, c))),
            pl.BlockSpec((width, model_width), lambda j, c: (chunk(j, c), 0)),
        ] + [whole() for _ in carried],
        (2,),
        [
            whole(), whole(), part(), part(), part(), part(),
            pl.BlockSpec((1, width), lambda j, c: (0, chunk(j, c))),
        ],
        [jax.ShapeDtypeStruct((tokens, model_width), F32)] * 2
        + [jax.ShapeDtypeStruct((tokens, width), BF16)] * 4
        + [jax.ShapeDtypeStruct((1, hidden_here), F32)],
    )


def weight_grad_kernel(chunks, blocks, where_ref, left_mine, left_peer, *refs):
    rights, outs, left_ref = refs[: 2 * chunks], refs[2 * chunks : -1], refs[-1]
    tokens, model_width = left_mine.shape
    rows = model_width // blocks
    for first, left in ((0, left_mine), (tokens, left_peer)):
        turned = left[...].T
        for block in range(blocks):
            to = pl.ds(pl.multiple_of(where_ref[block] * rows, rows), rows)
            left_ref[to, first : first + tokens] = turned[block * rows : (block + 1) * rows]
    for chunk in range(chunks):
        for part in range(2):
            half = slice(part * model_width // 2, (part + 1) * model_width // 2)
            mine, peer = rights[2 * chunk : 2 * chunk + 2]
            total = jnp.dot(left_ref[half, :tokens], mine[...], preferred_element_type=F32)
            total += jnp.dot(left_ref[half, tokens:], peer[...], preferred_element_type=F32)
            total = total.astype(BF16)
            for block in range(blocks // 2):
                outs[2 * chunk + part][block] = total[block * rows : (block + 1) * rows]


def weight_grad(where, left_mine, left_peer, *rights, weight=0):
    tokens, model_width = untied(left_mine).shape
    blocks = where.shape[0]
    chunks = len(rights) // 2
    width = rights[0].shape[1]
    out = jax.ShapeDtypeStruct((blocks // 2, model_width // blocks, width), BF16)
    whole = lambda value: pl.BlockSpec(value.shape, lambda j, w: (0,) * len(value.shape))
    inputs = [left_mine, left_peer, *rights]
    return run(
        functools.partial(weight_grad_kernel, chunks, blocks), weight,
        [where], inputs, [whole(untied(value)) for value in inputs],
        (1,), [whole(out)] * (2 * chunks), [out] * (2 * chunks),
        [pltpu.VMEM((model_width, 2 * tokens), BF16)],
    )


def halve_kernel(bit_ref, kept_out, sent_out, kept_in, sent_in, sent_ref, kept_ref):
    sent_ref[...] = (kept_out[...].astype(F32) + sent_out[...].astype(F32)).astype(BF16)
    kept_ref[...] = (kept_in[...].astype(F32) + sent_in[...].astype(F32)).astype(BF16)


def halve(bit, kept, received):
    blocks, rows, width = kept.shape
    out = jax.ShapeDtypeStruct((blocks // 2, rows, width), BF16)
    leave = pl.BlockSpec((1, rows, width), lambda j, b: (2 * j + 1 - b[0], 0, 0))
    stay = pl.BlockSpec((1, rows, width), lambda j, b: (2 * j + b[0], 0, 0))
    here = pl.BlockSpec((1, rows, width), lambda j, b: (j, 0, 0))
    return run(
        halve_kernel, 0, [bit], [kept, received, kept, untied(received)],
        [leave, leave, stay, stay], (blocks // 2,), [here, here], [out, out],
    )


def project_kernel(with_norm, *refs):
    refs = refs[2:] if with_norm > 1 else refs
    if with_norm:
        tokens_ref, rows_ref, weight_ref, offset_ref, normed_ref, out_ref = refs
        norm, _ = normalize(tokens_ref[...].astype(F32))
        normed = (norm * (1.0 + rows_ref[1:2]) + rows_ref[0:1]).astype(BF16)
        normed_ref[...] = normed
    else:
        tokens_ref, weight_ref, offset_ref, out_ref = refs
        normed = tokens_ref[...]
    out = jnp.dot(normed, weight_ref[...], preferred_element_type=F32) + offset_ref[...]
    out_ref[...] = out.astype(BF16)


def constant_block(shape):
    return pl.BlockSpec(shape, lambda i: (0,) * len(shape), pipeline_mode=pl.Buffered(1))


def row_blocks(rows, width, first=0):
    return pl.BlockSpec((rows, width), lambda i: (i + first, 0))


def project(normed, weight, offset, rows=256):
    tokens, model_width = normed.shape
    width = weight.shape[1]
    return run(
        functools.partial(project_kernel, 0), 9, (), [normed, weight, offset],
        [row_blocks(rows, model_width), constant_block(weight.shape), constant_block((1, width))],
        (tokens // rows,), row_blocks(rows, width), jax.ShapeDtypeStruct((tokens, width), BF16),
    )


def normed_project(half, shifts, weight, offset, filled=None, rows=256):
    half_tokens, model_width = untied(half).shape
    width = weight.shape[1]
    first = 0 if filled is None else half_tokens // rows
    held = [] if filled is None else list(filled)
    return run(
        functools.partial(project_kernel, 1 if filled is None else 2), 7, (),
        [*held, half, shifts, weight, offset],
        [pl.BlockSpec(memory_space=pl.ANY)] * len(held)
        + [
            row_blocks(rows, model_width), constant_block(shifts.shape),
            constant_block(weight.shape), constant_block((1, width)),
        ],
        (half_tokens // rows,),
        [row_blocks(rows, model_width, first), row_blocks(rows, width, first)],
        [
            jax.ShapeDtypeStruct((2 * half_tokens, model_width), BF16),
            jax.ShapeDtypeStruct((2 * half_tokens, width), BF16),
        ],
        aliases={0: 0, 1: 1} if held else {},
    )


def halves(rows, width, blocks):
    half = blocks // 2
    return [
        pl.BlockSpec((rows, width), lambda i: (jnp.minimum(i, half - 1), 0)),
        pl.BlockSpec((rows, width), lambda i: (jnp.maximum(i - half, 0), 0)),
    ]


def merge_kernel(
    blocks, live_ref, own_ref, other_ref, weight_own, weight_other, first_ref, second_ref,
    grad_first, grad_second, rows_ref, branch_ref, mid_ref, normed_ref, grad_ref, grad_b2_ref,
):
    gate1, bias, shift2, scale2, gate2 = (rows_ref[row : row + 1] for row in range(5))
    early = pl.program_id(0) < blocks // 2
    stream = jnp.where(early, first_ref[...], second_ref[...])
    grad = jnp.where(early, grad_first[...], grad_second[...])
    grad = jnp.where(live_ref[0] > 0, grad, jnp.zeros_like(grad))
    grad_ref[...] = grad
    branch = jnp.dot(own_ref[...], weight_own[...], preferred_element_type=F32)
    branch += jnp.dot(other_ref[...], weight_other[...], preferred_element_type=F32)
    branch += bias
    branch_ref[...] = branch.astype(BF16)
    mid = stream.astype(F32) + gate1 * branch
    mid_ref[...] = mid
    norm, _ = normalize(mid)
    normed_ref[...] = (norm * (1.0 + scale2) + shift2).astype(BF16)
    grad_b2_ref[...] = (gate2 * grad.astype(F32)).astype(BF16)


def merge(
    live, own, other, weight_own, weight_other, first, second, grad_first, grad_second, vectors,
    rows=256,
):
    tokens, width = own.shape
    model_width = weight_own.shape[1]
    blocks = tokens // rows
    half = blocks // 2
    block = lambda columns: pl.BlockSpec((rows, columns), lambda i, v: (i, 0))
    whole = lambda shape: pl.BlockSpec(shape, lambda i, v: (0,) * len(shape))
    pair = lambda: [
        pl.BlockSpec((rows, model_width), lambda i, v: (jnp.minimum(i, half - 1), 0)),
        pl.BlockSpec((rows, model_width), lambda i, v: (jnp.maximum(i - half, 0), 0)),
    ]
    shape = lambda kind: jax.ShapeDtypeStruct((tokens, model_width), kind)
    return run(
        functools.partial(merge_kernel, blocks), 11, [live],
        [own, other, weight_own, weight_other, first, second, grad_first, grad_second, vectors],
        [
            block(width), block(width), whole(weight_own.shape), whole(weight_other.shape),
            *pair(), *pair(), whole(vectors.shape),
        ],
        (blocks,), [block(model_width) for _ in range(5)],
        [shape(BF16), shape(F32), shape(BF16), shape(BF16), shape(BF16)],
    )


def add_row_sums(sums_ref, *values):
    @pl.when(pl.program_id(0) == 0)
    def _():
        sums_ref[...] = jnp.zeros_like(sums_ref)

    for row, value in enumerate(values):
        sums_ref[row : row + 1] += jnp.sum(value, 0, keepdims=True)


def middle_back_kernel(
    blocks, branch2_ref, back_ref, mid_ref, branch1_ref, grad_ref, grad_b2_ref, weight_own, weight_other,
    rows_ref, kept_ref, sent_ref, grad_mid_ref, grad_b1_ref, att_own_ref, att_other_ref, sums_ref,
):
    gate1, bias, scale2, gate2 = (rows_ref[row : row + 1] for row in range(4))
    block = pl.program_id(0)
    grad = grad_ref[...].astype(F32)
    mid = mid_ref[...]
    branch2 = branch2_ref[...] + bias
    output = (mid + gate2 * branch2).astype(BF16)

    @pl.when(block < blocks // 2)
    def _():
        kept_ref[...] = output

    @pl.when(block >= blocks // 2)
    def _():
        sent_ref[...] = output

    norm, inverse = normalize(mid)
    back = back_ref[...]
    grad_mid = grad + normalize_back(back * (1.0 + scale2), norm, inverse)
    grad_mid_ref[...] = grad_mid
    grad_b1 = (gate1 * grad_mid).astype(BF16)
    grad_b1_ref[...] = grad_b1
    att_own_ref[...] = dot_dims(grad_b1, weight_own[...], 1, 1).astype(BF16)
    att_other_ref[...] = dot_dims(grad_b1, weight_other[...], 1, 1).astype(BF16)
    add_row_sums(
        sums_ref, grad * branch2, grad_b2_ref[...].astype(F32), back, back * norm,
        grad_mid * branch1_ref[...].astype(F32), grad_b1.astype(F32),
    )


def middle_back(
    branch2, back, mid, branch1, grad, grad_b2, weight_own, weight_other, vectors, rows=256
):
    tokens, model_width = mid.shape
    width = weight_own.shape[0]
    blocks = tokens // rows
    full = lambda: row_blocks(rows, model_width)
    shape = lambda count, columns, kind: jax.ShapeDtypeStruct((count, columns), kind)
    return run(
        functools.partial(middle_back_kernel, blocks), 17, (),
        [branch2, back, mid, branch1, grad, grad_b2, weight_own, weight_other, vectors],
        [full() for _ in range(6)]
        + [
            constant_block(weight_own.shape), constant_block(weight_other.shape),
            constant_block(vectors.shape),
        ],
        (blocks,),
        [
            *halves(rows, model_width, blocks), full(), full(), row_blocks(rows, width),
            row_blocks(rows, width), constant_block((8, model_width)),
        ],
        [
            shape(tokens // 2, model_width, BF16), shape(tokens // 2, model_width, BF16),
            shape(tokens, model_width, F32), shape(tokens, model_width, BF16),
            shape(tokens, width, BF16), shape(tokens, width, BF16), shape(8, model_width, F32),
        ],
    )


def first_back_kernel(
    blocks, own_ref, other_ref, weight_own, weight_other, first_ref, second_ref, grad_mid_ref, rows_ref,
    kept_ref, sent_ref, sums_ref, own_sums_ref, other_sums_ref,
):
    block = pl.program_id(0)
    stream = jnp.where(block < blocks // 2, first_ref[...], second_ref[...])
    own, other = own_ref[...], other_ref[...]
    grad = dot_dims(own, weight_own[...], 1, 1) + dot_dims(other, weight_other[...], 1, 1)
    norm, inverse = normalize(stream.astype(F32))
    total = grad_mid_ref[...] + normalize_back(grad * (1.0 + rows_ref[0:1]), norm, inverse)

    @pl.when(block < blocks // 2)
    def _():
        kept_ref[...] = total

    @pl.when(block >= blocks // 2)
    def _():
        sent_ref[...] = total.astype(BF16)

    add_row_sums(sums_ref, grad, grad * norm)
    add_row_sums(own_sums_ref, own.astype(F32))
    add_row_sums(other_sums_ref, other.astype(F32))


def first_back(own, other, weight_own, weight_other, first, second, grad_mid, vectors, rows=256):
    tokens, model_width = grad_mid.shape
    width = untied(own).shape[1]
    blocks = tokens // rows
    full = lambda: row_blocks(rows, model_width)
    part = lambda: row_blocks(rows, width)
    shape = jax.ShapeDtypeStruct
    return run(
        functools.partial(first_back_kernel, blocks), 21, (),
        [own, other, weight_own, weight_other, first, second, grad_mid, vectors],
        [
            part(), part(), constant_block(weight_own.shape), constant_block(weight_other.shape),
            *halves(rows, model_width, blocks), full(), constant_block(vectors.shape),
        ],
        (blocks,),
        [
            *halves(rows, model_width, blocks), constant_block((8, model_width)),
            constant_block((8, width)), constant_block((8, width)),
        ],
        [
            shape((tokens // 2, model_width), F32), shape((tokens // 2, model_width), BF16),
            shape((8, model_width), F32), shape((8, width), F32), shape((8, width), F32),
        ],
    )


def bit_pairs(size, bit):
    return [(index, index ^ bit) for index in range(size)]


def swap(values, axis, bit):
    return lax.ppermute(values, axis, bit_pairs(lax.axis_size(axis), bit))


def pick(values, index, axis):
    return lax.dynamic_index_in_dim(values, index, axis, keepdims=False)


def place(first, second, index, axis=0):
    return jnp.where(
        index == 0,
        jnp.concatenate([first, second], axis),
        jnp.concatenate([second, first], axis),
    )


def cut_kernel(sizes, starts_ref, *refs):
    count = len(sizes)
    semaphores = refs[-1]
    copies = []
    for index, size in enumerate(sizes):
        rows = pl.ds(pl.multiple_of(starts_ref[index] * size, size), size)
        copies.append(
            pltpu.make_async_copy(
                refs[index].at[rows], refs[count + index], semaphores.at[index]
            )
        )
    for copy in copies:
        copy.start()
    for copy in copies:
        copy.wait()


def cut(values, places, sizes):
    return run(
        functools.partial(cut_kernel, sizes), 0, [jnp.stack(places).astype(jnp.int32)], list(values),
        [pl.BlockSpec(memory_space=pl.ANY)] * len(sizes), (1,),
        [pl.BlockSpec(memory_space=pltpu.VMEM)] * len(sizes),
        [
            jax.ShapeDtypeStruct((size,) + untied(value).shape[1:], untied(value).dtype)
            for value, size in zip(values, sizes)
        ],
        [pltpu.SemaphoreType.DMA((len(sizes),))],
    )


def joined_kernel(count, places_ref, *refs):
    out_ref, semaphores = refs[count:]
    rows = refs[0].shape[0]
    copies = [
        pltpu.make_async_copy(
            refs[index],
            out_ref.at[pl.ds(pl.multiple_of(places_ref[index] * rows, rows), rows)],
            semaphores.at[index],
        )
        for index in range(count)
    ]
    for copy in copies:
        copy.start()
    for copy in copies:
        copy.wait()


def joined(pieces, places):
    count = len(pieces)
    rows, width = untied(pieces[0]).shape
    return run(
        functools.partial(joined_kernel, count), 0, [places], list(pieces),
        [pl.BlockSpec(memory_space=pltpu.VMEM)] * count, (1,), pl.BlockSpec(memory_space=pl.ANY),
        jax.ShapeDtypeStruct((count * rows, width), BF16),
        [pltpu.SemaphoreType.DMA((count,))],
    )


def added_kernel(left_ref, right_ref, out_ref):
    out_ref[...] = (left_ref[...].astype(F32) + right_ref[...].astype(F32)).astype(BF16)


def added(left, right, *behind):
    whole = pl.BlockSpec(memory_space=pltpu.VMEM)
    out = jax.ShapeDtypeStruct(left.shape, BF16)
    return run(added_kernel, 0, (), [after(left, *behind), right], [whole, whole], (), whole, out)


def relay_kernel(value_ref, out_ref):
    out_ref[...] = value_ref[...]


def relay(value, *behind):
    whole = pl.BlockSpec(memory_space=pltpu.VMEM)
    out = jax.ShapeDtypeStruct(value.shape, value.dtype)
    return run(relay_kernel, 0, (), [after(value, *behind)], [whole], (), whole, out)


def gather_dp(values):
    size = lax.axis_size("dp")
    here = lax.axis_index("dp")
    step = 1
    while step < size:
        values = place(values, swap(values, "dp", step), lax.rem(here // step, 2))
        step *= 2
    return values


def sum_dp(values):
    step = 1
    while step < lax.axis_size("dp"):
        values = values + swap(values, "dp", step)
        step *= 2
    return values


def slot_device(
    latents,
    condition,
    cotangent,
    group_counts,
    heads_weight,
    heads_bias,
    merge_weight,
    merge_bias,
    up_weight,
    up_bias,
    down_weight,
    down_bias,
    modulate_weight,
    modulate_bias,
):
    side = lax.axis_index("tensor")
    place_dp = lax.axis_index("dp")
    core, x_bit, near, far = (lax.rem(place_dp // step, 2) for step in (1, 2, 4, 8))
    bits = (far, near, x_bit)
    half, model_width = latents.shape[1:]
    columns = heads_weight.shape[3]
    features = modulate_weight.shape[3]
    hidden_here = up_weight.shape[2]
    merge_own, up_own, down_own = merge_weight[0], up_weight[0], down_weight[0]
    padded_rows = lambda *rows: jnp.pad(jnp.stack(rows), ((0, 8 - len(rows)), (0, 0)))
    bit_value = lambda value: jnp.reshape(value, (1,)).astype(jnp.int32)
    core_value = bit_value(core)
    quarter = 2 * near + core
    places = 2 * jnp.stack([near, 1 - near, near, 1 - near]) + jnp.stack(
        [core, core, 1 - core, 1 - core]
    )
    places = places.astype(jnp.int32)

    def fetch(values):
        return swap(values, "tensor", 1)

    def pass_on(got):
        return got, swap(got, "dp", 4), swap(got, "dp", 1)

    def pass_last(passed, *behind):
        got, from_near, from_core = passed
        to_core = relay(from_near, *behind) if behind else from_near
        return got, from_near, from_core, swap(to_core, "dp", 1)

    def joined_after(passed, *behind):
        return joined((after(passed[0], *behind),) + passed[1:], places)

    def quarter_of(weight, *behind):
        return cut((after(weight, *behind),), (quarter,), (weight.shape[0] // 4,))[0]

    latent_own, latent_sent, cotangent_own = cut(
        (latents, latents, cotangent), (side, 1 - side, side), (1, 1, 1)
    )
    latent_other = fetch(latent_sent[0])
    heads_own = heads_weight[0].reshape(model_width, 3 * columns)
    core_places = jnp.stack([core, 1 - core]).astype(jnp.int32)

    def half_of(weight, *behind):
        return cut((after(weight, *behind),), (core,), (weight.shape[0] // 2,))[0]

    silu_cond = jax.nn.silu(condition.astype(F32)).astype(BF16)
    local_mod = jnp.einsum(
        "sd,dkc->skc", silu_cond, modulate_weight[0], preferred_element_type=F32
    ) + modulate_bias[0].astype(F32)
    mod_other = swap(pick(local_mod, 1 - side, 0), "tensor", 1)
    bias_pack = swap(jnp.concatenate([heads_bias.reshape(-1), up_bias.reshape(-1)]), "tensor", 1)
    shift1, scale1, gate1, shift2, scale2, gate2 = place(
        pick(local_mod, side, 0), mod_other, side, 1
    )

    def heads_offset(pair):
        return jnp.concatenate([pair[0], jnp.zeros_like(pair[0]), pair[1]]).astype(F32)[None]

    offset_own = heads_offset(heads_bias[0])
    offset_other = heads_offset(bias_pack[: 2 * columns].reshape(2, columns))
    up_bias_own = up_bias.astype(F32)
    up_bias_other = bias_pack[2 * columns :].reshape(1, hidden_here).astype(F32)
    shifts1 = padded_rows(shift1, scale1)

    heads_half = half_of(heads_own, latent_sent)
    heads_got = fetch(heads_half)
    filled = normed_project(
        after(latent_own[0], heads_half), shifts1, heads_own, offset_own
    )
    normed1, qkv_own = normed_project(latent_other, shifts1, heads_own, offset_own, filled)
    attended_own, logsum_own = attend(qkv_own)
    heads_got = relay(heads_got, attended_own)
    heads_core = swap(heads_got, "dp", 1)
    merge_half_own = half_of(merge_own, heads_got)
    (cotangent_sent,) = cut((after(cotangent, merge_half_own),), (1 - side,), (1,))
    merge_got = fetch(merge_half_own)
    cotangent_other = fetch(cotangent_sent[0])
    heads_other = joined((after(heads_got, cotangent_sent), heads_core), core_places)
    qkv_other = project(normed1, heads_other, offset_other)
    attended_other, logsum_other = attend(qkv_other)
    up_quarter = quarter_of(up_own, attended_other)
    up_passed = pass_on(fetch(up_quarter))
    merge_got = relay(merge_got, up_quarter)
    merge_other = joined((merge_got, swap(merge_got, "dp", 1)), core_places)
    live = bit_value(side < group_counts[0])
    branch1, mid, normed2, grad, grad_b2 = merge(
        live, attended_own, attended_other, merge_own, merge_other, latent_own[0], latent_other, cotangent_own[0],
        cotangent_other, padded_rows(gate1, merge_bias[0].astype(F32), shift2, scale2, gate2),
    )
    down_half = half_of(down_own, normed2)
    down_got = fetch(down_half)
    normed1_peer = swap(normed1, "dp", 1)
    normed2_peer = swap(normed2, "dp", 1)
    grad_b2_peer = swap(grad_b2, "dp", 1)
    branch2, back2, *hidden_own, up_sums_own = feed(
        core_value, after(normed2, down_half), grad_b2, up_own, up_bias_own, down_own
    )
    hidden_sent_own, hidden_own, pre_sent_own, pre_own = hidden_own
    hidden_peer_own, pre_peer_own = swap(hidden_sent_own, "dp", 1), swap(pre_sent_own, "dp", 1)

    far_of, near_of, x_of = (
        jnp.arange(8, dtype=jnp.int32) // step % 2 for step in (4, 2, 1)
    )
    where_x = 4 * (x_of == x_bit) + 2 * far_of + near_of
    where_near = 4 * (near_of == near) + 2 * far_of + x_of
    near_next = (near, 4)
    x_next = (x_bit, 2)

    def halved(kept, received, step, *behind):
        sent, kept = halve(bit_value(step[0]), kept, after(received, *behind))
        return kept, swap(sent, "dp", step[1])

    def halved_last(pairs, *behind):
        halves_here = [
            halve(bit_value(far), kept, after(received, *behind)) for kept, received in pairs
        ]
        sent = jnp.concatenate([sent[0] for sent, _ in halves_here], 1)
        return jnp.concatenate([kept[0] for _, kept in halves_here], 1), swap(sent, "dp", 8)

    def pair_total(own, other, *behind):
        return own.astype(F32) + swap(other, "tensor", 1).astype(F32)

    def swap_rows(total, *behind):
        total = total.astype(BF16).reshape((2, -1) + total.shape[1:])
        return pick(total, core, 0), swap(pick(total, 1 - core, 0), "dp", 1)

    def join_columns(mine, others):
        return place(mine, others, core, mine.ndim - 1).astype(F32)

    down_parts_own = weight_grad(
        where_x, grad_b2, after(grad_b2_peer, normed2), hidden_own, hidden_peer_own
    )
    down_first_own = swap(down_parts_own[0], "dp", 2)
    up_parts_own = weight_grad(
        where_near, after(normed2, down_parts_own[0]), normed2_peer, pre_own, pre_peer_own,
        weight=13,
    )
    up_first_own = swap(up_parts_own[0], "dp", 4)
    up_passed = pass_last(up_passed, up_parts_own[0])
    down_pieces = (down_got, swap(down_got, "dp", 1))
    up_other = joined_after(up_passed, up_parts_own[0])
    down_other = joined(
        (after(down_pieces[0], up_other), down_pieces[1]), core_places
    )
    branch2, back2, *hidden_other, up_sums_other = feed(
        core_value, normed2, grad_b2, up_other, up_bias_other, down_other, (branch2, back2)
    )
    hidden_sent_other, hidden_other, pre_sent_other, pre_other = hidden_other
    hidden_peer_other = swap(hidden_sent_other, "dp", 1)
    pre_peer_other = swap(pre_sent_other, "dp", 1)
    down_half_own = halved(down_parts_own[1], down_first_own, near_next, hidden_other)
    up_half_own = halved(up_parts_own[1], up_first_own, x_next, hidden_other)
    output_own, output_sent, grad_mid, grad_b1, grad_att_own, grad_att_other, middle_sums = middle_back(
        after(branch2, down_half_own[0], up_half_own[0]), back2, mid, branch1, grad, grad_b2,
        merge_own, merge_other, padded_rows(gate1, down_bias[0].astype(F32), scale2, gate2),
    )
    grad_gate2, down_bias_sum, grad_shift2, grad_scale2, grad_gate1, merge_bias_sum = middle_sums[:6]
    down_parts_other = weight_grad(
        where_x, grad_b2, after(grad_b2_peer, grad_att_own, grad_att_other),
        hidden_other, hidden_peer_other,
    )
    down_first_other = swap(down_parts_other[0], "dp", 2)
    up_parts_other = weight_grad(
        where_near, after(normed2, down_parts_other[0]), normed2_peer, pre_other, pre_peer_other
    )
    up_first_other = swap(up_parts_other[0], "dp", 4)
    output_other = swap(output_sent, "tensor", 1)
    grads_own, sent_own, kept_own = attend_back(
        core_value, qkv_own, attended_own, after(grad_att_own, up_parts_other[0]), logsum_own
    )
    heads_peer_own = swap(sent_own, "dp", 1)
    merge_total = outer_rows(
        grad_b1,
        jnp.concatenate([attended_own, attended_other], 1),
    ).astype(BF16).reshape(8, 2, -1, 2 * columns)
    merge_sent = swap(pick(merge_total, 1 - core, 1), "dp", 1)
    merge_total = pick(merge_total, core, 1).astype(F32) + merge_sent.astype(F32)
    merge_total = merge_total.astype(BF16).reshape((2, 2, 2) + merge_total.shape[1:])
    merge_first = swap(pick(merge_total, 1 - near, 1), "dp", 4)
    merge_kept = pick(merge_total, near, 1).reshape((4,) + merge_total.shape[3:])
    merge_first = merge_first.reshape(merge_kept.shape)
    down_half_other = halved(down_parts_other[1], down_first_other, near_next, grads_own)
    up_half_other = halved(up_parts_other[1], up_first_other, x_next, grads_own)
    feed_last_own = halved_last([down_half_own, up_half_own], down_half_other[0], up_half_other[0])
    block_output = place(output_own[None], output_other[None], side)
    grads_other, sent_other, kept_other = attend_back(
        core_value, qkv_other, attended_other,
        after(grad_att_other, feed_last_own[0], down_half_other[0], up_half_other[0]), logsum_other,
    )
    heads_peer_other = swap(sent_other, "dp", 1)
    feed_last_other = halved_last([down_half_other, up_half_other], grads_other)
    heads_parts_own = weight_grad(
        where_x, normed1, after(normed1_peer, feed_last_other[0], merge_kept),
        kept_own, heads_peer_own, weight=13,
    )
    heads_first_own = swap(heads_parts_own[0], "dp", 2)
    heads_parts_other = weight_grad(
        where_x, normed1, after(normed1_peer, heads_parts_own[0]), kept_other, heads_peer_other
    )
    heads_first_other = swap(heads_parts_other[0], "dp", 2)
    done = heads_parts_other[0]
    merge_half = halved(merge_kept, merge_first, x_next, done)
    feed_own = added(*feed_last_own, done)
    grad_latent, latent_sent, first_sums, heads_sums_own, heads_sums_other = first_back(
        grads_own, after(grads_other, done, merge_half[0], feed_own), heads_own, heads_other,
        latent_own[0], latent_other, grad_mid, padded_rows(scale1),
    )
    heads_half_own = halved(heads_parts_own[1], heads_first_own, near_next, grad_latent)
    heads_half_other = halved(
        heads_parts_other[1], heads_first_other, near_next, heads_half_own[0]
    )
    latent_sent = swap(latent_sent, "tensor", 1)
    feed_other = added(*feed_last_other, heads_half_other[0])
    feed_total = pair_total(feed_own, feed_other)
    merge_last = halved_last([merge_half], feed_other)
    heads_last = halved_last([heads_half_own, heads_half_other], feed_other)
    feed_mine, feed_others = swap_rows(feed_total)
    cut_at = feed_mine.shape[1] // 2
    down_grad = join_columns(feed_mine[:, :cut_at], feed_others[:, :cut_at])
    up_grad = join_columns(feed_mine[:, cut_at:], feed_others[:, cut_at:])
    grad_shift1, grad_scale1 = first_sums[0], first_sums[1]
    merge_total = added(*merge_last, heads_last[0])
    heads_total = added(*heads_last, merge_total)
    cut_at = heads_total.shape[1] // 2
    heads_total = pair_total(heads_total[:, :cut_at], heads_total[:, cut_at:])
    latent_sent = latent_sent.astype(F32)
    heads_total = heads_total[:, : 3 * columns // 2]
    heads_grad = join_columns(
        *swap_rows(heads_total.reshape(heads_total.shape[0], 3, columns // 2))
    )
    merge_grad = pair_total(merge_total[:, :columns], merge_total[:, columns:], latent_sent)

    def query_value_sums(sums):
        return jnp.concatenate([sums[0, :columns], sums[0, 2 * columns :]])

    def by_side(rows):
        rows = rows.reshape(rows.shape[:-1] + (2, features))
        return pick(rows, side, rows.ndim - 2), pick(rows, 1 - side, rows.ndim - 2)

    grad_mod = jnp.stack(
        [grad_shift1, grad_scale1, grad_gate1, grad_shift2, grad_scale2, grad_gate2]
    ).astype(BF16)
    grad_mod_own, grad_mod_sent = by_side(grad_mod)
    merge_own_sum, merge_other_sum = by_side(merge_bias_sum)
    down_own_sum, down_other_sum = by_side(down_bias_sum)
    bias_own = jnp.concatenate(
        [query_value_sums(heads_sums_own), merge_own_sum, up_sums_own[0], down_own_sum]
    )
    bias_other = jnp.concatenate(
        [query_value_sums(heads_sums_other), merge_other_sum, up_sums_other[0], down_other_sum]
    )
    crossing = jnp.concatenate([bias_other, grad_mod_sent.astype(F32).reshape(-1)])
    crossing = swap(relay(crossing.reshape(-1, 128), heads_last[0]), "tensor", 1).reshape(-1)
    bias_total = sum_dp(bias_own + crossing[: bias_own.shape[0]])
    grad_mod_slots = place(
        grad_mod_own[None],
        crossing[bias_own.shape[0] :].astype(BF16).reshape(grad_mod_own[None].shape), side,
    )
    slots_here = silu_cond.shape[0]
    tail = jnp.concatenate([silu_cond, grad_mod_slots.reshape(slots_here, -1)], 1)
    tail_all = gather_dp(tail)
    silu_all = tail_all[:, :model_width]
    grad_mod_all = tail_all[:, model_width:].reshape((-1,) + grad_mod_slots.shape[1:])
    rows_here = model_width // lax.axis_size("dp")
    silu_rows = lax.dynamic_slice_in_dim(silu_all, place_dp * rows_here, rows_here, 1)
    modulate_grad = jnp.einsum("sd,skc->dkc", silu_rows, grad_mod_all, preferred_element_type=F32)
    modulate_bias_grad = jnp.sum(grad_mod_all.astype(F32), 0)
    cond_partial = jnp.einsum(
        "dkc,skc->sd", modulate_weight[0], grad_mod_slots, preferred_element_type=F32
    )
    cond_total = cond_partial + swap(cond_partial, "tensor", 1)
    condition_grad = jax.vjp(jax.nn.silu, condition.astype(F32))[1](cond_total)[0]
    latent_grad = place(grad_latent[None], latent_sent[None], side)
    edges = (0, 2 * columns, 2 * columns + features, 2 * columns + features + hidden_here, None)
    heads_bias_grad, merge_bias_grad, up_bias_grad, down_bias_grad = (
        bias_total[first:last] for first, last in zip(edges, edges[1:])
    )
    return (
        block_output,
        latent_grad,
        condition_grad,
        heads_grad[None],
        heads_bias_grad.reshape(1, 2, columns),
        merge_grad.T[None],
        merge_bias_grad[None],
        up_grad[None],
        up_bias_grad[None],
        down_grad.T[None],
        down_bias_grad[None],
        modulate_grad[None],
        modulate_bias_grad[None],
    )


def solution(mesh):
    in_specs = (
        P("dp", "tensor", None),
        P("dp", None),
        P("dp", "tensor", None),
        P("dp"),
        P(None, None, None, "tensor"),
        P(None, None, "tensor"),
        P(None, "tensor", None),
        P(),
        P(None, None, "tensor"),
        P(None, "tensor"),
        P(None, "tensor", None),
        P(),
        P(None, None, None, "tensor"),
        P(None, None, "tensor"),
    )
    out_specs = (
        P("dp", "tensor", None),
        P("dp", "tensor", None),
        P("dp", None),
        P(None, "dp", None, "tensor"),
        P(None, None, "tensor"),
        P(None, "tensor", "dp"),
        P(None, "tensor"),
        P(None, "dp", "tensor"),
        P(None, "tensor"),
        P(None, "tensor", "dp"),
        P(None, "tensor"),
        P(None, "dp", None, "tensor"),
        P(None, None, "tensor"),
    )
    whole_slots = mesh.shape["tensor"] == 2 and mesh.shape["dp"] == 16
    return jax.shard_map(
        slot_device if whole_slots else per_device, mesh=mesh, in_specs=in_specs, out_specs=out_specs, check_vma=False
    )
```

```python
import functools
import math

import jax
import jax.numpy as jnp
from jax import lax
from jax.experimental import pallas as pl
from jax.experimental.pallas import tpu as pltpu
from jax.sharding import PartitionSpec as P

HEAD_DIM = 72
QUERY_BLOCK = 512


epsilon = 1e-06


def normalize(stream):
    average = jnp.mean(stream, -1, keepdims=True)
    centered = stream - average
    variance = jnp.mean(centered * centered, -1, keepdims=True)
    inverse = lax.rsqrt(variance + epsilon)
    return (centered * inverse, inverse)


def normalize_back(grad_norm, normed, inverse):
    first_mean = jnp.mean(grad_norm, -1, keepdims=True)
    second_mean = jnp.mean(grad_norm * normed, -1, keepdims=True)
    return inverse * (grad_norm - first_mean - normed * second_mean)


def gelu_tanh(values):
    return jax.nn.gelu(values, approximate=True)


def column_sums(operand):
    return jnp.sum(operand.astype(jnp.float32), 0)


def outer_rows(operand, other):
    return lax.dot_general(
        operand, other, (((0,), (0,)), ((), ())), preferred_element_type=jnp.float32
    )


def times_transposed(operand, weight):
    return lax.dot_general(
        operand, weight, (((1,), (1,)), ((), ())), preferred_element_type=jnp.float32
    )


def gather_tokens(values):
    return lax.all_gather(values, "tensor", axis=0, tiled=True)


def gather_grads(values):
    return lax.all_gather(values, "tensor", axis=0, tiled=True)


def scatter_branch(operand, weight):

    def partial_rows(first_row, row_count):
        return jnp.dot(operand, weight, preferred_element_type=jnp.float32)

    return lax.psum_scatter(
        partial_rows(
            jnp.int32(0), operand.shape[0] // lax.axis_size("tensor") * lax.axis_size("tensor")
        ).astype(jnp.bfloat16),
        "tensor",
        scatter_dimension=0,
        tiled=True,
    ).astype(jnp.float32)


def scatter_inputs(operand, weight):

    def partial_rows(first_row, row_count):
        return times_transposed(operand, weight)

    return lax.psum_scatter(
        partial_rows(
            jnp.int32(0), operand.shape[0] // lax.axis_size("tensor") * lax.axis_size("tensor")
        ).astype(jnp.bfloat16),
        "tensor",
        scatter_dimension=0,
        tiled=True,
    ).astype(jnp.float32)


def stack_member(layer_tuples, member):
    return jnp.stack([entry_tuple[member] for entry_tuple in layer_tuples])


def attend_forward(queries, key_rows, value_rows):
    length, heads_here = (queries.shape[0], queries.shape[1])
    blocks = length // QUERY_BLOCK
    score_scale = HEAD_DIM ** (-0.5)

    def one_block(query_block):
        scores = (
            jnp.einsum("qhd,khd->hqk", query_block, key_rows, preferred_element_type=jnp.float32)
            * score_scale
        )
        row_max = jnp.max(scores, -1, keepdims=True)
        exponent = jnp.exp(scores - row_max)
        row_total = jnp.sum(exponent, -1, keepdims=True)
        attn_probs = (exponent / row_total).astype(jnp.bfloat16)
        attended = jnp.einsum(
            "hqk,khd->qhd", attn_probs, value_rows, preferred_element_type=jnp.float32
        )
        return (attended.astype(jnp.bfloat16), (row_max + jnp.log(row_total))[:, :, 0])

    attended, logsum = lax.map(
        one_block, queries.reshape(blocks, QUERY_BLOCK, heads_here, HEAD_DIM)
    )
    return (attended.reshape(length, heads_here * HEAD_DIM), logsum)


def attend_backward(queries, key_rows, value_rows, logsum, grad_attended):
    length, heads_here = (queries.shape[0], queries.shape[1])
    blocks = length // QUERY_BLOCK
    score_scale = HEAD_DIM ** (-0.5)
    block_shape = (blocks, QUERY_BLOCK, heads_here, HEAD_DIM)

    def one_block(running, inputs_here):
        grad_keys, grad_values = running
        query_block, grad_block, logsum_block = inputs_here
        scores = (
            jnp.einsum("qhd,khd->hqk", query_block, key_rows, preferred_element_type=jnp.float32)
            * score_scale
        )
        attn_probs = jnp.exp(scores - logsum_block[:, :, None])
        grad_values = grad_values + jnp.einsum(
            "hqk,qhd->khd",
            attn_probs.astype(jnp.bfloat16),
            grad_block,
            preferred_element_type=jnp.float32,
        )
        grad_probs = jnp.einsum(
            "qhd,khd->hqk", grad_block, value_rows, preferred_element_type=jnp.float32
        )
        row_dot = jnp.sum(attn_probs * grad_probs, -1, keepdims=True)
        grad_scores = (attn_probs * (grad_probs - row_dot)).astype(jnp.bfloat16)
        grad_queries = (
            jnp.einsum("hqk,khd->qhd", grad_scores, key_rows, preferred_element_type=jnp.float32)
            * score_scale
        )
        grad_keys = (
            grad_keys
            + jnp.einsum(
                "hqk,qhd->khd", grad_scores, query_block, preferred_element_type=jnp.float32
            )
            * score_scale
        )
        return ((grad_keys, grad_values), grad_queries.astype(jnp.bfloat16))

    zeros_kv = jnp.zeros((length, heads_here, HEAD_DIM), jnp.float32)
    scanned = (queries.reshape(block_shape), grad_attended.reshape(block_shape), logsum)
    (grad_keys, grad_values), grad_queries = lax.scan(one_block, (zeros_kv, zeros_kv), scanned)
    flat_shape = (length, heads_here * HEAD_DIM)
    return (
        grad_queries.reshape(flat_shape),
        grad_keys.astype(jnp.bfloat16).reshape(flat_shape),
        grad_values.astype(jnp.bfloat16).reshape(flat_shape),
    )


def forward_layer(stream, modulation, layer_weights, heads_here):
    (
        flat_heads,
        heads_offset,
        merge_weight,
        merge_bias,
        up_weight,
        up_bias,
        down_weight,
        down_bias,
    ) = layer_weights
    length = stream.shape[0] * lax.axis_size("tensor")
    columns = flat_heads.shape[1] // 3
    norm_first, inverse_first = normalize(stream)
    normed_first = (norm_first * (1.0 + modulation[1]) + modulation[0]).astype(jnp.bfloat16)
    gathered_first = gather_tokens(normed_first)
    projected = (
        jnp.dot(gathered_first, flat_heads, preferred_element_type=jnp.float32) + heads_offset
    ).astype(jnp.bfloat16)
    split_shape = (length, heads_here, HEAD_DIM)
    queries = projected[:, :columns].reshape(split_shape)
    key_rows = projected[:, columns : 2 * columns].reshape(split_shape)
    value_rows = projected[:, 2 * columns :].reshape(split_shape)
    attended, logsum = attend_forward(queries, key_rows, value_rows)
    branch_first = scatter_branch(attended, merge_weight) + merge_bias.astype(jnp.float32)
    stream_mid = stream + modulation[2] * branch_first
    norm_second, inverse_second = normalize(stream_mid)
    normed_second = (norm_second * (1.0 + modulation[4]) + modulation[3]).astype(jnp.bfloat16)
    gathered_second = gather_tokens(normed_second)
    hidden_pre = jnp.dot(
        gathered_second, up_weight, preferred_element_type=jnp.float32
    ) + up_bias.astype(jnp.float32)
    hidden = gelu_tanh(hidden_pre).astype(jnp.bfloat16)
    branch_second = scatter_branch(hidden, down_weight) + down_bias.astype(jnp.float32)
    stream_next = stream_mid + modulation[5] * branch_second
    first_input, second_input = (gathered_first, gathered_second)
    kept = (
        norm_first,
        inverse_first,
        first_input,
        queries,
        key_rows,
        value_rows,
        logsum,
        attended,
        branch_first,
        norm_second,
        inverse_second,
        second_input,
        hidden_pre,
        hidden,
        branch_second,
    )
    return (stream_next, kept)


def backward_layer(grad_stream, modulation, layer_weights, kept):
    (
        flat_heads,
        heads_offset,
        merge_weight,
        merge_bias,
        up_weight,
        up_bias,
        down_weight,
        down_bias,
    ) = layer_weights
    (
        norm_first,
        inverse_first,
        first_input,
        queries,
        key_rows,
        value_rows,
        logsum,
        attended,
        branch_first,
        norm_second,
        inverse_second,
        second_input,
        hidden_pre,
        hidden,
        branch_second,
    ) = kept
    model_width = flat_heads.shape[0]
    columns = flat_heads.shape[1] // 3
    grad_branch_second = (modulation[5] * grad_stream).astype(jnp.bfloat16)
    grad_gate_second = jnp.sum(grad_stream * branch_second, 0)
    grad_down_bias = column_sums(grad_branch_second)
    gathered_grad = gather_grads(grad_branch_second)
    down_grad = outer_rows(hidden, gathered_grad)
    grad_hidden = times_transposed(gathered_grad, down_weight)
    grad_pre = jax.vjp(gelu_tanh, hidden_pre)[1](grad_hidden)[0].astype(jnp.bfloat16)
    up_bias_grad = column_sums(grad_pre)
    up_grad = outer_rows(second_input, grad_pre)
    grad_normed_second = scatter_inputs(grad_pre, up_weight)
    grad_shift_second = jnp.sum(grad_normed_second, 0)
    grad_scale_second = jnp.sum(grad_normed_second * norm_second, 0)
    grad_mid = grad_stream + normalize_back(
        grad_normed_second * (1.0 + modulation[4]), norm_second, inverse_second
    )
    grad_branch_first = (modulation[2] * grad_mid).astype(jnp.bfloat16)
    grad_gate_first = jnp.sum(grad_mid * branch_first, 0)
    grad_merge_bias = column_sums(grad_branch_first)
    gathered_grad = gather_grads(grad_branch_first)
    merge_grad = outer_rows(attended, gathered_grad)
    grad_attended = times_transposed(gathered_grad, merge_weight).astype(jnp.bfloat16)
    grad_queries, grad_keys, grad_values = attend_backward(
        queries, key_rows, value_rows, logsum, grad_attended
    )
    grad_projected = jnp.concatenate([grad_queries, grad_keys, grad_values], 1)
    heads_bias_grad = jnp.stack([column_sums(grad_queries), column_sums(grad_values)])
    heads_grad = outer_rows(first_input, grad_projected).reshape(model_width, 3, columns)
    grad_normed_first = scatter_inputs(grad_projected, flat_heads)
    grad_shift_first = jnp.sum(grad_normed_first, 0)
    grad_scale_first = jnp.sum(grad_normed_first * norm_first, 0)
    grad_before = grad_mid + normalize_back(
        grad_normed_first * (1.0 + modulation[1]), norm_first, inverse_first
    )
    extra = jnp.stack(
        [
            grad_shift_first,
            grad_scale_first,
            grad_gate_first,
            grad_shift_second,
            grad_scale_second,
            grad_gate_second,
            grad_merge_bias,
            grad_down_bias,
        ]
    )
    return (
        grad_before,
        (heads_grad, heads_bias_grad, merge_grad, up_grad, up_bias_grad, down_grad),
        extra,
    )


def per_device(
    latents,
    condition,
    cotangent,
    group_counts,
    heads_weight,
    heads_bias,
    merge_weight,
    merge_bias,
    up_weight,
    up_bias,
    down_weight,
    down_bias,
    modulate_weight,
    modulate_bias,
):
    slot_count = latents.shape[0]
    model_width = latents.shape[2]
    layer_count = heads_weight.shape[0]
    columns = heads_weight.shape[3]
    heads_here = columns // HEAD_DIM
    silu_cond = jax.nn.silu(condition.astype(jnp.float32)).astype(jnp.bfloat16)
    local_mod = jnp.einsum(
        "sd,bdkc->sbkc", silu_cond, modulate_weight, preferred_element_type=jnp.float32
    ) + modulate_bias.astype(jnp.float32)
    modulation_all = lax.all_gather(local_mod, "tensor", axis=3, tiled=True)
    flat_heads = heads_weight.reshape(layer_count, model_width, 3 * columns)
    zero_bias = jnp.zeros((layer_count, columns), heads_bias.dtype)
    heads_offset = (
        jnp.stack([heads_bias[:, 0], zero_bias, heads_bias[:, 1]], 1)
        .reshape(layer_count, 3 * columns)
        .astype(jnp.float32)
    )
    per_layer = [
        (
            flat_heads[0],
            heads_offset[0],
            merge_weight[0],
            merge_bias[0],
            up_weight[0],
            up_bias[0],
            down_weight[0],
            down_bias[0],
        )
    ]
    layer_sums = [None] * layer_count
    modulate_sum = jnp.zeros(modulate_weight.shape, jnp.float32)
    modulate_bias_sum = jnp.zeros(modulate_bias.shape, jnp.float32)
    merge_bias_sum = jnp.zeros((layer_count, columns), jnp.float32)
    down_bias_sum = jnp.zeros((layer_count, columns), jnp.float32)
    output_list, latent_list, condition_list = ([], [], [])
    for slot_index in range(slot_count):
        live_flag = (slot_index < group_counts[0]).astype(jnp.float32)
        stream = latents[slot_index].astype(jnp.float32)
        layer_index = 0
        stream, kept = forward_layer(
            stream, modulation_all[slot_index, layer_index], per_layer[layer_index], heads_here
        )
        saved_layers = [kept]
        output_list.append(stream.astype(jnp.bfloat16))
        grad_stream = cotangent[slot_index].astype(jnp.float32) * live_flag
        extras = [None] * layer_count
        for layer_index in reversed(range(layer_count)):
            grad_stream, layer_grads, extra = backward_layer(
                grad_stream,
                modulation_all[slot_index, layer_index],
                per_layer[layer_index],
                saved_layers[layer_index],
            )
            if layer_sums[layer_index] is None:
                layer_sums[layer_index] = layer_grads
            else:
                layer_sums[layer_index] = jax.tree.map(
                    jnp.add, layer_sums[layer_index], layer_grads
                )
            extras[layer_index] = extra
        latent_list.append(grad_stream)
        shared = lax.psum_scatter(
            jnp.stack(extras).astype(jnp.bfloat16), "tensor", scatter_dimension=2, tiled=True
        ).astype(jnp.float32)
        grad_mod = shared[:, :6].astype(jnp.bfloat16)
        modulate_sum = modulate_sum + jnp.einsum(
            "d,bkc->bdkc", silu_cond[slot_index], grad_mod, preferred_element_type=jnp.float32
        )
        modulate_bias_sum = modulate_bias_sum + grad_mod.astype(jnp.float32)
        merge_bias_sum = merge_bias_sum + shared[:, 6]
        down_bias_sum = down_bias_sum + shared[:, 7]
        cond_partial = jnp.einsum(
            "bdkc,bkc->d", modulate_weight, grad_mod, preferred_element_type=jnp.float32
        )
        cond_total = lax.psum(cond_partial, "tensor")
        silu_grad = jax.vjp(jax.nn.silu, condition[slot_index].astype(jnp.float32))[1](cond_total)[
            0
        ]
        condition_list.append(silu_grad)
    weight_grads = (
        lax.psum_scatter(
            stack_member(layer_sums, 0).astype(jnp.bfloat16), "dp", scatter_dimension=1, tiled=True
        ).astype(jnp.float32),
        lax.psum_scatter(
            stack_member(layer_sums, 2).astype(jnp.bfloat16), "dp", scatter_dimension=2, tiled=True
        ).astype(jnp.float32),
        lax.psum_scatter(
            stack_member(layer_sums, 3).astype(jnp.bfloat16), "dp", scatter_dimension=1, tiled=True
        ).astype(jnp.float32),
        lax.psum_scatter(
            stack_member(layer_sums, 5).astype(jnp.bfloat16), "dp", scatter_dimension=2, tiled=True
        ).astype(jnp.float32),
        lax.psum_scatter(
            modulate_sum.astype(jnp.bfloat16), "dp", scatter_dimension=1, tiled=True
        ).astype(jnp.float32),
    )
    bias_grads = lax.psum(
        (
            stack_member(layer_sums, 1),
            merge_bias_sum,
            stack_member(layer_sums, 4),
            down_bias_sum,
            modulate_bias_sum,
        ),
        "dp",
    )
    block_output = jnp.stack(output_list)
    latent_grad = jnp.stack(latent_list)
    condition_grad = jnp.stack(condition_list)
    return (
        block_output,
        latent_grad,
        condition_grad,
        weight_grads[0],
        bias_grads[0],
        weight_grads[1],
        bias_grads[1],
        weight_grads[2],
        bias_grads[2],
        weight_grads[3],
        bias_grads[3],
        weight_grads[4],
        bias_grads[4],
    )


F32 = jnp.float32
BF16 = jnp.bfloat16
SCORE_SCALE = HEAD_DIM ** (-0.5)
SCORE_LOG2 = SCORE_SCALE * math.log2(math.e)
VMEM_BYTES = 60 * 2**20


def cost(weight):
    return pl.CostEstimate(flops=weight * 50 * 10**8, bytes_accessed=10**5, transcendentals=0)


class Tied:
    def __init__(self, value, behind):
        self.value, self.behind = value, behind


def untied(value):
    return value.value if isinstance(value, Tied) else value


def after(value, *behind):
    return Tied(value, behind)


def run(kernel, weight, scalars, inputs, in_specs, grid, out_specs, out_shape, scratch=(), aliases={}):
    behind = []
    for value in inputs:
        if isinstance(value, Tied):
            behind += [untied(other) for other in value.behind]
    inputs = [untied(value) for value in inputs]
    first = len(scalars) + len(inputs)

    def without_ties(*refs):
        kernel(*refs[:first], *refs[first + len(behind) :])

    return pl.pallas_call(
        without_ties,
        grid_spec=pltpu.PrefetchScalarGridSpec(
            num_scalar_prefetch=len(scalars),
            grid=grid,
            in_specs=list(in_specs) + [pl.BlockSpec(memory_space=pl.ANY)] * len(behind),
            out_specs=out_specs,
            scratch_shapes=list(scratch),
        ),
        out_shape=out_shape,
        input_output_aliases=aliases,
        compiler_params=pltpu.CompilerParams(vmem_limit_bytes=VMEM_BYTES),
        cost_estimate=cost(weight),
    )(*scalars, *inputs, *behind)


def dot_dims(left, right, left_dim, right_dim):
    return lax.dot_general(
        left, right, (((left_dim,), (right_dim,)), ((), ())), preferred_element_type=F32
    )


def head_slice(part, head, width):
    return slice(part * width + head * HEAD_DIM, part * width + (head + 1) * HEAD_DIM)


def attend_kernel(heads, qkv_ref, out_ref, logsum_ref):
    width = heads * HEAD_DIM
    rows_here = out_ref.shape[0]
    rows = pl.ds(pl.multiple_of(pl.program_id(0) * rows_here, rows_here), rows_here)
    for head in range(heads):
        queries = qkv_ref[rows, head_slice(0, head, width)]
        scores = dot_dims(qkv_ref[:, head_slice(1, head, width)], queries, 1, 1)
        top = jnp.max(scores, 0, keepdims=True)
        exponent = jnp.exp2((scores - top) * SCORE_LOG2)
        total = jnp.sum(exponent, 0, keepdims=True)
        mixed = dot_dims(qkv_ref[:, head_slice(2, head, width)], exponent.astype(BF16), 0, 0)
        out_ref[:, head_slice(0, head, width)] = (mixed / total).T.astype(BF16)
        logsum_ref[head : head + 1, :] = top * SCORE_LOG2 + jnp.log2(total)


def attend(qkv, query_rows=1024):
    tokens, width = untied(qkv).shape[0], untied(qkv).shape[1] // 3
    heads = width // HEAD_DIM
    return run(
        functools.partial(attend_kernel, heads), 18, (), [qkv],
        [pl.BlockSpec((tokens, 3 * width), lambda i: (0, 0))],
        (tokens // query_rows,),
        [
            pl.BlockSpec((query_rows, width), lambda i: (i, 0)),
            pl.BlockSpec((heads, query_rows), lambda i: (0, i)),
        ],
        [
            jax.ShapeDtypeStruct((tokens, width), BF16),
            jax.ShapeDtypeStruct((heads, tokens), F32),
        ],
    )


def attend_back_kernel(
    heads, key_rows, steps, core_ref,
    qkv_ref, out_ref, grad_ref, logsum_ref, grads_ref, sent_ref, kept_ref, dot_ref, query_ref,
):
    step = pl.program_id(0)
    width = heads * HEAD_DIM
    rows = pl.ds(pl.multiple_of(step * key_rows, key_rows), key_rows)

    @pl.when(step == 0)
    def _():
        owner = lax.broadcasted_iota(jnp.int32, (heads, width), 1)
        first = lax.broadcasted_iota(jnp.int32, (heads, width), 0) * HEAD_DIM
        member = ((owner >= first) & (owner < first + HEAD_DIM)).astype(BF16)
        product = grad_ref[...].astype(F32) * out_ref[...].astype(F32)
        high = product.astype(BF16)
        low = (product - high.astype(F32)).astype(BF16)
        dot_ref[...] = dot_dims(member, high, 1, 1) + dot_dims(member, low, 1, 1)
        query_ref[...] = jnp.zeros_like(query_ref)

    def store(part, head, rows, value):
        grads_ref[rows, head_slice(part, head, width)] = value

    for head in range(heads):
        queries = qkv_ref[:, head_slice(0, head, width)]
        keys = qkv_ref[rows, head_slice(1, head, width)]
        grad = grad_ref[:, head_slice(0, head, width)]
        scores = dot_dims(keys, queries, 1, 1)
        probs = jnp.exp2(scores * SCORE_LOG2 - logsum_ref[head : head + 1, :])
        grad_probs = dot_dims(qkv_ref[rows, head_slice(2, head, width)], grad, 1, 1)
        grad_scores = (probs * (grad_probs - dot_ref[head : head + 1, :])).astype(BF16)
        grad_values = jnp.dot(probs.astype(BF16), grad, preferred_element_type=F32)
        store(2, head, rows, grad_values.astype(BF16))
        grad_keys = jnp.dot(grad_scores, queries, preferred_element_type=F32) * SCORE_SCALE
        store(1, head, rows, grad_keys.astype(BF16))
        query_ref[head] += dot_dims(keys, grad_scores, 0, 0)

    @pl.when(step == steps - 1)
    def _():
        for head in range(heads):
            store(0, head, slice(None), (query_ref[head] * SCORE_SCALE).T.astype(BF16))
        half = width // 2
        for first in range(2):

            @pl.when(core_ref[0] == first)
            def _():
                for part in range(3):
                    here, there = (part * width + side * half for side in (first, 1 - first))
                    to = slice(part * half, (part + 1) * half)
                    kept_ref[:, to] = grads_ref[:, here : here + half]
                    sent_ref[:, to] = grads_ref[:, there : there + half]
                rest = slice(3 * half, kept_ref.shape[1])
                kept_ref[:, rest] = jnp.zeros_like(kept_ref[:, rest])
                sent_ref[:, rest] = jnp.zeros_like(sent_ref[:, rest])


def attend_back(core, qkv, attended, grad_attended, logsum, key_rows=1024):
    tokens, width = attended.shape
    heads = width // HEAD_DIM
    steps = tokens // key_rows
    whole = lambda *shape: pl.BlockSpec(shape, lambda i, core_ref: (0,) * len(shape))
    half = (tokens, -(-3 * width // 256) * 128)
    return run(
        functools.partial(attend_back_kernel, heads, key_rows, steps), 32,
        [core], [qkv, attended, grad_attended, logsum],
        [
            whole(tokens, 3 * width), whole(tokens, width), whole(tokens, width),
            whole(heads, tokens),
        ],
        (steps,),
        [whole(tokens, 3 * width), whole(*half), whole(*half)],
        [
            jax.ShapeDtypeStruct((tokens, 3 * width), BF16),
            jax.ShapeDtypeStruct(half, BF16),
            jax.ShapeDtypeStruct(half, BF16),
        ],
        [pltpu.VMEM((heads, tokens), F32), pltpu.VMEM((heads, HEAD_DIM, tokens), F32)],
    )


GELU_OUTER = math.sqrt(2 / math.pi)
GELU_CUBIC = 0.044715


def gelu_and_slope(values):
    square = values * values
    tanh = jnp.tanh(values * (GELU_OUTER + GELU_OUTER * GELU_CUBIC * square))
    half = 0.5 + 0.5 * tanh
    inner = 0.5 * GELU_OUTER + 1.5 * GELU_OUTER * GELU_CUBIC * square
    return values * half, half + values * (1.0 - tanh * tanh) * inner


def feed_kernel(
    token_rows, carried, core_ref, normed_ref, grad_ref, up_ref, bias_ref, down_ref, *refs
):
    if carried:
        branch_in, normed_in = refs[:2]
        refs = refs[2:]
    branch_ref, back_ref, hidden_sent, hidden_kept, pre_sent, pre_kept, bias_grad_ref = refs
    chunk = pl.program_id(0)
    bias_grad_ref[...] = jnp.zeros_like(bias_grad_ref)

    def block(hidden_ref, pre_ref, index, _):
        rows = pl.ds(pl.multiple_of(index * token_rows, token_rows), token_rows)
        pre = jnp.dot(normed_ref[rows, :], up_ref[...], preferred_element_type=F32)
        grad_hidden = dot_dims(grad_ref[rows, :], down_ref[...], 1, 1)
        hidden, slope = gelu_and_slope(pre + bias_ref[...])
        hidden = hidden.astype(BF16)
        grad_pre = (grad_hidden * slope).astype(BF16)
        bias_grad_ref[...] += jnp.sum(grad_pre.astype(F32), 0, keepdims=True)
        hidden_ref[rows, :] = hidden
        pre_ref[rows, :] = grad_pre
        branch = jnp.dot(hidden, down_ref[...], preferred_element_type=F32)
        back = dot_dims(grad_pre, up_ref[...], 1, 1)
        if hidden_ref is hidden_kept:
            branch_ref[rows, :] += branch
            back_ref[rows, :] += back
        else:
            branch_ref[rows, :] = branch + branch_in[rows, :] if carried else branch
            back_ref[rows, :] = back + normed_in[rows, :] if carried else back
        return 0

    for step, refs_here in enumerate(((hidden_sent, pre_sent), (hidden_kept, pre_kept))):

        @pl.when(chunk == step)
        def _():
            lax.fori_loop(
                0, normed_ref.shape[0] // token_rows, functools.partial(block, *refs_here), 0
            )


def feed(core, normed, grad, up, bias, down, carried=(), token_rows=512):
    tokens, model_width = untied(normed).shape
    hidden_here = up.shape[1]
    width = hidden_here // 2
    chunk = lambda j, core_ref: lax.rem(j + 1 + core_ref[0], 2)
    single = pl.Buffered(1)
    whole = lambda: pl.BlockSpec((tokens, model_width), lambda j, c: (0, 0), pipeline_mode=single)
    part = lambda: pl.BlockSpec((tokens, width), lambda j, c: (0, 0), pipeline_mode=single)
    return run(
        functools.partial(feed_kernel, token_rows, len(carried) > 0), 44,
        [core], [normed, grad, up, bias, down, *carried],
        [
            whole(), whole(),
            pl.BlockSpec((model_width, width), lambda j, c: (0, chunk(j, c))),
            pl.BlockSpec((1, width), lambda j, c: (0, chunk(j, c))),
            pl.BlockSpec((width, model_width), lambda j, c: (chunk(j, c), 0)),
        ] + [whole() for _ in carried],
        (2,),
        [
            whole(), whole(), part(), part(), part(), part(),
            pl.BlockSpec((1, width), lambda j, c: (0, chunk(j, c))),
        ],
        [jax.ShapeDtypeStruct((tokens, model_width), F32)] * 2
        + [jax.ShapeDtypeStruct((tokens, width), BF16)] * 4
        + [jax.ShapeDtypeStruct((1, hidden_here), F32)],
    )


def weight_grad_kernel(chunks, blocks, where_ref, left_mine, left_peer, *refs):
    rights, outs, left_ref = refs[: 2 * chunks], refs[2 * chunks : -1], refs[-1]
    tokens, model_width = left_mine.shape
    rows = model_width // blocks
    for first, left in ((0, left_mine), (tokens, left_peer)):
        turned = left[...].T
        for block in range(blocks):
            to = pl.ds(pl.multiple_of(where_ref[block] * rows, rows), rows)
            left_ref[to, first : first + tokens] = turned[block * rows : (block + 1) * rows]
    for chunk in range(chunks):
        for part in range(2):
            half = slice(part * model_width // 2, (part + 1) * model_width // 2)
            mine, peer = rights[2 * chunk : 2 * chunk + 2]
            total = jnp.dot(left_ref[half, :tokens], mine[...], preferred_element_type=F32)
            total += jnp.dot(left_ref[half, tokens:], peer[...], preferred_element_type=F32)
            total = total.astype(BF16)
            for block in range(blocks // 2):
                outs[2 * chunk + part][block] = total[block * rows : (block + 1) * rows]


def weight_grad(where, left_mine, left_peer, *rights, weight=0):
    tokens, model_width = untied(left_mine).shape
    blocks = where.shape[0]
    chunks = len(rights) // 2
    width = rights[0].shape[1]
    out = jax.ShapeDtypeStruct((blocks // 2, model_width // blocks, width), BF16)
    whole = lambda value: pl.BlockSpec(value.shape, lambda j, w: (0,) * len(value.shape))
    inputs = [left_mine, left_peer, *rights]
    return run(
        functools.partial(weight_grad_kernel, chunks, blocks), weight,
        [where], inputs, [whole(untied(value)) for value in inputs],
        (1,), [whole(out)] * (2 * chunks), [out] * (2 * chunks),
        [pltpu.VMEM((model_width, 2 * tokens), BF16)],
    )


def halve_kernel(bit_ref, kept_out, sent_out, kept_in, sent_in, sent_ref, kept_ref):
    sent_ref[...] = (kept_out[...].astype(F32) + sent_out[...].astype(F32)).astype(BF16)
    kept_ref[...] = (kept_in[...].astype(F32) + sent_in[...].astype(F32)).astype(BF16)


def halve(bit, kept, received):
    blocks, rows, width = kept.shape
    out = jax.ShapeDtypeStruct((blocks // 2, rows, width), BF16)
    leave = pl.BlockSpec((1, rows, width), lambda j, b: (2 * j + 1 - b[0], 0, 0))
    stay = pl.BlockSpec((1, rows, width), lambda j, b: (2 * j + b[0], 0, 0))
    here = pl.BlockSpec((1, rows, width), lambda j, b: (j, 0, 0))
    return run(
        halve_kernel, 0, [bit], [kept, received, kept, untied(received)],
        [leave, leave, stay, stay], (blocks // 2,), [here, here], [out, out],
    )


def project_kernel(with_norm, *refs):
    refs = refs[2:] if with_norm > 1 else refs
    if with_norm:
        tokens_ref, rows_ref, weight_ref, offset_ref, normed_ref, out_ref = refs
        norm, _ = normalize(tokens_ref[...].astype(F32))
        normed = (norm * (1.0 + rows_ref[1:2]) + rows_ref[0:1]).astype(BF16)
        normed_ref[...] = normed
    else:
        tokens_ref, weight_ref, offset_ref, out_ref = refs
        normed = tokens_ref[...]
    out = jnp.dot(normed, weight_ref[...], preferred_element_type=F32) + offset_ref[...]
    out_ref[...] = out.astype(BF16)


def constant_block(shape):
    return pl.BlockSpec(shape, lambda i: (0,) * len(shape), pipeline_mode=pl.Buffered(1))


def row_blocks(rows, width, first=0):
    return pl.BlockSpec((rows, width), lambda i: (i + first, 0))


def project(normed, weight, offset, rows=256):
    tokens, model_width = normed.shape
    width = weight.shape[1]
    return run(
        functools.partial(project_kernel, 0), 9, (), [normed, weight, offset],
        [row_blocks(rows, model_width), constant_block(weight.shape), constant_block((1, width))],
        (tokens // rows,), row_blocks(rows, width), jax.ShapeDtypeStruct((tokens, width), BF16),
    )


def normed_project(half, shifts, weight, offset, filled=None, rows=256):
    half_tokens, model_width = untied(half).shape
    width = weight.shape[1]
    first = 0 if filled is None else half_tokens // rows
    held = [] if filled is None else list(filled)
    return run(
        functools.partial(project_kernel, 1 if filled is None else 2), 7, (),
        [*held, half, shifts, weight, offset],
        [pl.BlockSpec(memory_space=pl.ANY)] * len(held)
        + [
            row_blocks(rows, model_width), constant_block(shifts.shape),
            constant_block(weight.shape), constant_block((1, width)),
        ],
        (half_tokens // rows,),
        [row_blocks(rows, model_width, first), row_blocks(rows, width, first)],
        [
            jax.ShapeDtypeStruct((2 * half_tokens, model_width), BF16),
            jax.ShapeDtypeStruct((2 * half_tokens, width), BF16),
        ],
        aliases={0: 0, 1: 1} if held else {},
    )


def halves(rows, width, blocks):
    half = blocks // 2
    return [
        pl.BlockSpec((rows, width), lambda i: (jnp.minimum(i, half - 1), 0)),
        pl.BlockSpec((rows, width), lambda i: (jnp.maximum(i - half, 0), 0)),
    ]


def merge_kernel(
    blocks, live_ref, own_ref, other_ref, weight_own, weight_other, first_ref, second_ref,
    grad_first, grad_second, rows_ref, branch_ref, mid_ref, normed_ref, grad_ref, grad_b2_ref,
):
    gate1, bias, shift2, scale2, gate2 = (rows_ref[row : row + 1] for row in range(5))
    early = pl.program_id(0) < blocks // 2
    stream = jnp.where(early, first_ref[...], second_ref[...])
    grad = jnp.where(early, grad_first[...], grad_second[...])
    grad = jnp.where(live_ref[0] > 0, grad, jnp.zeros_like(grad))
    grad_ref[...] = grad
    branch = jnp.dot(own_ref[...], weight_own[...], preferred_element_type=F32)
    branch += jnp.dot(other_ref[...], weight_other[...], preferred_element_type=F32)
    branch += bias
    branch_ref[...] = branch.astype(BF16)
    mid = stream.astype(F32) + gate1 * branch
    mid_ref[...] = mid
    norm, _ = normalize(mid)
    normed_ref[...] = (norm * (1.0 + scale2) + shift2).astype(BF16)
    grad_b2_ref[...] = (gate2 * grad.astype(F32)).astype(BF16)


def merge(
    live, own, other, weight_own, weight_other, first, second, grad_first, grad_second, vectors,
    rows=256,
):
    tokens, width = own.shape
    model_width = weight_own.shape[1]
    blocks = tokens // rows
    half = blocks // 2
    block = lambda columns: pl.BlockSpec((rows, columns), lambda i, v: (i, 0))
    whole = lambda shape: pl.BlockSpec(shape, lambda i, v: (0,) * len(shape))
    pair = lambda: [
        pl.BlockSpec((rows, model_width), lambda i, v: (jnp.minimum(i, half - 1), 0)),
        pl.BlockSpec((rows, model_width), lambda i, v: (jnp.maximum(i - half, 0), 0)),
    ]
    shape = lambda kind: jax.ShapeDtypeStruct((tokens, model_width), kind)
    return run(
        functools.partial(merge_kernel, blocks), 11, [live],
        [own, other, weight_own, weight_other, first, second, grad_first, grad_second, vectors],
        [
            block(width), block(width), whole(weight_own.shape), whole(weight_other.shape),
            *pair(), *pair(), whole(vectors.shape),
        ],
        (blocks,), [block(model_width) for _ in range(5)],
        [shape(BF16), shape(F32), shape(BF16), shape(BF16), shape(BF16)],
    )


def add_row_sums(sums_ref, *values):
    @pl.when(pl.program_id(0) == 0)
    def _():
        sums_ref[...] = jnp.zeros_like(sums_ref)

    for row, value in enumerate(values):
        sums_ref[row : row + 1] += jnp.sum(value, 0, keepdims=True)


def middle_back_kernel(
    blocks, branch2_ref, back_ref, mid_ref, branch1_ref, grad_ref, grad_b2_ref, weight_own, weight_other,
    rows_ref, kept_ref, sent_ref, grad_mid_ref, grad_b1_ref, att_own_ref, att_other_ref, sums_ref,
):
    gate1, bias, scale2, gate2 = (rows_ref[row : row + 1] for row in range(4))
    block = pl.program_id(0)
    grad = grad_ref[...].astype(F32)
    mid = mid_ref[...]
    branch2 = branch2_ref[...] + bias
    output = (mid + gate2 * branch2).astype(BF16)

    @pl.when(block < blocks // 2)
    def _():
        kept_ref[...] = output

    @pl.when(block >= blocks // 2)
    def _():
        sent_ref[...] = output

    norm, inverse = normalize(mid)
    back = back_ref[...]
    grad_mid = grad + normalize_back(back * (1.0 + scale2), norm, inverse)
    grad_mid_ref[...] = grad_mid
    grad_b1 = (gate1 * grad_mid).astype(BF16)
    grad_b1_ref[...] = grad_b1
    att_own_ref[...] = dot_dims(grad_b1, weight_own[...], 1, 1).astype(BF16)
    att_other_ref[...] = dot_dims(grad_b1, weight_other[...], 1, 1).astype(BF16)
    add_row_sums(
        sums_ref, grad * branch2, grad_b2_ref[...].astype(F32), back, back * norm,
        grad_mid * branch1_ref[...].astype(F32), grad_b1.astype(F32),
    )


def middle_back(
    branch2, back, mid, branch1, grad, grad_b2, weight_own, weight_other, vectors, rows=256
):
    tokens, model_width = mid.shape
    width = weight_own.shape[0]
    blocks = tokens // rows
    full = lambda: row_blocks(rows, model_width)
    shape = lambda count, columns, kind: jax.ShapeDtypeStruct((count, columns), kind)
    return run(
        functools.partial(middle_back_kernel, blocks), 17, (),
        [branch2, back, mid, branch1, grad, grad_b2, weight_own, weight_other, vectors],
        [full() for _ in range(6)]
        + [
            constant_block(weight_own.shape), constant_block(weight_other.shape),
            constant_block(vectors.shape),
        ],
        (blocks,),
        [
            *halves(rows, model_width, blocks), full(), full(), row_blocks(rows, width),
            row_blocks(rows, width), constant_block((8, model_width)),
        ],
        [
            shape(tokens // 2, model_width, BF16), shape(tokens // 2, model_width, BF16),
            shape(tokens, model_width, F32), shape(tokens, model_width, BF16),
            shape(tokens, width, BF16), shape(tokens, width, BF16), shape(8, model_width, F32),
        ],
    )


def first_back_kernel(
    blocks, own_ref, other_ref, weight_own, weight_other, first_ref, second_ref, grad_mid_ref, rows_ref,
    kept_ref, sent_ref, sums_ref, own_sums_ref, other_sums_ref,
):
    block = pl.program_id(0)
    stream = jnp.where(block < blocks // 2, first_ref[...], second_ref[...])
    own, other = own_ref[...], other_ref[...]
    grad = dot_dims(own, weight_own[...], 1, 1) + dot_dims(other, weight_other[...], 1, 1)
    norm, inverse = normalize(stream.astype(F32))
    total = grad_mid_ref[...] + normalize_back(grad * (1.0 + rows_ref[0:1]), norm, inverse)

    @pl.when(block < blocks // 2)
    def _():
        kept_ref[...] = total

    @pl.when(block >= blocks // 2)
    def _():
        sent_ref[...] = total.astype(BF16)

    add_row_sums(sums_ref, grad, grad * norm)
    add_row_sums(own_sums_ref, own.astype(F32))
    add_row_sums(other_sums_ref, other.astype(F32))


def first_back(own, other, weight_own, weight_other, first, second, grad_mid, vectors, rows=256):
    tokens, model_width = grad_mid.shape
    width = untied(own).shape[1]
    blocks = tokens // rows
    full = lambda: row_blocks(rows, model_width)
    part = lambda: row_blocks(rows, width)
    shape = jax.ShapeDtypeStruct
    return run(
        functools.partial(first_back_kernel, blocks), 21, (),
        [own, other, weight_own, weight_other, first, second, grad_mid, vectors],
        [
            part(), part(), constant_block(weight_own.shape), constant_block(weight_other.shape),
            *halves(rows, model_width, blocks), full(), constant_block(vectors.shape),
        ],
        (blocks,),
        [
            *halves(rows, model_width, blocks), constant_block((8, model_width)),
            constant_block((8, width)), constant_block((8, width)),
        ],
        [
            shape((tokens // 2, model_width), F32), shape((tokens // 2, model_width), BF16),
            shape((8, model_width), F32), shape((8, width), F32), shape((8, width), F32),
        ],
    )


def bit_pairs(size, bit):
    return [(index, index ^ bit) for index in range(size)]


def swap(values, axis, bit):
    return lax.ppermute(values, axis, bit_pairs(lax.axis_size(axis), bit))


def pick(values, index, axis):
    return lax.dynamic_index_in_dim(values, index, axis, keepdims=False)


def place(first, second, index, axis=0):
    return jnp.where(
        index == 0,
        jnp.concatenate([first, second], axis),
        jnp.concatenate([second, first], axis),
    )


def cut_kernel(sizes, starts_ref, *refs):
    count = len(sizes)
    semaphores = refs[-1]
    copies = []
    for index, size in enumerate(sizes):
        rows = pl.ds(pl.multiple_of(starts_ref[index] * size, size), size)
        copies.append(
            pltpu.make_async_copy(
                refs[index].at[rows], refs[count + index], semaphores.at[index]
            )
        )
    for copy in copies:
        copy.start()
    for copy in copies:
        copy.wait()


def cut(values, places, sizes):
    return run(
        functools.partial(cut_kernel, sizes), 0, [jnp.stack(places).astype(jnp.int32)], list(values),
        [pl.BlockSpec(memory_space=pl.ANY)] * len(sizes), (1,),
        [pl.BlockSpec(memory_space=pltpu.VMEM)] * len(sizes),
        [
            jax.ShapeDtypeStruct((size,) + untied(value).shape[1:], untied(value).dtype)
            for value, size in zip(values, sizes)
        ],
        [pltpu.SemaphoreType.DMA((len(sizes),))],
    )


def joined_kernel(count, places_ref, *refs):
    out_ref, semaphores = refs[count:]
    rows = refs[0].shape[0]
    copies = [
        pltpu.make_async_copy(
            refs[index],
            out_ref.at[pl.ds(pl.multiple_of(places_ref[index] * rows, rows), rows)],
            semaphores.at[index],
        )
        for index in range(count)
    ]
    for copy in copies:
        copy.start()
    for copy in copies:
        copy.wait()


def joined(pieces, places):
    count = len(pieces)
    rows, width = untied(pieces[0]).shape
    return run(
        functools.partial(joined_kernel, count), 0, [places], list(pieces),
        [pl.BlockSpec(memory_space=pltpu.VMEM)] * count, (1,), pl.BlockSpec(memory_space=pl.ANY),
        jax.ShapeDtypeStruct((count * rows, width), BF16),
        [pltpu.SemaphoreType.DMA((count,))],
    )


def added_kernel(left_ref, right_ref, out_ref):
    out_ref[...] = (left_ref[...].astype(F32) + right_ref[...].astype(F32)).astype(BF16)


def added(left, right, *behind):
    whole = pl.BlockSpec(memory_space=pltpu.VMEM)
    out = jax.ShapeDtypeStruct(left.shape, BF16)
    return run(added_kernel, 0, (), [after(left, *behind), right], [whole, whole], (), whole, out)


def relay_kernel(value_ref, out_ref):
    out_ref[...] = value_ref[...]


def relay(value, *behind):
    whole = pl.BlockSpec(memory_space=pltpu.VMEM)
    out = jax.ShapeDtypeStruct(value.shape, value.dtype)
    return run(relay_kernel, 0, (), [after(value, *behind)], [whole], (), whole, out)


def gather_dp(values):
    size = lax.axis_size("dp")
    here = lax.axis_index("dp")
    step = 1
    while step < size:
        values = place(values, swap(values, "dp", step), lax.rem(here // step, 2))
        step *= 2
    return values


def sum_dp(values):
    step = 1
    while step < lax.axis_size("dp"):
        values = values + swap(values, "dp", step)
        step *= 2
    return values


def slot_device(
    latents,
    condition,
    cotangent,
    group_counts,
    heads_weight,
    heads_bias,
    merge_weight,
    merge_bias,
    up_weight,
    up_bias,
    down_weight,
    down_bias,
    modulate_weight,
    modulate_bias,
):
    side = lax.axis_index("tensor")
    place_dp = lax.axis_index("dp")
    core, x_bit, near, far = (lax.rem(place_dp // step, 2) for step in (1, 2, 4, 8))
    bits = (far, near, x_bit)
    half, model_width = latents.shape[1:]
    columns = heads_weight.shape[3]
    features = modulate_weight.shape[3]
    hidden_here = up_weight.shape[2]
    merge_own, up_own, down_own = merge_weight[0], up_weight[0], down_weight[0]
    padded_rows = lambda *rows: jnp.pad(jnp.stack(rows), ((0, 8 - len(rows)), (0, 0)))
    bit_value = lambda value: jnp.reshape(value, (1,)).astype(jnp.int32)
    core_value = bit_value(core)
    quarter = 2 * near + core
    places = 2 * jnp.stack([near, 1 - near, near, 1 - near]) + jnp.stack(
        [core, core, 1 - core, 1 - core]
    )
    places = places.astype(jnp.int32)

    def fetch(values):
        return swap(values, "tensor", 1)

    def pass_on(got):
        return got, swap(got, "dp", 4), swap(got, "dp", 1)

    def pass_last(passed, *behind):
        got, from_near, from_core = passed
        to_core = relay(from_near, *behind) if behind else from_near
        return got, from_near, from_core, swap(to_core, "dp", 1)

    def joined_after(passed, *behind):
        return joined((after(passed[0], *behind),) + passed[1:], places)

    def quarter_of(weight, *behind):
        return cut((after(weight, *behind),), (quarter,), (weight.shape[0] // 4,))[0]

    latent_own, latent_sent, cotangent_own = cut(
        (latents, latents, cotangent), (side, 1 - side, side), (1, 1, 1)
    )
    latent_other = fetch(latent_sent[0])
    heads_own = heads_weight[0].reshape(model_width, 3 * columns)
    core_places = jnp.stack([core, 1 - core]).astype(jnp.int32)

    def half_of(weight, *behind):
        return cut((after(weight, *behind),), (core,), (weight.shape[0] // 2,))[0]

    silu_cond = jax.nn.silu(condition.astype(F32)).astype(BF16)
    local_mod = jnp.einsum(
        "sd,dkc->skc", silu_cond, modulate_weight[0], preferred_element_type=F32
    ) + modulate_bias[0].astype(F32)
    mod_other = swap(pick(local_mod, 1 - side, 0), "tensor", 1)
    bias_pack = swap(jnp.concatenate([heads_bias.reshape(-1), up_bias.reshape(-1)]), "tensor", 1)
    shift1, scale1, gate1, shift2, scale2, gate2 = place(
        pick(local_mod, side, 0), mod_other, side, 1
    )

    def heads_offset(pair):
        return jnp.concatenate([pair[0], jnp.zeros_like(pair[0]), pair[1]]).astype(F32)[None]

    offset_own = heads_offset(heads_bias[0])
    offset_other = heads_offset(bias_pack[: 2 * columns].reshape(2, columns))
    up_bias_own = up_bias.astype(F32)
    up_bias_other = bias_pack[2 * columns :].reshape(1, hidden_here).astype(F32)
    shifts1 = padded_rows(shift1, scale1)

    heads_half = half_of(heads_own, latent_sent)
    heads_got = fetch(heads_half)
    filled = normed_project(
        after(latent_own[0], heads_half), shifts1, heads_own, offset_own
    )
    normed1, qkv_own = normed_project(latent_other, shifts1, heads_own, offset_own, filled)
    attended_own, logsum_own = attend(qkv_own)
    heads_got = relay(heads_got, attended_own)
    heads_core = swap(heads_got, "dp", 1)
    merge_half_own = half_of(merge_own, heads_got)
    (cotangent_sent,) = cut((after(cotangent, merge_half_own),), (1 - side,), (1,))
    merge_got = fetch(merge_half_own)
    cotangent_other = fetch(cotangent_sent[0])
    heads_other = joined((after(heads_got, cotangent_sent), heads_core), core_places)
    qkv_other = project(normed1, heads_other, offset_other)
    attended_other, logsum_other = attend(qkv_other)
    up_quarter = quarter_of(up_own, attended_other)
    up_passed = pass_on(fetch(up_quarter))
    merge_got = relay(merge_got, up_quarter)
    merge_other = joined((merge_got, swap(merge_got, "dp", 1)), core_places)
    live = bit_value(side < group_counts[0])
    branch1, mid, normed2, grad, grad_b2 = merge(
        live, attended_own, attended_other, merge_own, merge_other, latent_own[0], latent_other, cotangent_own[0],
        cotangent_other, padded_rows(gate1, merge_bias[0].astype(F32), shift2, scale2, gate2),
    )
    down_half = half_of(down_own, normed2)
    down_got = fetch(down_half)
    normed1_peer = swap(normed1, "dp", 1)
    normed2_peer = swap(normed2, "dp", 1)
    grad_b2_peer = swap(grad_b2, "dp", 1)
    branch2, back2, *hidden_own, up_sums_own = feed(
        core_value, after(normed2, down_half), grad_b2, up_own, up_bias_own, down_own
    )
    hidden_sent_own, hidden_own, pre_sent_own, pre_own = hidden_own
    hidden_peer_own, pre_peer_own = swap(hidden_sent_own, "dp", 1), swap(pre_sent_own, "dp", 1)

    far_of, near_of, x_of = (
        jnp.arange(8, dtype=jnp.int32) // step % 2 for step in (4, 2, 1)
    )
    where_x = 4 * (x_of == x_bit) + 2 * far_of + near_of
    where_near = 4 * (near_of == near) + 2 * far_of + x_of
    near_next = (near, 4)
    x_next = (x_bit, 2)

    def halved(kept, received, step, *behind):
        sent, kept = halve(bit_value(step[0]), kept, after(received, *behind))
        return kept, swap(sent, "dp", step[1])

    def halved_last(pairs, *behind):
        halves_here = [
            halve(bit_value(far), kept, after(received, *behind)) for kept, received in pairs
        ]
        sent = jnp.concatenate([sent[0] for sent, _ in halves_here], 1)
        return jnp.concatenate([kept[0] for _, kept in halves_here], 1), swap(sent, "dp", 8)

    def pair_total(own, other, *behind):
        return own.astype(F32) + swap(other, "tensor", 1).astype(F32)

    def swap_rows(total, *behind):
        total = total.astype(BF16).reshape((2, -1) + total.shape[1:])
        return pick(total, core, 0), swap(pick(total, 1 - core, 0), "dp", 1)

    def join_columns(mine, others):
        return place(mine, others, core, mine.ndim - 1).astype(F32)

    down_parts_own = weight_grad(
        where_x, grad_b2, after(grad_b2_peer, normed2), hidden_own, hidden_peer_own
    )
    down_first_own = swap(down_parts_own[0], "dp", 2)
    up_parts_own = weight_grad(
        where_near, after(normed2, down_parts_own[0]), normed2_peer, pre_own, pre_peer_own,
        weight=13,
    )
    up_first_own = swap(up_parts_own[0], "dp", 4)
    up_passed = pass_last(up_passed, up_parts_own[0])
    down_pieces = (down_got, swap(down_got, "dp", 1))
    up_other = joined_after(up_passed, up_parts_own[0])
    down_other = joined(
        (after(down_pieces[0], up_other), down_pieces[1]), core_places
    )
    branch2, back2, *hidden_other, up_sums_other = feed(
        core_value, normed2, grad_b2, up_other, up_bias_other, down_other, (branch2, back2)
    )
    hidden_sent_other, hidden_other, pre_sent_other, pre_other = hidden_other
    hidden_peer_other = swap(hidden_sent_other, "dp", 1)
    pre_peer_other = swap(pre_sent_other, "dp", 1)
    down_half_own = halved(down_parts_own[1], down_first_own, near_next, hidden_other)
    up_half_own = halved(up_parts_own[1], up_first_own, x_next, hidden_other)
    output_own, output_sent, grad_mid, grad_b1, grad_att_own, grad_att_other, middle_sums = middle_back(
        after(branch2, down_half_own[0], up_half_own[0]), back2, mid, branch1, grad, grad_b2,
        merge_own, merge_other, padded_rows(gate1, down_bias[0].astype(F32), scale2, gate2),
    )
    grad_gate2, down_bias_sum, grad_shift2, grad_scale2, grad_gate1, merge_bias_sum = middle_sums[:6]
    down_parts_other = weight_grad(
        where_x, grad_b2, after(grad_b2_peer, grad_att_own, grad_att_other),
        hidden_other, hidden_peer_other,
    )
    down_first_other = swap(down_parts_other[0], "dp", 2)
    up_parts_other = weight_grad(
        where_near, after(normed2, down_parts_other[0]), normed2_peer, pre_other, pre_peer_other
    )
    up_first_other = swap(up_parts_other[0], "dp", 4)
    output_other = swap(output_sent, "tensor", 1)
    grads_own, sent_own, kept_own = attend_back(
        core_value, qkv_own, attended_own, after(grad_att_own, up_parts_other[0]), logsum_own
    )
    heads_peer_own = swap(sent_own, "dp", 1)
    merge_total = outer_rows(
        grad_b1,
        jnp.concatenate([attended_own, attended_other], 1),
    ).astype(BF16).reshape(8, 2, -1, 2 * columns)
    merge_sent = swap(pick(merge_total, 1 - core, 1), "dp", 1)
    merge_total = pick(merge_total, core, 1).astype(F32) + merge_sent.astype(F32)
    merge_total = merge_total.astype(BF16).reshape((2, 2, 2) + merge_total.shape[1:])
    merge_first = swap(pick(merge_total, 1 - near, 1), "dp", 4)
    merge_kept = pick(merge_total, near, 1).reshape((4,) + merge_total.shape[3:])
    merge_first = merge_first.reshape(merge_kept.shape)
    down_half_other = halved(down_parts_other[1], down_first_other, near_next, grads_own)
    up_half_other = halved(up_parts_other[1], up_first_other, x_next, grads_own)
    feed_last_own = halved_last([down_half_own, up_half_own], down_half_other[0], up_half_other[0])
    block_output = place(output_own[None], output_other[None], side)
    grads_other, sent_other, kept_other = attend_back(
        core_value, qkv_other, attended_other,
        after(grad_att_other, feed_last_own[0], down_half_other[0], up_half_other[0]), logsum_other,
    )
    heads_peer_other = swap(sent_other, "dp", 1)
    feed_last_other = halved_last([down_half_other, up_half_other], grads_other)
    heads_parts_own = weight_grad(
        where_x, normed1, after(normed1_peer, feed_last_other[0], merge_kept),
        kept_own, heads_peer_own, weight=13,
    )
    heads_first_own = swap(heads_parts_own[0], "dp", 2)
    heads_parts_other = weight_grad(
        where_x, normed1, after(normed1_peer, heads_parts_own[0]), kept_other, heads_peer_other
    )
    heads_first_other = swap(heads_parts_other[0], "dp", 2)
    done = heads_parts_other[0]
    merge_half = halved(merge_kept, merge_first, x_next, done)
    feed_own = added(*feed_last_own, done)
    grad_latent, latent_sent, first_sums, heads_sums_own, heads_sums_other = first_back(
        grads_own, after(grads_other, done, merge_half[0], feed_own), heads_own, heads_other,
        latent_own[0], latent_other, grad_mid, padded_rows(scale1),
    )
    heads_half_own = halved(heads_parts_own[1], heads_first_own, near_next, grad_latent)
    heads_half_other = halved(
        heads_parts_other[1], heads_first_other, near_next, heads_half_own[0]
    )
    latent_sent = swap(latent_sent, "tensor", 1)
    feed_other = added(*feed_last_other, heads_half_other[0])
    feed_total = pair_total(feed_own, feed_other)
    merge_last = halved_last([merge_half], feed_other)
    heads_last = halved_last([heads_half_own, heads_half_other], feed_other)
    feed_mine, feed_others = swap_rows(feed_total)
    cut_at = feed_mine.shape[1] // 2
    down_grad = join_columns(feed_mine[:, :cut_at], feed_others[:, :cut_at])
    up_grad = join_columns(feed_mine[:, cut_at:], feed_others[:, cut_at:])
    grad_shift1, grad_scale1 = first_sums[0], first_sums[1]
    merge_total = added(*merge_last, heads_last[0])
    heads_total = added(*heads_last, merge_total)
    cut_at = heads_total.shape[1] // 2
    heads_total = pair_total(heads_total[:, :cut_at], heads_total[:, cut_at:])
    latent_sent = latent_sent.astype(F32)
    heads_total = heads_total[:, : 3 * columns // 2]
    heads_grad = join_columns(
        *swap_rows(heads_total.reshape(heads_total.shape[0], 3, columns // 2))
    )
    merge_grad = pair_total(merge_total[:, :columns], merge_total[:, columns:], latent_sent)

    def query_value_sums(sums):
        return jnp.concatenate([sums[0, :columns], sums[0, 2 * columns :]])

    def by_side(rows):
        rows = rows.reshape(rows.shape[:-1] + (2, features))
        return pick(rows, side, rows.ndim - 2), pick(rows, 1 - side, rows.ndim - 2)

    grad_mod = jnp.stack(
        [grad_shift1, grad_scale1, grad_gate1, grad_shift2, grad_scale2, grad_gate2]
    ).astype(BF16)
    grad_mod_own, grad_mod_sent = by_side(grad_mod)
    merge_own_sum, merge_other_sum = by_side(merge_bias_sum)
    down_own_sum, down_other_sum = by_side(down_bias_sum)
    bias_own = jnp.concatenate(
        [query_value_sums(heads_sums_own), merge_own_sum, up_sums_own[0], down_own_sum]
    )
    bias_other = jnp.concatenate(
        [query_value_sums(heads_sums_other), merge_other_sum, up_sums_other[0], down_other_sum]
    )
    crossing = jnp.concatenate([bias_other, grad_mod_sent.astype(F32).reshape(-1)])
    crossing = swap(relay(crossing.reshape(-1, 128), heads_last[0]), "tensor", 1).reshape(-1)
    bias_total = sum_dp(bias_own + crossing[: bias_own.shape[0]])
    grad_mod_slots = place(
        grad_mod_own[None],
        crossing[bias_own.shape[0] :].astype(BF16).reshape(grad_mod_own[None].shape), side,
    )
    slots_here = silu_cond.shape[0]
    tail = jnp.concatenate([silu_cond, grad_mod_slots.reshape(slots_here, -1)], 1)
    tail_all = gather_dp(tail)
    silu_all = tail_all[:, :model_width]
    grad_mod_all = tail_all[:, model_width:].reshape((-1,) + grad_mod_slots.shape[1:])
    rows_here = model_width // lax.axis_size("dp")
    silu_rows = lax.dynamic_slice_in_dim(silu_all, place_dp * rows_here, rows_here, 1)
    modulate_grad = jnp.einsum("sd,skc->dkc", silu_rows, grad_mod_all, preferred_element_type=F32)
    modulate_bias_grad = jnp.sum(grad_mod_all.astype(F32), 0)
    cond_partial = jnp.einsum(
        "dkc,skc->sd", modulate_weight[0], grad_mod_slots, preferred_element_type=F32
    )
    cond_total = cond_partial + swap(cond_partial, "tensor", 1)
    condition_grad = jax.vjp(jax.nn.silu, condition.astype(F32))[1](cond_total)[0]
    latent_grad = place(grad_latent[None], latent_sent[None], side)
    edges = (0, 2 * columns, 2 * columns + features, 2 * columns + features + hidden_here, None)
    heads_bias_grad, merge_bias_grad, up_bias_grad, down_bias_grad = (
        bias_total[first:last] for first, last in zip(edges, edges[1:])
    )
    return (
        block_output,
        latent_grad,
        condition_grad,
        heads_grad[None],
        heads_bias_grad.reshape(1, 2, columns),
        merge_grad.T[None],
        merge_bias_grad[None],
        up_grad[None],
        up_bias_grad[None],
        down_grad.T[None],
        down_bias_grad[None],
        modulate_grad[None],
        modulate_bias_grad[None],
    )


def solution(mesh):
    in_specs = (
        P("dp", "tensor", None),
        P("dp", None),
        P("dp", "tensor", None),
        P("dp"),
        P(None, None, None, "tensor"),
        P(None, None, "tensor"),
        P(None, "tensor", None),
        P(),
        P(None, None, "tensor"),
        P(None, "tensor"),
        P(None, "tensor", None),
        P(),
        P(None, None, None, "tensor"),
        P(None, None, "tensor"),
    )
    out_specs = (
        P("dp", "tensor", None),
        P("dp", "tensor", None),
        P("dp", None),
        P(None, "dp", None, "tensor"),
        P(None, None, "tensor"),
        P(None, "tensor", "dp"),
        P(None, "tensor"),
        P(None, "dp", "tensor"),
        P(None, "tensor"),
        P(None, "tensor", "dp"),
        P(None, "tensor"),
        P(None, "dp", None, "tensor"),
        P(None, None, "tensor"),
    )
    whole_slots = mesh.shape["tensor"] == 2 and mesh.shape["dp"] == 16
    return jax.shard_map(
        slot_device if whole_slots else per_device, mesh=mesh, in_specs=in_specs, out_specs=out_specs, check_vma=False
    )
```
